32 devices in a mesh: dp: 8 (over z, x), row: 2 (over y), col: 2 (over core).
Axes of the slice: x: 2, y: 2, z: 4, core: 2. Of those that a mesh axis runs over, the one named last changes fastest.
Arguments:
- hidden_in: bfloat16 [16384, 960], P(('dp', 'row'), 'col'), may hold values from -6 to 6
- query_weight: bfloat16 [960, 2, 576], P('col', 'row'), may hold values from -0.1875 to 0.1875
- key_weight: bfloat16 [960, 2, 192], P('col', 'row'), may hold values from -0.1875 to 0.1875
- value_weight: bfloat16 [960, 2, 192], P('col', 'row'), may hold values from -0.1875 to 0.1875
- output_weight: bfloat16 [2, 576, 960], P('row', None, 'col'), may hold values from -1.5 to 1.5
- gate_weight: bfloat16 [960, 2560], P('col', 'row'), may hold values from -0.1875 to 0.1875
- up_weight: bfloat16 [960, 2560], P('col', 'row'), may hold values from -0.1875 to 0.1875
- down_weight: bfloat16 [2560, 960], P('row', 'col'), may hold values from -0.125 to 0.125
- attn_gain: bfloat16 [960], P('col'), may hold values from 0.5 to 1.5
- ffn_gain: bfloat16 [960], P('col'), may hold values from 0.5 to 1.5
- out_grad: bfloat16 [16384, 960], P(('dp', 'row'), 'col'), may hold values from -6 to 6
- segment_ids: int32 [16384], P(('dp', 'col')), may hold values from 0 to 15, as said below
Outputs:
- block_out: bfloat16 [16384, 960], P(('dp', 'row'), 'col')
- input_grad: bfloat16 [16384, 960], P(('dp', 'row'), 'col')
- query_weight_grad: float32 [960, 2, 576], P('col', 'row')
- key_weight_grad: float32 [960, 2, 192], P('col', 'row')
- value_weight_grad: float32 [960, 2, 192], P('col', 'row')
- output_weight_grad: float32 [2, 576, 960], P('row', None, 'col')
- gate_weight_grad: float32 [960, 2560], P('col', 'row')
- up_weight_grad: float32 [960, 2560], P('col', 'row')
- down_weight_grad: float32 [2560, 960], P('row', 'col')
- attn_gain_grad: float32 [960], P('col')
- ffn_gain_grad: float32 [960], P('col')
The draws below stay inside these ranges and needn't reach their ends.
Inputs may be any that keep to these rules, and one draw needn't show every extreme that they name: `segment_ids`: inside each aligned window of 1024 tokens the ids start at 0 and rise by one where a new sequence begins, so no sequence crosses a window's edge; some window holds a single sequence of 1024 tokens.
All inputs are finite; a program needn't handle non-finite values.
Results may differ from the reference program's by a relative error of at most 0.013.
Values may be sent and summed in bfloat16 or wider, within the bound.
No kernel may reach another device: no remote copies, remote signals or barrier semaphores. Data moves between devices by JAX's collectives and lax.ppermute only.
A program may use at most 256 MiB of HBM per device.

```python
import math
import jax
import jax.numpy as jnp
from jax import lax

D = 960
HEADS = 15
KV_HEADS = 5
HDIM = 64
FF = 2560
SLOT_HEADS = 9
MAXLEN = 1024
TOKENS = 16384
N_ROW = 2


def draw_segment_ids(key, part):
    key = jax.random.fold_in(key, 7)
    windows = TOKENS // MAXLEN
    span_cap = min(16, MAXLEN)
    spacing = MAXLEN // span_cap
    count_key, place_key, pick_key = jax.random.split(key, 3)
    counts = jax.random.randint(count_key, (windows, 1), 0, span_cap)
    places = jax.random.randint(place_key, (windows, span_cap - 1), 1, MAXLEN)
    active = jnp.arange(span_cap - 1)[None, :] < counts
    column = jnp.arange(MAXLEN)[None, None, :]
    starts = jnp.any((places[:, :, None] == column) & active[:, :, None], axis=1)
    single_pick = jax.random.randint(pick_key, (), 0, windows)
    window_index = jnp.arange(windows)[:, None]
    single = window_index == single_pick
    busy = window_index == (single_pick + 1) % windows
    position_row = jnp.arange(MAXLEN)[None, :]
    busy_starts = (position_row % spacing == 0) & (position_row // spacing >= 1) & (position_row // spacing < span_cap)
    starts = jnp.where(busy, busy_starts, starts)
    starts = starts & jnp.logical_not(single)
    starts = starts & (position_row > 0)
    return jnp.cumsum(starts.astype(jnp.int32), axis=1).reshape(TOKENS).astype(jnp.int32)


def block_levels(stream_key, dims, pieces, least, high):
    loudness, own = 1.0, jax.random.fold_in(stream_key, 6)
    for dim, blocks in pieces:
        steps = jnp.exp(jax.random.uniform(jax.random.fold_in(own, dim), (blocks,), jnp.float32, least / len(pieces), high / len(pieces)))
        loudness = loudness * jnp.repeat(steps, dims[dim] // blocks).reshape([-1 if axis == dim else 1 for axis in range(len(dims))])
    return loudness


def scatter_about(key, dims, width, bound, shards=(), held_as=jnp.bfloat16):
    array = width * jax.random.normal(key, dims, jnp.float32)
    if shards:
        array = array * block_levels(key, dims, shards, -0.22, 0.18)
    return jnp.clip(array, -bound, bound).astype(held_as)


def setup_inputs(seed: int = 0) -> dict:
    key_list = jax.random.split(jax.random.key(seed), 13)
    return {
        "hidden_in": scatter_about(key_list[0], (TOKENS, D), 1.0, 6.0, ((0, 16), (1, 2))),
        "query_weight": scatter_about(key_list[1], (D, N_ROW, SLOT_HEADS * HDIM), D ** -0.5, 0.1875, ((0, 2), (1, 2))),
        "key_weight": scatter_about(key_list[2], (D, N_ROW, SLOT_HEADS // (HEADS // KV_HEADS) * HDIM), D ** -0.5, 0.1875, ((0, 2), (1, 2))),
        "value_weight": scatter_about(key_list[3], (D, N_ROW, SLOT_HEADS // (HEADS // KV_HEADS) * HDIM), D ** -0.5, 0.1875, ((0, 2), (1, 2))),
        "output_weight": scatter_about(key_list[4], (N_ROW, SLOT_HEADS * HDIM, D), (HDIM // 4) ** -0.5, 1.5, ((0, 2), (2, 2))),
        "gate_weight": scatter_about(key_list[5], (D, FF), D ** -0.5, 0.1875, ((0, 2), (1, 2))),
        "up_weight": scatter_about(key_list[6], (D, FF), D ** -0.5, 0.1875, ((0, 2), (1, 2))),
        "down_weight": scatter_about(key_list[7], (FF, D), FF ** -0.5, 0.125, ((0, 2), (1, 2))),
        "attn_gain": jnp.clip(1.0 + 0.1 * jax.random.normal(key_list[8], (D,), jnp.float32), 0.5, 1.5).astype(jnp.bfloat16),
        "ffn_gain": jnp.clip(1.0 + 0.1 * jax.random.normal(key_list[9], (D,), jnp.float32), 0.5, 1.5).astype(jnp.bfloat16),
        "out_grad": scatter_about(key_list[10], (TOKENS, D), 1.0, 6.0, ((0, 16), (1, 2))),
        "segment_ids": draw_segment_ids(jax.random.fold_in(key_list[12], 71), 0),
    }


@jax.custom_vjp
def low(v):
    return lax.optimization_barrier(v.astype(jnp.bfloat16)).astype(jnp.float32)

@jax.custom_vjp
def low_back(v):
    return v

def low_keep(v):
    return (low(v), None)

def low_pass(kept, grad):
    return (grad,)

def back_keep(v):
    return (v, None)

def back_low(kept, grad):
    return (low(grad),)
low.defvjp(low_keep, low_pass)
low_back.defvjp(back_keep, back_low)
NORM_EPS = 1e-05
ROPE_BASE = 100000.0
MASKED_SCORE = -1e+30
FULL_PRECISION = lax.Precision.HIGHEST

def matmul(left, right):
    return jnp.dot(left, right, precision=FULL_PRECISION, preferred_element_type=jnp.float32)

def positions_of(segment):
    position_index = jnp.arange(segment.shape[0], dtype=jnp.int32)
    is_start = jnp.concatenate([jnp.ones((1,), dtype=bool), segment[1:] != segment[:-1]])
    seg_begin = lax.cummax(jnp.where(is_start, position_index, jnp.zeros_like(position_index)), axis=0)
    return position_index - seg_begin

def rope_tables(position):
    half_dim = HDIM // 2
    frequency = ROPE_BASE ** (-(jnp.arange(half_dim, dtype=jnp.float32) * 2.0 / HDIM))
    angles = position.astype(jnp.float32)[:, None] * frequency[None, :]
    cosine_table = jnp.concatenate([jnp.cos(angles), jnp.cos(angles)], axis=1)
    sine_table = jnp.concatenate([jnp.sin(angles), jnp.sin(angles)], axis=1)
    return (cosine_table, sine_table)

def rotate(heads_in, cosine_table, sine_table):
    half_dim = heads_in.shape[-1] // 2
    turned = jnp.concatenate([-heads_in[..., half_dim:], heads_in[..., :half_dim]], axis=-1)
    return heads_in * cosine_table[:, None, :] + turned * sine_table[:, None, :]

def window_attention(packed):
    queries, keys_in, values, segment = packed
    span_rows = queries.shape[0]
    group = HEADS // KV_HEADS
    grouped = queries.reshape(span_rows, KV_HEADS, group, HDIM)
    scores = jnp.einsum('qgjd,kgd->gjqk', grouped, keys_in, precision=FULL_PRECISION) * (1.0 / math.sqrt(HDIM))
    scores = low_back(scores)
    position_index = jnp.arange(span_rows, dtype=jnp.int32)
    allowed = (segment[:, None] == segment[None, :]) & (position_index[None, :] <= position_index[:, None])
    scores = jnp.where(allowed[None, None], scores, MASKED_SCORE)
    highest = lax.optimization_barrier(jnp.max(scores, axis=-1, keepdims=True))
    weights_exp = jnp.exp(scores - highest)
    probability = weights_exp / lax.optimization_barrier(jnp.sum(weights_exp, axis=-1, keepdims=True))
    mixture = jnp.einsum('gjqk,kgd->qgjd', low(probability), values, precision=FULL_PRECISION)
    return mixture.reshape(span_rows, HEADS, HDIM)

def layer(hidden_in, query_weight, key_weight, value_weight, output_weight, gate_weight, up_weight, down_weight, attn_gain, ffn_gain, segment_ids):
    group = HEADS // KV_HEADS
    slot_kv = SLOT_HEADS // group
    query_real = jnp.concatenate([query_weight[:, 0], query_weight[:, 1, :(HEADS - SLOT_HEADS) * HDIM]], axis=1)
    key_real = jnp.concatenate([key_weight[:, 0], key_weight[:, 1, :(KV_HEADS - slot_kv) * HDIM]], axis=1)
    value_real = jnp.concatenate([value_weight[:, 0], value_weight[:, 1, :(KV_HEADS - slot_kv) * HDIM]], axis=1)
    output_real = jnp.concatenate([output_weight[0], output_weight[1, :(HEADS - SLOT_HEADS) * HDIM]], axis=0)
    tokens = hidden_in.shape[0]
    level_in = lax.rsqrt(lax.optimization_barrier(jnp.mean(hidden_in * hidden_in, axis=1, keepdims=True)) + NORM_EPS)
    normed_in = low(hidden_in * level_in * attn_gain)
    joined = low_back(matmul(normed_in, jnp.concatenate([query_real, key_real, value_real], axis=1)))
    query_cols = HEADS * HDIM
    key_cols = KV_HEADS * HDIM
    windows = tokens // MAXLEN
    position = jax.vmap(positions_of)(segment_ids.reshape(windows, MAXLEN)).reshape(tokens)
    cosine_table, sine_table = rope_tables(position)
    queries = low(rotate(joined[:, :query_cols].reshape(tokens, HEADS, HDIM), cosine_table, sine_table))
    keys_in = low(rotate(joined[:, query_cols:query_cols + key_cols].reshape(tokens, KV_HEADS, HDIM), cosine_table, sine_table))
    values = low(joined[:, query_cols + key_cols:].reshape(tokens, KV_HEADS, HDIM))
    mixture = lax.map(jax.checkpoint(window_attention), (queries.reshape(windows, MAXLEN, HEADS, HDIM), keys_in.reshape(windows, MAXLEN, KV_HEADS, HDIM), values.reshape(windows, MAXLEN, KV_HEADS, HDIM), segment_ids.reshape(windows, MAXLEN)))
    attended = low(low_back(mixture.reshape(tokens, query_cols)))
    mid = hidden_in + low_back(matmul(attended, output_real))
    level_mid = lax.rsqrt(lax.optimization_barrier(jnp.mean(mid * mid, axis=1, keepdims=True)) + NORM_EPS)
    normed_mid = low(mid * level_mid * ffn_gain)
    gate_part = low_back(matmul(normed_mid, gate_weight))
    up_part = low_back(matmul(normed_mid, up_weight))
    active = low(gate_part * jax.nn.sigmoid(gate_part) * up_part)
    return mid + low_back(matmul(active, down_weight))

def reference(hidden_in, query_weight, key_weight, value_weight, output_weight, gate_weight, up_weight, down_weight, attn_gain, ffn_gain, out_grad, segment_ids):
    float_args = tuple((item.astype(jnp.float32) for item in (hidden_in, query_weight, key_weight, value_weight, output_weight, gate_weight, up_weight, down_weight, attn_gain, ffn_gain)))

    def forward_fn(*weights_all):
        return layer(*weights_all, segment_ids)
    result_out, pullback = jax.vjp(forward_fn, *float_args)
    gradients = pullback(out_grad.astype(jnp.float32))
    return (result_out.astype(jnp.bfloat16), gradients[0].astype(jnp.bfloat16), gradients[1], gradients[2], gradients[3], gradients[4], gradients[5], gradients[6], gradients[7], gradients[8], gradients[9])
```

```python
import functools
import math

import jax
import jax.numpy as jnp
from jax import lax
from jax.experimental import pallas as pl
from jax.experimental.pallas import tpu as pltpu
from jax.sharding import PartitionSpec as P

D = 960
HEADS = 15
KV_HEADS = 5
GROUP = 3
HDIM = 64
MAXLEN = 1024
SLOTS = 9
BLOCK = MAXLEN // 4
LOCAL = 2 * BLOCK
HALF = D // 2

NORM_EPS = 1e-05
ROPE_BASE = 100000.0
MASKED_SCORE = -1e30
SCALE = 1.0 / math.sqrt(HDIM)
BF16 = jnp.bfloat16
F32 = jnp.float32
VMEM_BYTES = 56 * 1024 * 1024

QUERY_AT = [(0, h * HDIM) for h in range(9)] + [(1, h * HDIM) for h in range(6)]
KEY_AT = [(0, 576 + h * HDIM) for h in range(3)] + [(1, 576 + h * HDIM) for h in range(2)]
VALUE_AT = [(0, 768 + h * HDIM) for h in range(3)] + [(1, 768 + h * HDIM) for h in range(2)]
KEY_BLOCKS = ((1, 4), (2, 3))
HELD = ((0, 3), (1, 2))


def dot(left, right, left_dim=1, right_dim=0):
    return lax.dot_general(
        left, right, (((left_dim,), (right_dim,)), ((), ())), preferred_element_type=F32
    )


def params():
    return pltpu.CompilerParams(vmem_limit_bytes=VMEM_BYTES)


def level_of(rows):
    return lax.rsqrt(jnp.sum(rows * rows, axis=1, keepdims=True) / D + NORM_EPS)


def turn(chunk):
    lane = lax.broadcasted_iota(jnp.int32, chunk.shape, 1)
    return jnp.where(lane % HDIM < HDIM // 2, pltpu.roll(chunk, 96, 1), pltpu.roll(chunk, 32, 1))


def qkv_kernel(x_ref, gain_ref, cos_ref, sin_ref, w0_ref, w1_ref, nm_ref, q_ref, kv_ref):
    rows = x_ref[...].astype(F32)
    nm = (rows * level_of(rows) * gain_ref[...]).astype(BF16)
    nm_ref[...] = nm
    cosine, sine = cos_ref[...], sin_ref[...]
    joined = [dot(nm, w0_ref[...]), dot(nm, w1_ref[...])]
    turned = {}

    def piece(block, lane, rotate):
        start = lane // 128 * 128
        stop = min(start + 128, D)
        chunk = joined[block][:, start:stop]
        if rotate:
            if (block, start) not in turned:
                turned[block, start] = chunk * cosine + turn(chunk) * sine
            chunk = turned[block, start]
        return chunk[:, lane - start : lane - start + HDIM]

    for h, (block, lane) in enumerate(QUERY_AT):
        q_ref[h] = (piece(block, lane, True).astype(BF16).astype(F32) * SCALE).astype(BF16)
    for g, (block, lane) in enumerate(KEY_AT):
        kv_ref[g] = piece(block, lane, True).astype(BF16)
    for g, (block, lane) in enumerate(VALUE_AT):
        kv_ref[KV_HEADS + g] = piece(block, lane, False).astype(BF16)


def fill_bias(bias_ref, index_ref, begin_ref):
    key_index = lax.broadcasted_iota(jnp.int32, (MAXLEN, LOCAL), 0)
    allowed = (key_index >= begin_ref[...]) & (key_index <= index_ref[...])
    bias_ref[...] = jnp.where(allowed, 0.0, MASKED_SCORE)


def attend_kernel(
    core_ref, index_ref, begin_ref, q_ref, k_ref, v_ref, x_ref, gain_ref, wo_ref,
    att_ref, mid_ref, nm_ref, lse_ref, bias_ref, heads_ref,
):
    group = pl.program_id(0)

    @pl.when(group == 0)
    def _():
        fill_bias(bias_ref, index_ref, begin_ref)

    for core in range(2):

        @pl.when(core_ref[0] == core)
        def _():
            for slot in range(2):
                rows = pl.ds(slot * BLOCK, BLOCK)
                span = KEY_BLOCKS[core][slot] * BLOCK
                keys = k_ref[0, :span, :]
                values = v_ref[0, :span, :]
                bias = bias_ref[:span, slot * BLOCK : (slot + 1) * BLOCK]
                for j in range(GROUP):
                    scores = dot(keys, q_ref[j, rows, :], 1, 1) + bias
                    highest = jnp.max(scores, axis=0, keepdims=True)
                    weights = jnp.exp(scores - highest)
                    total = jnp.sum(weights, axis=0, keepdims=True)
                    mixed = dot(values, weights.astype(BF16), 0, 0) / total
                    heads_ref[group * GROUP + j, rows, :] = mixed.T.astype(BF16)
                    lse_ref[0, j : j + 1, rows] = highest + jnp.log(total)

    @pl.when(group == KV_HEADS - 1)
    def _():
        att = jnp.concatenate([heads_ref[h] for h in range(HEADS)], axis=1)
        att_ref[...] = att
        mid = x_ref[...].astype(F32) + dot(att, wo_ref[...])
        mid_ref[...] = mid
        nm_ref[...] = (mid * level_of(mid) * gain_ref[...]).astype(BF16)


def mlp_kernel(nm_ref, og_ref, wg_ref, wu_ref, wd_ref, out_ref, gnm_ref, act_ref, ggu_ref):
    nm, og = nm_ref[...], og_ref[...]
    hidden = wg_ref.shape[1]
    gate = dot(nm, wg_ref[...])
    up = dot(nm, wu_ref[...])
    sig = jax.nn.sigmoid(gate)
    silu = gate * sig
    act = (silu * up).astype(BF16)
    act_ref[...] = act
    grad_act = dot(og, wd_ref[...], 1, 1)
    grad_gate = (grad_act * up * sig * (1.0 + gate * (1.0 - sig))).astype(BF16)
    grad_up = (grad_act * silu).astype(BF16)
    ggu_ref[:, :hidden] = grad_gate
    ggu_ref[:, hidden:] = grad_up
    gnm = dot(grad_gate, wg_ref[...], 1, 1) + dot(grad_up, wu_ref[...], 1, 1)
    gnm_ref[...] = gnm.astype(gnm_ref.dtype)
    out_ref[...] = dot(act, wd_ref[...]).astype(out_ref.dtype)


def mid_back_kernel(
    og_ref, mid_ref, own_ref, got_ref, gain_ref, wo_ref, gmid_ref, gb_ref, gatt_ref, ggain_ref
):
    mid = mid_ref[...]
    level = level_of(mid)
    gnm = own_ref[...] + got_ref[...].astype(F32)
    scaled = gnm * gain_ref[...]
    ggain_ref[...] = jnp.sum(gnm * mid * level, axis=0, keepdims=True)
    inner = jnp.sum(scaled * mid, axis=1, keepdims=True)
    gmid = og_ref[...].astype(F32) + scaled * level - mid * (level**3 * inner / D)
    gmid_ref[...] = gmid
    gb = gmid.astype(BF16)
    gb_ref[...] = gb
    gatt = dot(gb, wo_ref[...], 1, 1).astype(BF16)
    for h in range(HEADS):
        gatt_ref[h] = gatt[:, h * HDIM : (h + 1) * HDIM]


def attend_back_kernel(
    core_ref, index_ref, begin_ref, q_ref, k_ref, v_ref, gatt_ref, lse_ref,
    dq_ref, mine_ref, other_ref, bias_ref, dkv_ref,
):
    @pl.when(pl.program_id(0) == 0)
    def _():
        fill_bias(bias_ref, index_ref, begin_ref)

    for core in range(2):

        @pl.when(core_ref[0] == core)
        def _():
            dkv_ref[...] = jnp.zeros_like(dkv_ref)
            for slot in range(2):
                rows = pl.ds(slot * BLOCK, BLOCK)
                span = KEY_BLOCKS[core][slot] * BLOCK
                keys = k_ref[0, :span, :]
                values = v_ref[0, :span, :]
                bias = bias_ref[:span, slot * BLOCK : (slot + 1) * BLOCK]
                for j in range(GROUP):
                    queries = q_ref[j, rows, :]
                    grads = gatt_ref[j, rows, :]
                    scores = dot(keys, queries, 1, 1) + bias
                    probs = jnp.exp(scores - lse_ref[0, j : j + 1, rows])
                    dprobs = dot(values, grads, 1, 1)
                    inner = jnp.sum(probs * dprobs, axis=0, keepdims=True)
                    dscores = (probs * (dprobs - inner)).astype(BF16)
                    dkv_ref[1, :span, :] += dot(probs.astype(BF16), grads)
                    dkv_ref[0, :span, :] += dot(dscores, queries)
                    dq_ref[j, rows, :] = dot(dscores, keys, 0, 0) * SCALE
            for kind in range(2):
                for slot in range(2):
                    rows = pl.ds(slot * BLOCK, BLOCK)
                    here, there = HELD[core][slot], HELD[1 - core][slot]
                    mine_ref[kind, 0, rows, :] = dkv_ref[kind, here * BLOCK : (here + 1) * BLOCK, :]
                    other_ref[kind, 0, rows, :] = dkv_ref[
                        kind, there * BLOCK : (there + 1) * BLOCK, :
                    ].astype(BF16)


def joined_back_kernel(
    dq_ref, mine_ref, got_ref, cos_ref, sin_ref, w0_ref, w1_ref, x_ref, gain_ref, gmid_ref,
    gj0_ref, gj1_ref, grad_ref, ggain_ref,
):
    cosine, sine = cos_ref[...], sin_ref[...]
    zero = jnp.zeros((LOCAL, HDIM), F32)

    def head(kind, h):
        if h is None:
            return zero
        if kind == "q":
            return dq_ref[h]
        which = 0 if kind == "k" else 1
        return mine_ref[which, h] + got_ref[which, h].astype(F32)

    layout = (
        [("q", h) for h in range(9)] + [("k", h) for h in range(3)] + [("v", h) for h in range(3)],
        [("q", h) for h in range(9, 15)] + [("q", None)] * 3 + [("k", 3), ("k", 4), ("k", None)]
        + [("v", 3), ("v", 4), ("v", None)],
    )
    gnm = None
    for heads, gj_ref, w_ref in zip(layout, (gj0_ref, gj1_ref), (w0_ref, w1_ref)):
        parts = []
        for at in range(0, 12, 2):
            chunk = jnp.concatenate([head(*heads[at]), head(*heads[at + 1])], axis=1)
            parts.append((chunk * cosine - turn(chunk) * sine).astype(BF16))
        parts += [head(*heads[at]).astype(BF16) for at in range(12, 15)]
        gj = jnp.concatenate(parts, axis=1)
        gj_ref[...] = gj
        product = dot(gj, w_ref[...], 1, 1)
        gnm = product if gnm is None else gnm + product
    rows = x_ref[...].astype(F32)
    level = level_of(rows)
    scaled = gnm * gain_ref[...]
    ggain_ref[...] = jnp.sum(gnm * rows * level, axis=0, keepdims=True)
    inner = jnp.sum(scaled * rows, axis=1, keepdims=True)
    grad = gmid_ref[...] + scaled * level - rows * (level**3 * inner / D)
    grad_ref[...] = grad.astype(BF16)


def shape(dims, dtype=BF16):
    return jax.ShapeDtypeStruct(dims, dtype)


def whole(dims):
    return pl.BlockSpec(dims, lambda *_: (0,) * len(dims))


def cost(flops, moved):
    return pl.CostEstimate(flops=int(flops), bytes_accessed=int(moved), transcendentals=0)


SMEM_SPEC = pl.BlockSpec(memory_space=pltpu.SMEM)


def project(x, gain, cosine, sine, w0, w1):
    return pl.pallas_call(
        qkv_kernel,
        out_shape=(
            shape((LOCAL, D)), shape((HEADS, LOCAL, HDIM)), shape((2 * KV_HEADS, LOCAL, HDIM))
        ),
        compiler_params=params(),
        cost_estimate=cost(4 * LOCAL * D * D, 10e6),
    )(x, gain, cosine, sine, w0, w1)


def attend(core, index, begin, q, kv, x, gain, wo):
    per_group = lambda *dims: pl.BlockSpec(dims, lambda g: (g, 0, 0))
    return pl.pallas_call(
        attend_kernel,
        grid=(KV_HEADS,),
        in_specs=[
            SMEM_SPEC, whole((1, LOCAL)), whole((1, LOCAL)), per_group(GROUP, LOCAL, HDIM),
            per_group(1, MAXLEN, HDIM),
            pl.BlockSpec((1, MAXLEN, HDIM), lambda g: (g + KV_HEADS, 0, 0)),
            whole((LOCAL, D)), whole((1, D)), whole((D, D)),
        ],
        out_specs=(
            whole((LOCAL, D)), whole((LOCAL, D)), whole((LOCAL, D)), per_group(1, 8, LOCAL)
        ),
        out_shape=(
            shape((LOCAL, D)), shape((LOCAL, D), F32), shape((LOCAL, D)),
            shape((KV_HEADS, 8, LOCAL), F32),
        ),
        scratch_shapes=[
            pltpu.VMEM((MAXLEN, LOCAL), F32), pltpu.VMEM((HEADS, LOCAL, HDIM), BF16)
        ],
        compiler_params=params(),
        cost_estimate=cost(12e9, 12e6),
    )(core, index, begin, q, kv, kv, x, gain, wo)


def feed_forward(nm, og, wg, wu, wd, dtype):
    hidden = wg.shape[1]
    rows = lambda width: pl.BlockSpec((BLOCK, width), lambda i: (i, 0))
    return pl.pallas_call(
        mlp_kernel,
        grid=(LOCAL // BLOCK,),
        in_specs=[
            rows(D), rows(D), whole((D, hidden)), whole((D, hidden)), whole((hidden, D))
        ],
        out_specs=(rows(D), rows(D), rows(hidden), rows(2 * hidden)),
        out_shape=(
            shape((LOCAL, D), dtype), shape((LOCAL, D), dtype), shape((LOCAL, hidden)),
            shape((LOCAL, 2 * hidden)),
        ),
        compiler_params=params(),
        cost_estimate=cost(12 * LOCAL * D * hidden, 16e6),
    )(nm, og, wg, wu, wd)


def mid_back(og, mid, own, got, gain, wo):
    return pl.pallas_call(
        mid_back_kernel,
        out_shape=(
            shape((LOCAL, D), F32), shape((LOCAL, D)), shape((HEADS, LOCAL, HDIM)),
            shape((1, D), F32),
        ),
        compiler_params=params(),
        cost_estimate=cost(2 * LOCAL * D * D, 14e6),
    )(og, mid, own, got, gain, wo)


def attend_back(core, index, begin, q, kv, gatt, lse):
    per_group = lambda *dims: pl.BlockSpec(dims, lambda g: (g, 0, 0))
    pair = pl.BlockSpec((2, 1, LOCAL, HDIM), lambda g: (0, g, 0, 0))
    return pl.pallas_call(
        attend_back_kernel,
        grid=(KV_HEADS,),
        in_specs=[
            SMEM_SPEC, whole((1, LOCAL)), whole((1, LOCAL)), per_group(GROUP, LOCAL, HDIM),
            per_group(1, MAXLEN, HDIM),
            pl.BlockSpec((1, MAXLEN, HDIM), lambda g: (g + KV_HEADS, 0, 0)),
            per_group(GROUP, LOCAL, HDIM), per_group(1, 8, LOCAL),
        ],
        out_specs=(per_group(GROUP, LOCAL, HDIM), pair, pair),
        out_shape=(
            shape((HEADS, LOCAL, HDIM), F32), shape((2, KV_HEADS, LOCAL, HDIM), F32),
            shape((2, KV_HEADS, LOCAL, HDIM)),
        ),
        scratch_shapes=[
            pltpu.VMEM((MAXLEN, LOCAL), F32), pltpu.VMEM((2, MAXLEN, HDIM), F32)
        ],
        compiler_params=params(),
        cost_estimate=cost(30e9, 20e6),
    )(core, index, begin, q, kv, kv, gatt, lse)


def joined_back(dq, mine, got, cosine, sine, w0, w1, x, gain, gmid):
    return pl.pallas_call(
        joined_back_kernel,
        out_shape=(
            shape((LOCAL, D)), shape((LOCAL, D)), shape((LOCAL, D)), shape((1, D), F32)
        ),
        compiler_params=params(),
        cost_estimate=cost(4 * LOCAL * D * D, 20e6),
    )(dq, mine, got, cosine, sine, w0, w1, x, gain, gmid)


def swap(array, axis):
    return lax.ppermute(array, axis, [(0, 1), (1, 0)])


def stages(count):
    found, stride = [], 1
    for size in (2,) + (4,) * 16:
        size = min(size, count // stride)
        if size < 2:
            break
        found.append((stride, size))
        stride *= size
    return found


def shift_pairs(count, stride, size, step):
    pairs = []
    for i in range(count):
        digit = i // stride % size
        pairs.append((i, i + ((digit + step) % size - digit) * stride))
    return pairs


def sum_over_dp(array, count):
    steps = stages(count)
    sizes = [size for _, size in steps]
    rows, cols = array.shape
    place = lax.axis_index("dp")
    total = array.reshape(*sizes, rows // count, cols)
    for stride, size in steps:
        digit = place // stride % size
        kept = lax.dynamic_index_in_dim(total, digit, 0, keepdims=False).astype(F32)
        for step in range(1, size):
            sent = lax.dynamic_index_in_dim(total, (digit + step) % size, 0, keepdims=False)
            kept = kept + lax.ppermute(
                sent.astype(BF16), "dp", shift_pairs(count, stride, size, step)
            ).astype(F32)
        total = kept
    total = total.astype(BF16)
    for stride, size in reversed(steps):
        digit = place // stride % size
        spread = jnp.zeros((size,) + total.shape, BF16)
        spread = lax.dynamic_update_index_in_dim(spread, total, digit, 0)
        for step in range(1, size):
            got = lax.ppermute(total, "dp", shift_pairs(count, stride, size, step))
            spread = lax.dynamic_update_index_in_dim(spread, got, (digit - step) % size, 0)
        total = spread
    return total.reshape(rows, cols).astype(F32)


def segment_begin(segment):
    index = jnp.arange(segment.shape[0], dtype=jnp.int32)
    is_start = jnp.concatenate([jnp.ones((1,), dtype=bool), segment[1:] != segment[:-1]])
    return lax.cummax(jnp.where(is_start, index, jnp.zeros_like(index)), axis=0)


def rope_tables(position):
    half_dim = HDIM // 2
    frequency = ROPE_BASE ** (-(jnp.arange(half_dim, dtype=F32) * 2.0 / HDIM))
    angles = position.astype(F32)[:, None] * frequency[None, :]
    cosine, sine = jnp.cos(angles), jnp.sin(angles)
    return (
        jnp.concatenate([cosine] * 4, axis=1),
        jnp.concatenate([-sine, sine, -sine, sine], axis=1),
    )


def per_device(
    count,
    hidden_in,
    query_weight,
    key_weight,
    value_weight,
    output_weight,
    gate_weight,
    up_weight,
    down_weight,
    attn_gain,
    ffn_gain,
    out_grad,
    segment_ids,
):
    col, row = lax.axis_index("col"), lax.axis_index("row")
    first, top = col == 0, row == 0
    hidden = gate_weight.shape[1]

    def ordered(own, got):
        return jnp.where(first, own, got), jnp.where(first, got, own)

    def own_tokens(array):
        outer = jnp.concatenate([array[:BLOCK], array[3 * BLOCK :]], axis=0)
        return ordered(outer, array[BLOCK : 3 * BLOCK])

    def in_window(own, got, axis=0):
        outer, inner = ordered(own, got)
        return jnp.concatenate(
            [
                lax.slice_in_dim(outer, 0, BLOCK, axis=axis),
                inner,
                lax.slice_in_dim(outer, BLOCK, LOCAL, axis=axis),
            ],
            axis=axis,
        )

    def token_rows(array):
        own, other = own_tokens(array)
        return jnp.concatenate(ordered(own, swap(other, "col")), axis=1)

    def feature_cols(array):
        keep, send = ordered(array[:, :HALF], array[:, HALF:])
        return in_window(keep, swap(send, "col"))

    def joined_by_col(own, axis):
        return jnp.concatenate(ordered(own, swap(own, "col")), axis=axis)

    joined_weight = jnp.concatenate(
        [query_weight[:, 0], key_weight[:, 0], value_weight[:, 0]], axis=1
    )
    joined_far = swap(joined_weight, "row")
    x = token_rows(hidden_in)
    gains = joined_by_col(jnp.stack([attn_gain, ffn_gain]), 1).astype(F32)
    gain_in, gain_mid = gains[:1], gains[1:]
    near_weight = joined_by_col(joined_weight, 0)
    far_weight = joined_by_col(joined_far, 0)
    w0 = jnp.where(top, near_weight, far_weight)
    w1 = jnp.where(top, far_weight, near_weight)
    out_weight = output_weight[0]
    out_far = swap(out_weight, "row")
    near_out = joined_by_col(out_weight, 1)
    far_out = joined_by_col(out_far, 1)
    wo = jnp.concatenate(
        [
            jnp.where(top, near_out, far_out),
            jnp.where(top, far_out, near_out)[: (HEADS - SLOTS) * HDIM],
        ],
        axis=0,
    )

    segment = jnp.where(col == row, segment_ids, swap(segment_ids, "col"))
    begin, _ = own_tokens(segment_begin(segment))
    index, _ = own_tokens(jnp.arange(MAXLEN, dtype=jnp.int32))
    cosine, sine = rope_tables(index - begin)
    index, begin = index[None], begin[None]
    core = col.astype(jnp.int32)[None]

    nm_in, q, kv_own = project(x, gain_in, cosine, sine, w0, w1)
    kv = in_window(kv_own, swap(kv_own, "col"), 1)
    att, mid, nm, lse = attend(core, index, begin, q, kv, x, gain_mid, wo)

    og = token_rows(out_grad)
    og_far = swap(og, "row")
    wg = joined_by_col(gate_weight, 0)
    wu = joined_by_col(up_weight, 0)
    wd = joined_by_col(down_weight, 1)
    nm_far = swap(nm, "row")
    out_own, gnm_own, act, ggu = feed_forward(nm, og, wg, wu, wd, F32)
    out_far, gnm_far, act_far, ggu_far = feed_forward(nm_far, og_far, wg, wu, wd, BF16)
    gnm_got = swap(gnm_far, "row")
    out_got = swap(out_far, "row")

    def halves(array):
        return ordered(array[:, :HALF], array[:, HALF:])

    def weight_grads(rows, grads):
        keep, send = rows
        return dot(keep, grads, 0, 0), dot(send, grads, 0, 0).astype(BF16)

    nm_all = jnp.concatenate([nm, nm_far], axis=0)
    og_all = jnp.concatenate([og, og_far], axis=0)
    act_all = jnp.concatenate([act, act_far], axis=0)
    ggu_all = jnp.concatenate([ggu, ggu_far], axis=0)
    og_keep, og_send = halves(og_all)
    down_keep, down_send = dot(act_all, og_keep, 0, 0), dot(act_all, og_send, 0, 0).astype(BF16)
    down_sum = down_keep + swap(down_send, "col").astype(F32)
    mlp_keep, mlp_send = weight_grads(halves(nm_all), ggu_all)
    mlp_sum = mlp_keep + swap(mlp_send, "col").astype(F32)
    down_grad = sum_over_dp(down_sum, count)
    mlp_grad = sum_over_dp(
        jnp.concatenate([mlp_sum[:, :hidden], mlp_sum[:, hidden:]], axis=0), count
    )

    block_out = feature_cols((mid + out_own + out_got.astype(F32)).astype(BF16))

    gmid, gb, gatt, ggain_mid = mid_back(og, mid, gnm_own, gnm_got, gain_mid, wo)

    gb_keep, gb_send = halves(gb)
    wo_keep = dot(att, gb_keep, 0, 0)
    wo_send = dot(att, gb_send, 0, 0).astype(BF16)
    wo_sum = wo_keep + swap(wo_send, "col").astype(F32)

    def row_blocks(low, high):
        return jnp.where(top, low, high), jnp.where(top, high, low)

    wo_low = wo_sum[: SLOTS * HDIM]
    wo_high = jnp.pad(wo_sum[SLOTS * HDIM :], ((0, (2 * SLOTS - HEADS) * HDIM), (0, 0)))
    wo_near, wo_far = row_blocks(wo_low, wo_high)
    wo_near = wo_near + swap(wo_far.astype(BF16), "row").astype(F32)
    wo_grad = sum_over_dp(wo_near, count)

    dq, dkv_own, dkv_other = attend_back(core, index, begin, q, kv, gatt, lse)
    dkv_got = swap(dkv_other, "col")
    gj0, gj1, grad, ggain_in = joined_back(
        dq, dkv_own, dkv_got, cosine, sine, w0, w1, x, gain_in, gmid
    )
    nm_keep, nm_send = halves(nm_in)
    gj_near, gj_far = row_blocks(gj0, gj1)
    far_keep, far_send = weight_grads((nm_keep, nm_send), gj_far)
    near_keep, near_send = weight_grads((nm_keep, nm_send), gj_near)
    far_sum = far_keep + swap(far_send, "col").astype(F32)
    near_sum = near_keep + swap(near_send, "col").astype(F32)
    near_sum = near_sum + swap(far_sum.astype(BF16), "row").astype(F32)
    padded = jnp.pad(near_sum, ((0, 512 - HALF), (0, 0)))
    joined_grad = sum_over_dp(padded, count)[:HALF]

    input_grad = feature_cols(grad)
    gain_grads = lax.psum(jnp.concatenate([ggain_in, ggain_mid], axis=0), ("dp", "row", "col"))
    gain_grads = jnp.where(first, gain_grads[:, :HALF], gain_grads[:, HALF:])

    query_cols = SLOTS * HDIM
    key_cols = SLOTS // GROUP * HDIM
    return (
        block_out,
        input_grad,
        joined_grad[:, :query_cols][:, None, :],
        joined_grad[:, query_cols : query_cols + key_cols][:, None, :],
        joined_grad[:, query_cols + key_cols :][:, None, :],
        wo_grad[None],
        mlp_grad[:HALF],
        mlp_grad[HALF:],
        down_grad,
        gain_grads[0],
        gain_grads[1],
    )


def solution(mesh):
    return jax.shard_map(
        functools.partial(per_device, mesh.shape["dp"]),
        mesh=mesh,
        in_specs=(
            P(("dp", "row"), "col"),
            P("col", "row", None),
            P("col", "row", None),
            P("col", "row", None),
            P("row", None, "col"),
            P("col", "row"),
            P("col", "row"),
            P("row", "col"),
            P("col"),
            P("col"),
            P(("dp", "row"), "col"),
            P(("dp", "col")),
        ),
        out_specs=(
            P(("dp", "row"), "col"),
            P(("dp", "row"), "col"),
            P("col", "row", None),
            P("col", "row", None),
            P("col", "row", None),
            P("row", None, "col"),
            P("col", "row"),
            P("col", "row"),
            P("row", "col"),
            P("col"),
            P("col"),
        ),
        check_vma=False,
    )
```

```python
import functools
import math

import jax
import jax.numpy as jnp
from jax import lax
from jax.experimental import pallas as pl
from jax.experimental.pallas import tpu as pltpu
from jax.sharding import PartitionSpec as P

D = 960
HALF = D // 2
HDIM = 64
ROT = HDIM // 2
GROUP = 3
GROUPS = 3
QUERY = GROUPS * GROUP * HDIM
KEY = GROUPS * HDIM
MAXLEN = 1024
BLOCK = MAXLEN // 4
LOCAL = 2 * BLOCK
LIVE = (3, 2)

NORM_EPS = 1e-05
ROPE_BASE = 100000.0
MASKED_SCORE = -1e30
SCALE = 1.0 / math.sqrt(HDIM)
BF16 = jnp.bfloat16
F32 = jnp.float32
VMEM_BYTES = 56 * 1024 * 1024

HELD = ((0, 3), (1, 2))
LAID = ((0, 3, 1, 2), (0, 1, 2))
SPANS = ((1, 4), (2, 3))


def dot(left, right, left_dim=1, right_dim=0):
    return lax.dot_general(
        left, right, (((left_dim,), (right_dim,)), ((), ())), preferred_element_type=F32
    )


def shape(dims, dtype=BF16):
    return jax.ShapeDtypeStruct(dims, dtype)


def whole(dims):
    return pl.BlockSpec(dims, lambda *_: (0,) * len(dims))


SMEM_SPEC = pl.BlockSpec(memory_space=pltpu.SMEM)


def run(kernel, ins, outs, flops, grid=None, in_specs=None, out_specs=None, scratch=(), after=()):
    moved = sum(a.size * a.dtype.itemsize for a in ins)
    moved += sum(math.prod(o.shape) * jnp.dtype(o.dtype).itemsize for o in outs)
    if in_specs is None:
        in_specs = [whole(a.shape) for a in ins]
    if out_specs is None:
        out_specs = [whole(o.shape) for o in outs]
    count = len(ins)

    def body(*refs):
        kernel(*refs[:count], *refs[count + len(after) :])

    return pl.pallas_call(
        body,
        grid=grid if grid is not None else (1,),
        in_specs=list(in_specs) + [pl.BlockSpec(memory_space=pl.ANY)] * len(after),
        out_specs=tuple(out_specs),
        out_shape=tuple(outs),
        scratch_shapes=list(scratch),
        compiler_params=pltpu.CompilerParams(vmem_limit_bytes=VMEM_BYTES),
        cost_estimate=pl.CostEstimate(
            flops=int(flops), bytes_accessed=int(moved), transcendentals=0
        ),
    )(*ins, *after)


def level_of(own, got):
    total = jnp.sum(own * own, axis=0, keepdims=True) + jnp.sum(got * got, axis=0, keepdims=True)
    return lax.rsqrt(total / D + NORM_EPS)


def project_heads(nm, cos_ref, sin_ref, own_ref, got_ref, q_ref, kv_ref):
    cosine, sine = cos_ref[...], sin_ref[...]
    joined = dot(own_ref[...], nm[:HALF]) + dot(got_ref[...], nm[HALF:])
    for at in range(0, QUERY + KEY, HDIM):
        low, high = joined[at : at + ROT], joined[at + ROT : at + HDIM]
        parts = (low * cosine - high * sine, high * cosine + low * sine)
        for part, turned in enumerate(parts):
            turned = turned.astype(BF16)
            if at < QUERY:
                turned = (turned.astype(F32) * SCALE).astype(BF16)
                q_ref[at + part * ROT : at + (part + 1) * ROT, :] = turned
            else:
                row = at - QUERY + part * ROT
                kv_ref[row : row + ROT, :] = turned
    kv_ref[KEY:, :] = joined[QUERY + KEY :].astype(BF16)


def project_near_kernel(
    xo_ref, xg_ref, go_ref, gg_ref, cos_ref, sin_ref, own_ref, got_ref, nm_ref, q_ref, kv_ref
):
    own, got = xo_ref[...].astype(F32), xg_ref[...].astype(F32)
    level = level_of(own, got)
    nm_ref[:HALF, :] = (own * level * go_ref[...]).astype(BF16)
    nm_ref[HALF:, :] = (got * level * gg_ref[...]).astype(BF16)
    project_heads(nm_ref[...], cos_ref, sin_ref, own_ref, got_ref, q_ref, kv_ref)


def project_far_kernel(nm_ref, cos_ref, sin_ref, own_ref, got_ref, q_ref, kv_ref):
    project_heads(nm_ref[...], cos_ref, sin_ref, own_ref, got_ref, q_ref, kv_ref)


def laid(core, own, got, axis):
    if core == 0:
        return jnp.concatenate([own, got], axis=axis)
    return jnp.concatenate([lax.slice_in_dim(got, 0, BLOCK, axis=axis), own], axis=axis)


def fill_bias(core, bias_ref, begin_ref):
    for at, block in enumerate(LAID[core]):
        for slot in range(2):
            cols = slice(slot * BLOCK, (slot + 1) * BLOCK)
            key = block * BLOCK + lax.broadcasted_iota(jnp.int32, (BLOCK, BLOCK), 0)
            query = HELD[core][slot] * BLOCK + lax.broadcasted_iota(jnp.int32, (BLOCK, BLOCK), 1)
            allowed = (key >= begin_ref[:, cols]) & (key <= query)
            bias_ref[at * BLOCK : (at + 1) * BLOCK, cols] = jnp.where(allowed, 0.0, MASKED_SCORE)


def attend_kernel(
    where_ref, begin_ref, q_ref, ko_ref, vo_ref, kg_ref, vg_ref, att_ref, lse_ref, bias_ref
):
    group = pl.program_id(0)
    live = group < where_ref[1]

    @pl.when(jnp.logical_not(live))
    def _():
        att_ref[...] = jnp.zeros_like(att_ref)
        lse_ref[...] = jnp.zeros_like(lse_ref)

    for core in range(2):

        @pl.when(live & (where_ref[0] == core))
        def _():
            @pl.when(group == 0)
            def _():
                fill_bias(core, bias_ref, begin_ref)

            keys = laid(core, ko_ref[...], kg_ref[...], 1).T
            values = laid(core, vo_ref[...], vg_ref[...], 1)
            for slot in range(2):
                cols = slice(slot * BLOCK, (slot + 1) * BLOCK)
                span = SPANS[core][slot] * BLOCK
                for j in range(GROUP):
                    heads = slice(j * HDIM, (j + 1) * HDIM)
                    scores = dot(keys[:span], q_ref[heads, cols]) + bias_ref[:span, cols]
                    highest = jnp.max(scores, axis=0, keepdims=True)
                    weights = jnp.exp(scores - highest)
                    total = jnp.sum(weights, axis=0, keepdims=True)
                    mixed = dot(values[:, :span], weights.astype(BF16)) / total
                    att_ref[heads, cols] = mixed.astype(BF16)
                    lse_ref[0, j : j + 1, cols] = highest + jnp.log(total)


def mid_kernel(
    near_ref, far_ref, no_ref, ng_ref, fo_ref, fg_ref, xo_ref, xg_ref, go_ref, gg_ref,
    mid_ref, nm_ref,
):
    near, far = near_ref[...], far_ref[...]
    own = xo_ref[...].astype(F32) + dot(no_ref[...], near, 0, 0) + dot(fo_ref[...], far, 0, 0)
    got = xg_ref[...].astype(F32) + dot(ng_ref[...], near, 0, 0) + dot(fg_ref[...], far, 0, 0)
    mid_ref[:HALF, :] = own
    mid_ref[HALF:, :] = got
    level = level_of(own, got)
    nm_ref[:HALF, :] = (own * level * go_ref[...]).astype(BF16)
    nm_ref[HALF:, :] = (got * level * gg_ref[...]).astype(BF16)


def mlp_kernel(
    nm_ref, og_ref, wgo_ref, wgg_ref, wuo_ref, wug_ref, wdo_ref, wdg_ref,
    out_ref, gnm_ref, act_ref, gg_ref, gu_ref, out_sum, gnm_sum,
):
    step = pl.program_id(0)

    def inward(own_ref, got_ref, rows_ref):
        return dot(own_ref[...], rows_ref[:HALF, :], 0, 0) + dot(
            got_ref[...], rows_ref[HALF:, :], 0, 0
        )

    @pl.when(step == 0)
    def _():
        out_sum[...] = jnp.zeros_like(out_sum)
        gnm_sum[...] = jnp.zeros_like(gnm_sum)

    gate = inward(wgo_ref, wgg_ref, nm_ref)
    up = inward(wuo_ref, wug_ref, nm_ref)
    grad_act = inward(wdo_ref, wdg_ref, og_ref)
    sig = jax.nn.sigmoid(gate)
    silu = gate * sig
    act = (silu * up).astype(BF16)
    grad_gate = (grad_act * up * sig * (1.0 + gate * (1.0 - sig))).astype(BF16)
    grad_up = (grad_act * silu).astype(BF16)
    act_ref[...] = act
    gg_ref[...] = grad_gate
    gu_ref[...] = grad_up
    gnm_sum[:HALF, :] += dot(wgo_ref[...], grad_gate) + dot(wuo_ref[...], grad_up)
    gnm_sum[HALF:, :] += dot(wgg_ref[...], grad_gate) + dot(wug_ref[...], grad_up)
    out_sum[:HALF, :] += dot(wdo_ref[...], act)
    out_sum[HALF:, :] += dot(wdg_ref[...], act)

    @pl.when(step == pl.num_programs(0) - 1)
    def _():
        out_ref[...] = out_sum[...].astype(out_ref.dtype)
        gnm_ref[...] = gnm_sum[...].astype(gnm_ref.dtype)


def grads_kernel(rows_ref, rows_far_ref, cols_ref, cols_far_ref, keep_ref, send_ref):
    for half, out_ref in enumerate((keep_ref, send_ref)):
        rows = slice(half * HALF, (half + 1) * HALF)
        product = dot(rows_ref[rows, :], cols_ref[...], 1, 1)
        product += dot(rows_far_ref[rows, :], cols_far_ref[...], 1, 1)
        out_ref[...] = product.astype(BF16)


def mid_back_kernel(
    og_ref, mid_ref, part_ref, back_ref, go_ref, gg_ref, no_ref, ng_ref, fo_ref, fg_ref,
    gmid_ref, gb_ref, near_ref, far_ref, ggain_ref,
):
    own, got = mid_ref[:HALF, :], mid_ref[HALF:, :]
    level = level_of(own, got)
    gnm = part_ref[...] + back_ref[...].astype(F32)
    scaled_own, scaled_got = gnm[:HALF] * go_ref[...], gnm[HALF:] * gg_ref[...]
    inner = jnp.sum(scaled_own * own, axis=0, keepdims=True)
    inner += jnp.sum(scaled_got * got, axis=0, keepdims=True)
    pull = level**3 * inner / D
    for rows, mid, scaled in (
        (slice(0, HALF), own, scaled_own), (slice(HALF, D), got, scaled_got)
    ):
        ggain_ref[rows, :] = jnp.sum(gnm[rows] * mid * level, axis=1, keepdims=True)
        gmid = og_ref[rows, :].astype(F32) + scaled * level - mid * pull
        gmid_ref[rows, :] = gmid
        gb_ref[rows, :] = gmid.astype(BF16)
    gb_own, gb_got = gb_ref[:HALF, :], gb_ref[HALF:, :]
    near_ref[...] = (dot(no_ref[...], gb_own) + dot(ng_ref[...], gb_got)).astype(BF16)
    far_ref[...] = (dot(fo_ref[...], gb_own) + dot(fg_ref[...], gb_got)).astype(BF16)


def attend_back_kernel(
    where_ref, begin_ref, q_ref, ko_ref, vo_ref, kg_ref, vg_ref, gatt_ref, lse_ref,
    dq_ref, own_ref, got_ref, bias_ref, dk_ref, dv_ref,
):
    group = pl.program_id(0)
    live = group < where_ref[1]

    @pl.when(jnp.logical_not(live))
    def _():
        dq_ref[...] = jnp.zeros_like(dq_ref)
        own_ref[...] = jnp.zeros_like(own_ref)
        got_ref[...] = jnp.zeros_like(got_ref)

    for core in range(2):

        @pl.when(live & (where_ref[0] == core))
        def _():
            @pl.when(group == 0)
            def _():
                fill_bias(core, bias_ref, begin_ref)

            keys_t = laid(core, ko_ref[...], kg_ref[...], 1)
            keys = keys_t.T
            values = laid(core, vo_ref[...], vg_ref[...], 1).T
            dk_ref[...] = jnp.zeros_like(dk_ref)
            dv_ref[...] = jnp.zeros_like(dv_ref)
            for slot in range(2):
                cols = slice(slot * BLOCK, (slot + 1) * BLOCK)
                span = SPANS[core][slot] * BLOCK
                for j in range(GROUP):
                    heads = slice(j * HDIM, (j + 1) * HDIM)
                    queries, grads = q_ref[heads, cols], gatt_ref[heads, cols]
                    scores = dot(keys[:span], queries) + bias_ref[:span, cols]
                    probs = jnp.exp(scores - lse_ref[0, j : j + 1, cols])
                    dprobs = dot(values[:span], grads)
                    inner = jnp.sum(probs * dprobs, axis=0, keepdims=True)
                    dscores = (probs * (dprobs - inner)).astype(BF16)
                    dv_ref[:span, :] += dot(probs.astype(BF16), grads.T)
                    dk_ref[:span, :] += dot(dscores, queries.T)
                    dq_ref[heads, cols] = dot(keys_t[:, :span], dscores) * SCALE
            for kind, grad_ref in enumerate((dk_ref, dv_ref)):
                if core == 0:
                    own_ref[kind, 0] = grad_ref[:LOCAL, :].T
                    got_ref[kind, 0] = grad_ref[LOCAL:, :].T.astype(BF16)
                else:
                    own_ref[kind, 0] = grad_ref[BLOCK : BLOCK + LOCAL, :].T
                    got_ref[kind, 0, :, :BLOCK] = grad_ref[:BLOCK, :].T.astype(BF16)
                    got_ref[kind, 0, :, BLOCK:] = jnp.zeros((HDIM, BLOCK), BF16)


def turn_back(cos_ref, sin_ref, dq_ref, own_ref, got_ref, gj_ref):
    cosine, sine = cos_ref[...], sin_ref[...]

    def back(at, grad):
        low, high = grad[:ROT], grad[ROT:]
        gj_ref[at : at + ROT, :] = (low * cosine + high * sine).astype(BF16)
        gj_ref[at + ROT : at + HDIM, :] = (high * cosine - low * sine).astype(BF16)

    for at in range(0, QUERY, HDIM):
        back(at, dq_ref[at : at + HDIM, :])
    for g in range(GROUPS):
        back(QUERY + g * HDIM, own_ref[0, g] + got_ref[0, g].astype(F32))
        at = QUERY + KEY + g * HDIM
        gj_ref[at : at + HDIM, :] = (own_ref[1, g] + got_ref[1, g].astype(F32)).astype(BF16)


def joined_far_kernel(
    dq_ref, own_ref, got_ref, cos_ref, sin_ref, wo_ref, wg_ref, nm_ref,
    gnm_ref, keep_ref, send_ref, gj_ref,
):
    turn_back(cos_ref, sin_ref, dq_ref, own_ref, got_ref, gj_ref)
    gj = gj_ref[...]
    send_ref[...] = dot(gj, nm_ref[HALF:, :], 1, 1).astype(BF16)
    keep_ref[...] = dot(gj, nm_ref[:HALF, :], 1, 1).astype(BF16)
    gnm_ref[:HALF, :] = dot(wo_ref[...], gj, 0, 0)
    gnm_ref[HALF:, :] = dot(wg_ref[...], gj, 0, 0)


def joined_near_kernel(
    dq_ref, own_ref, got_ref, cos_ref, sin_ref, wo_ref, wg_ref, nm_ref, part_ref, xo_ref, xg_ref,
    go_ref, gg_ref, gmid_ref, keep_ref, send_ref, grad_ref, ggain_ref, gj_ref,
):
    turn_back(cos_ref, sin_ref, dq_ref, own_ref, got_ref, gj_ref)
    gj = gj_ref[...]
    send_ref[...] = dot(gj, nm_ref[HALF:, :], 1, 1).astype(BF16)
    keep_ref[...] = dot(gj, nm_ref[:HALF, :], 1, 1).astype(BF16)
    gnm_own = part_ref[:HALF, :] + dot(wo_ref[...], gj, 0, 0)
    gnm_got = part_ref[HALF:, :] + dot(wg_ref[...], gj, 0, 0)
    own, got = xo_ref[...].astype(F32), xg_ref[...].astype(F32)
    level = level_of(own, got)
    scaled_own, scaled_got = gnm_own * go_ref[...], gnm_got * gg_ref[...]
    inner = jnp.sum(scaled_own * own, axis=0, keepdims=True)
    inner += jnp.sum(scaled_got * got, axis=0, keepdims=True)
    pull = level**3 * inner / D
    for rows, x, gnm, scaled in (
        (slice(0, HALF), own, gnm_own, scaled_own), (slice(HALF, D), got, gnm_got, scaled_got)
    ):
        ggain_ref[rows, :] = jnp.sum(gnm * x * level, axis=1, keepdims=True)
        grad_ref[rows, :] = (gmid_ref[rows, :] + scaled * level - x * pull).astype(BF16)


def per_group(rows, at=0):
    return pl.BlockSpec((rows, LOCAL), lambda g: (g + at, 0))


LSE_SPEC = pl.BlockSpec((1, 8, LOCAL), lambda g: (g, 0, 0))
KV_SPECS = [per_group(HDIM), per_group(HDIM, GROUPS)] * 2
PAIR_SPEC = pl.BlockSpec((2, 1, HDIM, LOCAL), lambda g: (0, g, 0, 0))


def attend(where, begin, q, kv, kv_got, after=()):
    return run(
        attend_kernel,
        (where, begin, q, kv, kv, kv_got, kv_got),
        (shape((QUERY, LOCAL)), shape((GROUPS, 8, LOCAL), F32)),
        6e9,
        grid=(GROUPS,),
        in_specs=[SMEM_SPEC, whole((1, LOCAL)), per_group(GROUP * HDIM)] + KV_SPECS,
        out_specs=(per_group(GROUP * HDIM), LSE_SPEC),
        scratch=[pltpu.VMEM((MAXLEN, LOCAL), F32)],
        after=after,
    )


def attend_back(where, begin, q, kv, kv_got, gatt, lse, after=()):
    return run(
        attend_back_kernel,
        (where, begin, q, kv, kv, kv_got, kv_got, gatt, lse),
        (
            shape((QUERY, LOCAL), F32), shape((2, GROUPS, HDIM, LOCAL), F32),
            shape((2, GROUPS, HDIM, LOCAL)),
        ),
        14e9,
        grid=(GROUPS,),
        in_specs=[SMEM_SPEC, whole((1, LOCAL)), per_group(GROUP * HDIM)]
        + KV_SPECS
        + [per_group(GROUP * HDIM), LSE_SPEC],
        out_specs=(per_group(GROUP * HDIM), PAIR_SPEC, PAIR_SPEC),
        scratch=[
            pltpu.VMEM((MAXLEN, LOCAL), F32), pltpu.VMEM((MAXLEN, HDIM), F32),
            pltpu.VMEM((MAXLEN, HDIM), F32),
        ],
        after=after,
    )


def feed_forward(nm, og, weights, dtype, after=()):
    hidden = weights[0].shape[1]
    chunk = 256
    cols = pl.BlockSpec((HALF, chunk), lambda i: (0, i))
    rows = pl.BlockSpec((chunk, LOCAL), lambda i: (i, 0))
    act = shape((hidden, LOCAL))
    return run(
        mlp_kernel,
        (nm, og) + weights,
        (shape((D, LOCAL), dtype), shape((D, LOCAL), dtype), act, act, act),
        12 * LOCAL * D * hidden,
        grid=(hidden // chunk,),
        in_specs=[whole((D, LOCAL))] * 2 + [cols] * 6,
        out_specs=(whole((D, LOCAL)), whole((D, LOCAL)), rows, rows, rows),
        scratch=[pltpu.VMEM((D, LOCAL), F32)] * 2,
        after=after,
    )


def weight_grads(rows, rows_far, cols, cols_far, after=()):
    hidden = cols.shape[0]
    part = hidden // 2
    taken = pl.BlockSpec((part, LOCAL), lambda i: (i, 0))
    given = pl.BlockSpec((HALF, part), lambda i: (i, 0))
    return run(
        grads_kernel,
        (rows, rows_far, cols, cols_far),
        (shape((2 * HALF, part)),) * 2,
        4 * LOCAL * D * hidden,
        grid=(2,),
        in_specs=[whole((D, LOCAL))] * 2 + [taken] * 2,
        out_specs=(given, given),
        after=after,
    )


def swap(array, axis):
    return lax.ppermute(array, axis, [(0, 1), (1, 0)])


def stages(count):
    found, stride = [], 1
    for size in (2,) + (4,) * 16:
        size = min(size, count // stride)
        if size < 2:
            break
        found.append((stride, size))
        stride *= size
    return found


def shift_pairs(count, stride, size, step):
    pairs = []
    for i in range(count):
        digit = i // stride % size
        pairs.append((i, i + ((digit + step) % size - digit) * stride))
    return pairs


def split_rows(array, count):
    rows, cols = array.shape
    return array.reshape(*[size for _, size in stages(count)], rows // count, cols)


def reduce_stage(total, count, stage):
    stride, size = stages(count)[stage]
    digit = lax.axis_index("dp") // stride % size
    kept = lax.dynamic_index_in_dim(total, digit, 0, keepdims=False).astype(F32)
    for step in range(1, size):
        sent = lax.dynamic_index_in_dim(total, (digit + step) % size, 0, keepdims=False)
        got = lax.ppermute(sent, "dp", shift_pairs(count, stride, size, step))
        kept = kept + got.astype(F32)
    return kept.astype(BF16)


def gather_stage(part, count, stage):
    stride, size = stages(count)[stage]
    digit = lax.axis_index("dp") // stride % size
    spread = jnp.zeros((size,) + part.shape, BF16)
    spread = lax.dynamic_update_index_in_dim(spread, part, digit, 0)
    for step in range(1, size):
        got = lax.ppermute(part, "dp", shift_pairs(count, stride, size, step))
        spread = lax.dynamic_update_index_in_dim(spread, got, (digit - step) % size, 0)
    return spread


def sum_over_dp(array, count):
    total = split_rows(array, count)
    for stage in range(len(stages(count))):
        total = reduce_stage(total, count, stage)
    for stage in reversed(range(len(stages(count)))):
        total = gather_stage(total, count, stage)
    return total.reshape(array.shape).astype(F32)


def add(keep, got):
    return (keep.astype(F32) + got.astype(F32)).astype(BF16)


def segment_begin(segment):
    index = jnp.arange(segment.shape[0], dtype=jnp.int32)
    is_start = jnp.concatenate([jnp.ones((1,), dtype=bool), segment[1:] != segment[:-1]])
    return lax.cummax(jnp.where(is_start, index, jnp.zeros_like(index)), axis=0)


def rope_tables(position):
    frequency = ROPE_BASE ** (-(jnp.arange(ROT, dtype=F32) * 2.0 / HDIM))
    angles = frequency[:, None] * position.astype(F32)[None, :]
    return jnp.cos(angles), jnp.sin(angles)


def per_device(
    count,
    hidden_in,
    query_weight,
    key_weight,
    value_weight,
    output_weight,
    gate_weight,
    up_weight,
    down_weight,
    attn_gain,
    ffn_gain,
    out_grad,
    segment_ids,
):
    col, row = lax.axis_index("col"), lax.axis_index("row")
    first = col == 0

    def own_tokens(array):
        outer = jnp.concatenate([array[..., :BLOCK], array[..., 3 * BLOCK :]], axis=-1)
        inner = array[..., BLOCK : 3 * BLOCK]
        return jnp.where(first, outer, inner), jnp.where(first, inner, outer)

    def in_window(own, got):
        outer, inner = jnp.where(first, own, got), jnp.where(first, got, own)
        return jnp.concatenate([outer[:, :BLOCK], inner, outer[:, BLOCK:]], axis=1)

    w_near = jnp.concatenate(
        [query_weight[:, 0].T, key_weight[:, 0].T, value_weight[:, 0].T], axis=0
    )
    w_far = swap(w_near, "row")
    x_own, x_other = own_tokens(hidden_in.T)
    x_got = swap(x_other, "col")
    gains = jnp.stack([attn_gain, ffn_gain])
    gains_got = swap(gains, "col").astype(F32)
    gains = gains.astype(F32)
    gin_own, gmid_own = gains[0][:, None], gains[1][:, None]
    gin_got, gmid_got = gains_got[0][:, None], gains_got[1][:, None]
    segment = jnp.where(col == row, segment_ids, swap(segment_ids, "col"))
    begin, _ = own_tokens(segment_begin(segment))
    index, _ = own_tokens(jnp.arange(MAXLEN, dtype=jnp.int32))
    cosine, sine = rope_tables(index - begin)
    begin = begin[None]
    live_near = jnp.where(row == 0, LIVE[0], LIVE[1])
    where_near = jnp.stack([col, live_near]).astype(jnp.int32)
    where_far = jnp.stack([col, LIVE[0] + LIVE[1] - live_near]).astype(jnp.int32)

    w_near_got = swap(w_near, "col")
    heads = (shape((QUERY, LOCAL)), shape((2 * KEY, LOCAL)))
    nm_in, q_near, kv_near = run(
        project_near_kernel,
        (x_own, x_got, gin_own, gin_got, cosine, sine, w_near, w_near_got),
        (shape((D, LOCAL)),) + heads,
        2 * LOCAL * D * D,
    )
    kv_near_got = swap(kv_near, "col")
    wo_near = output_weight[0]
    wo_far = swap(wo_near, "row")
    wo_near_got = swap(wo_near, "col")
    att_near, lse_near = attend(where_near, begin, q_near, kv_near, kv_near_got)
    w_far_got = swap(w_far, "col")
    q_far, kv_far = run(
        project_far_kernel,
        (nm_in, cosine, sine, w_far, w_far_got),
        heads,
        2 * LOCAL * D * D,
    )
    kv_far_got = swap(kv_far, "col")
    att_far, lse_far = attend(where_far, begin, q_far, kv_far, kv_far_got)
    wo_far_got = swap(wo_far, "col")
    mid, nm = run(
        mid_kernel,
        (
            att_near, att_far, wo_near, wo_near_got, wo_far, wo_far_got, x_own, x_got,
            gmid_own, gmid_got,
        ),
        (shape((D, LOCAL), F32), shape((D, LOCAL))),
        2 * LOCAL * D * D,
    )

    og_own, og_other = own_tokens(out_grad.T)
    og = jnp.concatenate([og_own, swap(og_other, "col")], axis=0)
    og_far = swap(og, "row")
    mlp_weights = ()
    for weight in (gate_weight, up_weight, down_weight.T):
        mlp_weights += (weight, swap(weight, "col"))
    nm_far = swap(nm, "row")
    out_part, gnm_part, act, gg, gu = feed_forward(nm, og, mlp_weights, F32)
    out_send, gnm_send, act_far, gg_far, gu_far = feed_forward(nm_far, og_far, mlp_weights, BF16)
    gnm_back = swap(gnm_send, "row")
    down_keep, down_send = weight_grads(og, og_far, act, act_far)
    down_sum = add(down_keep, swap(down_send, "col"))
    gate_keep, gate_send = weight_grads(nm, nm_far, gg, gg_far)
    gate_sum = add(gate_keep, swap(gate_send, "col"))
    up_keep, up_send = weight_grads(nm, nm_far, gu, gu_far)
    up_sum = add(up_keep, swap(up_send, "col"))

    gmid, gb, gatt_near, gatt_far, ggain_mid = run(
        mid_back_kernel,
        (
            og, mid, gnm_part, gnm_back, gmid_own, gmid_got, wo_near, wo_near_got, wo_far,
            wo_far_got,
        ),
        (
            shape((D, LOCAL), F32), shape((D, LOCAL)), shape((QUERY, LOCAL)),
            shape((QUERY, LOCAL)), shape((D, 1), F32),
        ),
        2 * LOCAL * D * D,
    )

    wo_far_sum = add(
        dot(att_far, gb[:HALF], 1, 1), swap(dot(att_far, gb[HALF:], 1, 1).astype(BF16), "col")
    )
    wo_near_sum = add(
        dot(att_near, gb[:HALF], 1, 1), swap(dot(att_near, gb[HALF:], 1, 1).astype(BF16), "col")
    )
    wo_sum = add(wo_near_sum, swap(wo_far_sum, "row"))

    dq_far, own_far, other_far = attend_back(
        where_far, begin, q_far, kv_far, kv_far_got, gatt_far, lse_far
    )
    got_far = swap(other_far, "col")
    joined = shape((D, HALF))
    gnm_in_part, far_keep, far_send = run(
        joined_far_kernel,
        (dq_far, own_far, got_far, cosine, sine, w_far, w_far_got, nm_in),
        (shape((D, LOCAL), F32), joined, joined),
        4 * LOCAL * D * D,
        scratch=[pltpu.VMEM((D, LOCAL), BF16)],
    )
    dq_near, own_near, other_near = attend_back(
        where_near, begin, q_near, kv_near, kv_near_got, gatt_near, lse_near
    )
    got_near = swap(other_near, "col")
    near_keep, near_send, grad, ggain_in = run(
        joined_near_kernel,
        (
            dq_near, own_near, got_near, cosine, sine, w_near, w_near_got, nm_in, gnm_in_part,
            x_own, x_got, gin_own, gin_got, gmid,
        ),
        (joined, joined, shape((D, LOCAL)), shape((D, 1), F32)),
        4 * LOCAL * D * D,
        scratch=[pltpu.VMEM((D, LOCAL), BF16)],
    )
    ggain = jnp.concatenate([ggain_in, ggain_mid], axis=1).T.astype(BF16)
    ggain_sum = add(ggain[:, :HALF], swap(ggain[:, HALF:], "col"))
    far_sum = add(far_keep, swap(far_send, "col"))
    near_sum = add(near_keep, swap(near_send, "col"))
    near_sum = add(near_sum, swap(far_sum, "row"))
    ggain_sum = add(ggain_sum, swap(ggain_sum, "row"))
    last_sum = jnp.concatenate([near_sum, jnp.pad(ggain_sum, ((0, 62), (0, 0)))], axis=0)

    def feature_cols(array):
        return in_window(array[:HALF], swap(array[HALF:], "col")).T

    out_back = swap(out_send, "row")
    block_out = feature_cols((mid + out_part + out_back.astype(F32)).astype(BF16))
    input_grad = feature_cols(grad)

    def widened(array):
        total = sum_over_dp(array, count)
        return jnp.concatenate([total[:HALF], total[HALF:]], axis=1)

    down_grad = widened(down_sum).T
    gate_grad = widened(gate_sum)
    up_grad = widened(up_sum)
    out_weight_grad = sum_over_dp(wo_sum, count)
    last = sum_over_dp(last_sum, count)
    return (
        block_out,
        input_grad,
        last[:QUERY].T[:, None, :],
        last[QUERY : QUERY + KEY].T[:, None, :],
        last[QUERY + KEY : D].T[:, None, :],
        out_weight_grad[None],
        gate_grad,
        up_grad,
        down_grad,
        last[D],
        last[D + 1],
    )


def solution(mesh):
    return jax.shard_map(
        functools.partial(per_device, mesh.shape["dp"]),
        mesh=mesh,
        in_specs=(
            P(("dp", "row"), "col"),
            P("col", "row", None),
            P("col", "row", None),
            P("col", "row", None),
            P("row", None, "col"),
            P("col", "row"),
            P("col", "row"),
            P("row", "col"),
            P("col"),
            P("col"),
            P(("dp", "row"), "col"),
            P(("dp", "col")),
        ),
        out_specs=(
            P(("dp", "row"), "col"),
            P(("dp", "row"), "col"),
            P("col", "row", None),
            P("col", "row", None),
            P("col", "row", None),
            P("row", None, "col"),
            P("col", "row"),
            P("col", "row"),
            P("row", "col"),
            P("col"),
            P("col"),
        ),
        check_vma=False,
    )
```

```python
import functools
import math

import jax
import jax.numpy as jnp
from jax import lax
from jax.experimental import pallas as pl
from jax.experimental.pallas import tpu as pltpu
from jax.sharding import PartitionSpec as P

D = 960
HALF = D // 2
HDIM = 64
ROT = HDIM // 2
GROUP = 3
GROUPS = 3
QUERY = GROUPS * GROUP * HDIM
KEY = GROUPS * HDIM
MAXLEN = 1024
BLOCK = MAXLEN // 4
LOCAL = 2 * BLOCK
LIVE = (3, 2)

NORM_EPS = 1e-05
ROPE_BASE = 100000.0
MASKED_SCORE = -1e30
SCALE = 1.0 / math.sqrt(HDIM)
BF16 = jnp.bfloat16
F32 = jnp.float32
VMEM_BYTES = 56 * 1024 * 1024
COST = 0.03

HELD = ((0, 3), (1, 2))
LAID = ((0, 3, 1, 2), (0, 1, 2))
SPANS = ((1, 4), (2, 3))


def dot(left, right, left_dim=1, right_dim=0):
    return lax.dot_general(
        left, right, (((left_dim,), (right_dim,)), ((), ())), preferred_element_type=F32
    )


def shape(dims, dtype=BF16):
    return jax.ShapeDtypeStruct(dims, dtype)


def whole(dims):
    return pl.BlockSpec(dims, lambda *_: (0,) * len(dims))


SMEM_SPEC = pl.BlockSpec(memory_space=pltpu.SMEM)


def run(kernel, ins, outs, flops, grid=None, in_specs=None, out_specs=None, scratch=(), after=()):
    moved = sum(a.size * a.dtype.itemsize for a in ins)
    moved += sum(math.prod(o.shape) * jnp.dtype(o.dtype).itemsize for o in outs)
    if in_specs is None:
        in_specs = [whole(a.shape) for a in ins]
    if out_specs is None:
        out_specs = [whole(o.shape) for o in outs]
    count = len(ins)

    def body(*refs):
        kernel(*refs[:count], *refs[count + len(after) :])

    return pl.pallas_call(
        body,
        grid=grid if grid is not None else (1,),
        in_specs=list(in_specs) + [pl.BlockSpec(memory_space=pl.ANY)] * len(after),
        out_specs=tuple(out_specs),
        out_shape=tuple(outs),
        scratch_shapes=list(scratch),
        compiler_params=pltpu.CompilerParams(vmem_limit_bytes=VMEM_BYTES),
        cost_estimate=pl.CostEstimate(
            flops=int(flops * COST), bytes_accessed=int(moved * COST), transcendentals=0
        ),
    )(*ins, *after)


def level_of(own, got):
    total = jnp.sum(own * own, axis=0, keepdims=True) + jnp.sum(got * got, axis=0, keepdims=True)
    return lax.rsqrt(total / D + NORM_EPS)


def project_heads(nm, cos_ref, sin_ref, own_ref, got_ref, q_ref, kv_ref):
    cosine, sine = cos_ref[...], sin_ref[...]
    joined = dot(own_ref[...], nm[:HALF]) + dot(got_ref[...], nm[HALF:])
    for at in range(0, QUERY + KEY, HDIM):
        low, high = joined[at : at + ROT], joined[at + ROT : at + HDIM]
        parts = (low * cosine - high * sine, high * cosine + low * sine)
        for part, turned in enumerate(parts):
            turned = turned.astype(BF16)
            if at < QUERY:
                turned = (turned.astype(F32) * SCALE).astype(BF16)
                q_ref[at + part * ROT : at + (part + 1) * ROT, :] = turned
            else:
                row = at - QUERY + part * ROT
                kv_ref[row : row + ROT, :] = turned
    kv_ref[KEY:, :] = joined[QUERY + KEY :].astype(BF16)


def project_near_kernel(
    xo_ref, xg_ref, go_ref, gg_ref, cos_ref, sin_ref, own_ref, got_ref, nm_ref, q_ref, kv_ref
):
    own, got = xo_ref[...].astype(F32), xg_ref[...].astype(F32)
    level = level_of(own, got)
    nm_ref[:HALF, :] = (own * level * go_ref[...]).astype(BF16)
    nm_ref[HALF:, :] = (got * level * gg_ref[...]).astype(BF16)
    project_heads(nm_ref[...], cos_ref, sin_ref, own_ref, got_ref, q_ref, kv_ref)


def project_far_kernel(nm_ref, cos_ref, sin_ref, own_ref, got_ref, q_ref, kv_ref):
    project_heads(nm_ref[...], cos_ref, sin_ref, own_ref, got_ref, q_ref, kv_ref)


def laid(core, own, got, axis):
    if core == 0:
        return jnp.concatenate([own, got], axis=axis)
    return jnp.concatenate([lax.slice_in_dim(got, 0, BLOCK, axis=axis), own], axis=axis)


def fill_bias(core, bias_ref, begin_ref):
    for at, block in enumerate(LAID[core]):
        for slot in range(2):
            cols = slice(slot * BLOCK, (slot + 1) * BLOCK)
            key = block * BLOCK + lax.broadcasted_iota(jnp.int32, (BLOCK, BLOCK), 0)
            query = HELD[core][slot] * BLOCK + lax.broadcasted_iota(jnp.int32, (BLOCK, BLOCK), 1)
            allowed = (key >= begin_ref[:, cols]) & (key <= query)
            bias_ref[at * BLOCK : (at + 1) * BLOCK, cols] = jnp.where(allowed, 0.0, MASKED_SCORE)


def attend_kernel(
    where_ref, begin_ref, q_ref, ko_ref, vo_ref, kg_ref, vg_ref, att_ref, lse_ref, bias_ref
):
    group = pl.program_id(0)
    live = group < where_ref[1]

    @pl.when(jnp.logical_not(live))
    def _():
        att_ref[...] = jnp.zeros_like(att_ref)
        lse_ref[...] = jnp.zeros_like(lse_ref)

    for core in range(2):

        @pl.when(live & (where_ref[0] == core))
        def _():
            @pl.when(group == 0)
            def _():
                fill_bias(core, bias_ref, begin_ref)

            keys = laid(core, ko_ref[...], kg_ref[...], 1).T
            values = laid(core, vo_ref[...], vg_ref[...], 1)
            for slot in range(2):
                cols = slice(slot * BLOCK, (slot + 1) * BLOCK)
                span = SPANS[core][slot] * BLOCK
                for j in range(GROUP):
                    heads = slice(j * HDIM, (j + 1) * HDIM)
                    scores = dot(keys[:span], q_ref[heads, cols]) + bias_ref[:span, cols]
                    highest = jnp.max(scores, axis=0, keepdims=True)
                    weights = jnp.exp(scores - highest)
                    total = jnp.sum(weights, axis=0, keepdims=True)
                    mixed = dot(values[:, :span], weights.astype(BF16)) / total
                    att_ref[heads, cols] = mixed.astype(BF16)
                    lse_ref[0, j : j + 1, cols] = highest + jnp.log(total)


def mid_kernel(
    near_ref, far_ref, no_ref, ng_ref, fo_ref, fg_ref, xo_ref, xg_ref, go_ref, gg_ref,
    mid_ref, nm_ref,
):
    near, far = near_ref[...], far_ref[...]
    own = xo_ref[...].astype(F32) + dot(no_ref[...], near, 0, 0) + dot(fo_ref[...], far, 0, 0)
    got = xg_ref[...].astype(F32) + dot(ng_ref[...], near, 0, 0) + dot(fg_ref[...], far, 0, 0)
    mid_ref[:HALF, :] = own
    mid_ref[HALF:, :] = got
    level = level_of(own, got)
    nm_ref[:HALF, :] = (own * level * go_ref[...]).astype(BF16)
    nm_ref[HALF:, :] = (got * level * gg_ref[...]).astype(BF16)


def mlp_kernel(
    nm_ref, og_ref, wgo_ref, wgg_ref, wuo_ref, wug_ref, wdo_ref, wdg_ref,
    out_ref, gnm_ref, act_ref, gg_ref, gu_ref, out_sum, gnm_sum,
):
    step = pl.program_id(0)

    def inward(own_ref, got_ref, rows_ref):
        return dot(own_ref[...], rows_ref[:HALF, :], 0, 0) + dot(
            got_ref[...], rows_ref[HALF:, :], 0, 0
        )

    @pl.when(step == 0)
    def _():
        out_sum[...] = jnp.zeros_like(out_sum)
        gnm_sum[...] = jnp.zeros_like(gnm_sum)

    gate = inward(wgo_ref, wgg_ref, nm_ref)
    up = inward(wuo_ref, wug_ref, nm_ref)
    grad_act = inward(wdo_ref, wdg_ref, og_ref)
    sig = jax.nn.sigmoid(gate)
    silu = gate * sig
    act = (silu * up).astype(BF16)
    grad_gate = (grad_act * up * sig * (1.0 + gate * (1.0 - sig))).astype(BF16)
    grad_up = (grad_act * silu).astype(BF16)
    act_ref[...] = act
    gg_ref[...] = grad_gate
    gu_ref[...] = grad_up
    gnm_sum[:HALF, :] += dot(wgo_ref[...], grad_gate) + dot(wuo_ref[...], grad_up)
    gnm_sum[HALF:, :] += dot(wgg_ref[...], grad_gate) + dot(wug_ref[...], grad_up)
    out_sum[:HALF, :] += dot(wdo_ref[...], act)
    out_sum[HALF:, :] += dot(wdg_ref[...], act)

    @pl.when(step == pl.num_programs(0) - 1)
    def _():
        out_ref[...] = out_sum[...].astype(out_ref.dtype)
        gnm_ref[...] = gnm_sum[...].astype(gnm_ref.dtype)


def grads_kernel(rows_ref, rows_far_ref, cols_ref, cols_far_ref, keep_ref, send_ref):
    for half, out_ref in enumerate((keep_ref, send_ref)):
        rows = slice(half * HALF, (half + 1) * HALF)
        product = dot(rows_ref[rows, :], cols_ref[...], 1, 1)
        product += dot(rows_far_ref[rows, :], cols_far_ref[...], 1, 1)
        out_ref[...] = product.astype(BF16)


def mid_back_kernel(
    og_ref, mid_ref, part_ref, back_ref, go_ref, gg_ref, no_ref, ng_ref, fo_ref, fg_ref,
    gmid_ref, gb_ref, near_ref, far_ref, ggain_ref,
):
    own, got = mid_ref[:HALF, :], mid_ref[HALF:, :]
    level = level_of(own, got)
    gnm = part_ref[...] + back_ref[...].astype(F32)
    scaled_own, scaled_got = gnm[:HALF] * go_ref[...], gnm[HALF:] * gg_ref[...]
    inner = jnp.sum(scaled_own * own, axis=0, keepdims=True)
    inner += jnp.sum(scaled_got * got, axis=0, keepdims=True)
    pull = level**3 * inner / D
    for rows, mid, scaled in (
        (slice(0, HALF), own, scaled_own), (slice(HALF, D), got, scaled_got)
    ):
        ggain_ref[rows, :] = jnp.sum(gnm[rows] * mid * level, axis=1, keepdims=True)
        gmid = og_ref[rows, :].astype(F32) + scaled * level - mid * pull
        gmid_ref[rows, :] = gmid
        gb_ref[rows, :] = gmid.astype(BF16)
    gb_own, gb_got = gb_ref[:HALF, :], gb_ref[HALF:, :]
    near_ref[...] = (dot(no_ref[...], gb_own) + dot(ng_ref[...], gb_got)).astype(BF16)
    far_ref[...] = (dot(fo_ref[...], gb_own) + dot(fg_ref[...], gb_got)).astype(BF16)


def attend_back_kernel(
    where_ref, begin_ref, q_ref, ko_ref, vo_ref, kg_ref, vg_ref, gatt_ref, lse_ref,
    dq_ref, own_ref, got_ref, bias_ref, dk_ref, dv_ref,
):
    group = pl.program_id(0)
    live = group < where_ref[1]

    @pl.when(jnp.logical_not(live))
    def _():
        dq_ref[...] = jnp.zeros_like(dq_ref)
        own_ref[...] = jnp.zeros_like(own_ref)
        got_ref[...] = jnp.zeros_like(got_ref)

    for core in range(2):

        @pl.when(live & (where_ref[0] == core))
        def _():
            @pl.when(group == 0)
            def _():
                fill_bias(core, bias_ref, begin_ref)

            keys_t = laid(core, ko_ref[...], kg_ref[...], 1)
            keys = keys_t.T
            values = laid(core, vo_ref[...], vg_ref[...], 1).T
            dk_ref[...] = jnp.zeros_like(dk_ref)
            dv_ref[...] = jnp.zeros_like(dv_ref)
            for slot in range(2):
                cols = slice(slot * BLOCK, (slot + 1) * BLOCK)
                span = SPANS[core][slot] * BLOCK
                for j in range(GROUP):
                    heads = slice(j * HDIM, (j + 1) * HDIM)
                    queries, grads = q_ref[heads, cols], gatt_ref[heads, cols]
                    scores = dot(keys[:span], queries) + bias_ref[:span, cols]
                    probs = jnp.exp(scores - lse_ref[0, j : j + 1, cols])
                    dprobs = dot(values[:span], grads)
                    inner = jnp.sum(probs * dprobs, axis=0, keepdims=True)
                    dscores = (probs * (dprobs - inner)).astype(BF16)
                    dv_ref[:span, :] += dot(probs.astype(BF16), grads.T)
                    dk_ref[:span, :] += dot(dscores, queries.T)
                    dq_ref[heads, cols] = dot(keys_t[:, :span], dscores) * SCALE
            for kind, grad_ref in enumerate((dk_ref, dv_ref)):
                if core == 0:
                    own_ref[kind, 0] = grad_ref[:LOCAL, :].T
                    got_ref[kind, 0] = grad_ref[LOCAL:, :].T.astype(BF16)
                else:
                    own_ref[kind, 0] = grad_ref[BLOCK : BLOCK + LOCAL, :].T
                    got_ref[kind, 0, :, :BLOCK] = grad_ref[:BLOCK, :].T.astype(BF16)
                    got_ref[kind, 0, :, BLOCK:] = jnp.zeros((HDIM, BLOCK), BF16)


def turn_back(cos_ref, sin_ref, dq_ref, own_ref, got_ref, gj_ref):
    cosine, sine = cos_ref[...], sin_ref[...]

    def back(at, grad):
        low, high = grad[:ROT], grad[ROT:]
        gj_ref[at : at + ROT, :] = (low * cosine + high * sine).astype(BF16)
        gj_ref[at + ROT : at + HDIM, :] = (high * cosine - low * sine).astype(BF16)

    for at in range(0, QUERY, HDIM):
        back(at, dq_ref[at : at + HDIM, :])
    for g in range(GROUPS):
        back(QUERY + g * HDIM, own_ref[0, g] + got_ref[0, g].astype(F32))
        at = QUERY + KEY + g * HDIM
        gj_ref[at : at + HDIM, :] = (own_ref[1, g] + got_ref[1, g].astype(F32)).astype(BF16)


def joined_far_kernel(
    dq_ref, own_ref, got_ref, cos_ref, sin_ref, wo_ref, wg_ref, nm_ref,
    gnm_ref, keep_ref, send_ref, gj_ref,
):
    turn_back(cos_ref, sin_ref, dq_ref, own_ref, got_ref, gj_ref)
    gj = gj_ref[...]
    send_ref[...] = dot(gj, nm_ref[HALF:, :], 1, 1).astype(BF16)
    keep_ref[...] = dot(gj, nm_ref[:HALF, :], 1, 1).astype(BF16)
    gnm_ref[:HALF, :] = dot(wo_ref[...], gj, 0, 0)
    gnm_ref[HALF:, :] = dot(wg_ref[...], gj, 0, 0)


def joined_near_kernel(
    dq_ref, own_ref, got_ref, cos_ref, sin_ref, wo_ref, wg_ref, nm_ref, part_ref, xo_ref, xg_ref,
    go_ref, gg_ref, gmid_ref, keep_ref, send_ref, grad_ref, ggain_ref, gj_ref,
):
    turn_back(cos_ref, sin_ref, dq_ref, own_ref, got_ref, gj_ref)
    gj = gj_ref[...]
    send_ref[...] = dot(gj, nm_ref[HALF:, :], 1, 1).astype(BF16)
    keep_ref[...] = dot(gj, nm_ref[:HALF, :], 1, 1).astype(BF16)
    gnm_own = part_ref[:HALF, :] + dot(wo_ref[...], gj, 0, 0)
    gnm_got = part_ref[HALF:, :] + dot(wg_ref[...], gj, 0, 0)
    own, got = xo_ref[...].astype(F32), xg_ref[...].astype(F32)
    level = level_of(own, got)
    scaled_own, scaled_got = gnm_own * go_ref[...], gnm_got * gg_ref[...]
    inner = jnp.sum(scaled_own * own, axis=0, keepdims=True)
    inner += jnp.sum(scaled_got * got, axis=0, keepdims=True)
    pull = level**3 * inner / D
    for rows, x, gnm, scaled in (
        (slice(0, HALF), own, gnm_own, scaled_own), (slice(HALF, D), got, gnm_got, scaled_got)
    ):
        ggain_ref[rows, :] = jnp.sum(gnm * x * level, axis=1, keepdims=True)
        grad_ref[rows, :] = (gmid_ref[rows, :] + scaled * level - x * pull).astype(BF16)


def per_group(rows, at=0):
    return pl.BlockSpec((rows, LOCAL), lambda g: (g + at, 0))


LSE_SPEC = pl.BlockSpec((1, 8, LOCAL), lambda g: (g, 0, 0))
KV_SPECS = [per_group(HDIM), per_group(HDIM, GROUPS)] * 2
PAIR_SPEC = pl.BlockSpec((2, 1, HDIM, LOCAL), lambda g: (0, g, 0, 0))


def attend(where, begin, q, kv, kv_got, after=()):
    return run(
        attend_kernel,
        (where, begin, q, kv, kv, kv_got, kv_got),
        (shape((QUERY, LOCAL)), shape((GROUPS, 8, LOCAL), F32)),
        6e9,
        grid=(GROUPS,),
        in_specs=[SMEM_SPEC, whole((1, LOCAL)), per_group(GROUP * HDIM)] + KV_SPECS,
        out_specs=(per_group(GROUP * HDIM), LSE_SPEC),
        scratch=[pltpu.VMEM((MAXLEN, LOCAL), F32)],
        after=after,
    )


def attend_back(where, begin, q, kv, kv_got, gatt, lse, after=()):
    return run(
        attend_back_kernel,
        (where, begin, q, kv, kv, kv_got, kv_got, gatt, lse),
        (
            shape((QUERY, LOCAL), F32), shape((2, GROUPS, HDIM, LOCAL), F32),
            shape((2, GROUPS, HDIM, LOCAL)),
        ),
        14e9,
        grid=(GROUPS,),
        in_specs=[SMEM_SPEC, whole((1, LOCAL)), per_group(GROUP * HDIM)]
        + KV_SPECS
        + [per_group(GROUP * HDIM), LSE_SPEC],
        out_specs=(per_group(GROUP * HDIM), PAIR_SPEC, PAIR_SPEC),
        scratch=[
            pltpu.VMEM((MAXLEN, LOCAL), F32), pltpu.VMEM((MAXLEN, HDIM), F32),
            pltpu.VMEM((MAXLEN, HDIM), F32),
        ],
        after=after,
    )


def feed_forward(nm, og, weights, dtype, after=()):
    hidden = weights[0].shape[1]
    chunk = 256
    cols = pl.BlockSpec((HALF, chunk), lambda i: (0, i))
    rows = pl.BlockSpec((chunk, LOCAL), lambda i: (i, 0))
    act = shape((hidden, LOCAL))
    return run(
        mlp_kernel,
        (nm, og) + weights,
        (shape((D, LOCAL), dtype), shape((D, LOCAL), dtype), act, act, act),
        12 * LOCAL * D * hidden,
        grid=(hidden // chunk,),
        in_specs=[whole((D, LOCAL))] * 2 + [cols] * 6,
        out_specs=(whole((D, LOCAL)), whole((D, LOCAL)), rows, rows, rows),
        scratch=[pltpu.VMEM((D, LOCAL), F32)] * 2,
        after=after,
    )


def weight_grads(rows, rows_far, cols, cols_far, after=()):
    hidden = cols.shape[0]
    part = hidden // 2
    taken = pl.BlockSpec((part, LOCAL), lambda i: (i, 0))
    given = pl.BlockSpec((HALF, part), lambda i: (i, 0))
    return run(
        grads_kernel,
        (rows, rows_far, cols, cols_far),
        (shape((2 * HALF, part)),) * 2,
        4 * LOCAL * D * hidden,
        grid=(2,),
        in_specs=[whole((D, LOCAL))] * 2 + [taken] * 2,
        out_specs=(given, given),
        after=after,
    )


def swap(array, axis):
    return lax.ppermute(array, axis, [(0, 1), (1, 0)])


def stages(count):
    found, stride = [], 1
    for size in (2,) + (4,) * 16:
        size = min(size, count // stride)
        if size < 2:
            break
        found.append((stride, size))
        stride *= size
    return found


def shift_pairs(count, stride, size, step):
    pairs = []
    for i in range(count):
        digit = i // stride % size
        pairs.append((i, i + ((digit + step) % size - digit) * stride))
    return pairs


def split_rows(array, count):
    rows, cols = array.shape
    return array.reshape(*[size for _, size in stages(count)], rows // count, cols)


def reduce_stage(total, count, stage, held=()):
    stride, size = stages(count)[stage]
    digit = lax.axis_index("dp") // stride % size
    kept = lax.dynamic_index_in_dim(total, digit, 0, keepdims=False).astype(F32)
    found = []
    for step in range(1, size):
        sent = lax.dynamic_index_in_dim(total, (digit + step) % size, 0, keepdims=False)
        found.append(lax.ppermute(sent, "dp", shift_pairs(count, stride, size, step)))
    for got in hold_all(found, held):
        kept = kept + got.astype(F32)
    return kept.astype(BF16)


def gather_stage(part, count, stage, held=()):
    stride, size = stages(count)[stage]
    digit = lax.axis_index("dp") // stride % size
    found = [
        lax.ppermute(part, "dp", shift_pairs(count, stride, size, step)) for step in range(1, size)
    ]
    spread = jnp.zeros((size,) + part.shape, BF16)
    spread = lax.dynamic_update_index_in_dim(spread, part, digit, 0)
    for step, got in enumerate(hold_all(found, held), 1):
        spread = lax.dynamic_update_index_in_dim(spread, got, (digit - step) % size, 0)
    return spread


def reduce_first(array, count, held=()):
    return reduce_stage(split_rows(array, count), count, 0, held)


def reduce_rest(total, count, held=()):
    for stage in range(1, len(stages(count))):
        total = reduce_stage(total, count, stage, held)
    return total


def gather_rest(total, count, held=()):
    for stage in reversed(range(1, len(stages(count)))):
        total = gather_stage(total, count, stage, held)
    return total


def gather_first(total, count, dims, held=()):
    return gather_stage(total, count, 0, held).reshape(dims).astype(F32)


def hold_all(arrays, others):
    if not others:
        return arrays
    return lax.optimization_barrier(tuple(arrays) + tuple(others))[: len(arrays)]


def hold(array, *others):
    return lax.optimization_barrier((array,) + others)[0]


def add(keep, got):
    return (keep.astype(F32) + got.astype(F32)).astype(BF16)


def segment_begin(segment):
    index = jnp.arange(segment.shape[0], dtype=jnp.int32)
    is_start = jnp.concatenate([jnp.ones((1,), dtype=bool), segment[1:] != segment[:-1]])
    return lax.cummax(jnp.where(is_start, index, jnp.zeros_like(index)), axis=0)


def rope_tables(position):
    frequency = ROPE_BASE ** (-(jnp.arange(ROT, dtype=F32) * 2.0 / HDIM))
    angles = frequency[:, None] * position.astype(F32)[None, :]
    return jnp.cos(angles), jnp.sin(angles)


def per_device(
    count,
    hidden_in,
    query_weight,
    key_weight,
    value_weight,
    output_weight,
    gate_weight,
    up_weight,
    down_weight,
    attn_gain,
    ffn_gain,
    out_grad,
    segment_ids,
):
    col, row = lax.axis_index("col"), lax.axis_index("row")
    first = col == 0

    def own_tokens(array):
        outer = jnp.concatenate([array[..., :BLOCK], array[..., 3 * BLOCK :]], axis=-1)
        inner = array[..., BLOCK : 3 * BLOCK]
        return jnp.where(first, outer, inner), jnp.where(first, inner, outer)

    def in_window(own, got):
        outer, inner = jnp.where(first, own, got), jnp.where(first, got, own)
        return jnp.concatenate([outer[:, :BLOCK], inner, outer[:, BLOCK:]], axis=1)

    w_near = jnp.concatenate(
        [query_weight[:, 0].T, key_weight[:, 0].T, value_weight[:, 0].T], axis=0
    )
    w_far = swap(w_near, "row")
    x_own, x_other = own_tokens(hidden_in.T)
    x_got = swap(x_other, "col")
    gains = jnp.stack([attn_gain, ffn_gain])
    gains_got = swap(gains, "col").astype(F32)
    gains = gains.astype(F32)
    gin_own, gmid_own = gains[0][:, None], gains[1][:, None]
    gin_got, gmid_got = gains_got[0][:, None], gains_got[1][:, None]
    segment = jnp.where(col == row, segment_ids, swap(segment_ids, "col"))
    begin, _ = own_tokens(segment_begin(segment))
    index, _ = own_tokens(jnp.arange(MAXLEN, dtype=jnp.int32))
    cosine, sine = rope_tables(index - begin)
    begin = begin[None]
    live_near = jnp.where(row == 0, LIVE[0], LIVE[1])
    where_near = jnp.stack([col, live_near]).astype(jnp.int32)
    where_far = jnp.stack([col, LIVE[0] + LIVE[1] - live_near]).astype(jnp.int32)

    w_near_got = swap(w_near, "col")
    heads = (shape((QUERY, LOCAL)), shape((2 * KEY, LOCAL)))
    nm_in, q_near, kv_near = run(
        project_near_kernel,
        (x_own, x_got, gin_own, gin_got, cosine, sine, w_near, w_near_got),
        (shape((D, LOCAL)),) + heads,
        2 * LOCAL * D * D,
    )
    kv_near_got = swap(kv_near, "col")
    wo_near = output_weight[0]
    wo_far = swap(wo_near, "row")
    wo_near_got = swap(wo_near, "col")
    att_near, lse_near = attend(where_near, begin, q_near, kv_near, kv_near_got)
    w_far_got = swap(w_far, "col")
    q_far, kv_far = run(
        project_far_kernel,
        (nm_in, cosine, sine, w_far, w_far_got),
        heads,
        2 * LOCAL * D * D,
    )
    kv_far_got = swap(kv_far, "col")
    att_far, lse_far = attend(where_far, begin, q_far, kv_far, kv_far_got, after=(wo_far,))
    wo_far_got = swap(wo_far, "col")
    og_own, og_other = own_tokens(out_grad.T)
    og = jnp.concatenate([og_own, swap(og_other, "col")], axis=0)
    og_far = swap(og, "row")
    mid, nm = run(
        mid_kernel,
        (
            att_near, att_far, wo_near, wo_near_got, wo_far, wo_far_got, x_own, x_got,
            gmid_own, gmid_got,
        ),
        (shape((D, LOCAL), F32), shape((D, LOCAL))),
        2 * LOCAL * D * D,
        after=(og_far,),
    )

    mlp_weights = ()
    for weight in (gate_weight, up_weight, down_weight.T):
        mlp_weights += (weight, swap(weight, "col"))
    nm_far = swap(nm, "row")
    out_part, gnm_part, act, gg, gu = feed_forward(nm, og, mlp_weights, F32)
    out_send, gnm_send, act_far, gg_far, gu_far = feed_forward(
        nm_far, og_far, mlp_weights, BF16, after=(act,)
    )
    gnm_back = swap(gnm_send, "row")
    down_keep, down_send = weight_grads(og, og_far, act, act_far)
    gate_keep, gate_send = weight_grads(nm, nm_far, gg, gg_far, after=(down_keep,))
    down_sum = add(down_keep, hold(swap(down_send, "col"), gate_keep))
    up_keep, up_send = weight_grads(nm, nm_far, gu, gu_far, after=(down_sum,))
    gate_sum = add(gate_keep, hold(swap(gate_send, "col"), up_keep))

    gmid, gb, gatt_near, gatt_far, ggain_mid = run(
        mid_back_kernel,
        (
            og, mid, gnm_part, gnm_back, gmid_own, gmid_got, wo_near, wo_near_got, wo_far,
            wo_far_got,
        ),
        (
            shape((D, LOCAL), F32), shape((D, LOCAL)), shape((QUERY, LOCAL)),
            shape((QUERY, LOCAL)), shape((D, 1), F32),
        ),
        2 * LOCAL * D * D,
        after=(gate_sum,),
    )
    up_sum = add(up_keep, hold(swap(up_send, "col"), ggain_mid))
    down_x = reduce_first(down_sum, count, (ggain_mid,))

    dq_far, own_far, other_far = attend_back(
        where_far, begin, q_far, kv_far, kv_far_got, gatt_far, lse_far, after=(down_x, up_sum)
    )
    gate_x = reduce_first(gate_sum, count, (dq_far,))
    down_z = reduce_rest(down_x, count, (dq_far,))

    def out_grads(att):
        send = dot(att, gb[HALF:], 1, 1).astype(BF16)
        return add(dot(att, gb[:HALF], 1, 1), hold(swap(send, "col"), dq_far))

    wo_far_sum = out_grads(att_far)
    wo_near_sum = out_grads(att_near)
    got_far = swap(other_far, "col")
    joined = shape((D, HALF))
    gnm_in_part, far_keep, far_send = run(
        joined_far_kernel,
        (dq_far, own_far, got_far, cosine, sine, w_far, w_far_got, nm_in),
        (shape((D, LOCAL), F32), joined, joined),
        4 * LOCAL * D * D,
        after=(gate_x, down_z, wo_far_sum, wo_near_sum),
        scratch=[pltpu.VMEM((D, LOCAL), BF16)],
    )
    dq_near, own_near, other_near = attend_back(
        where_near, begin, q_near, kv_near, kv_near_got, gatt_near, lse_near, after=(far_keep,)
    )
    far_sum = add(far_keep, hold(swap(far_send, "col"), dq_near))
    wo_sum = add(wo_near_sum, hold(swap(wo_far_sum, "row"), dq_near))
    up_x = reduce_first(up_sum, count, (dq_near,))
    gate_z = reduce_rest(gate_x, count, (dq_near,))
    down_y = gather_rest(down_z, count, (dq_near,))
    got_near = swap(other_near, "col")
    near_keep, near_send, grad, ggain_in = run(
        joined_near_kernel,
        (
            dq_near, own_near, got_near, cosine, sine, w_near, w_near_got, nm_in, gnm_in_part,
            x_own, x_got, gin_own, gin_got, gmid,
        ),
        (joined, joined, shape((D, LOCAL)), shape((D, 1), F32)),
        4 * LOCAL * D * D,
        after=(up_x, gate_z, down_y, wo_sum, far_sum),
        scratch=[pltpu.VMEM((D, LOCAL), BF16)],
    )
    ggain = jnp.concatenate([ggain_in, ggain_mid], axis=1).T.astype(BF16)
    ggain_sum = add(ggain[:, :HALF], swap(ggain[:, HALF:], "col"))
    near_sum = add(near_keep, swap(near_send, "col"))
    near_sum = add(near_sum, swap(far_sum, "row"))
    ggain_sum = add(ggain_sum, swap(ggain_sum, "row"))
    last_sum = jnp.concatenate([near_sum, jnp.pad(ggain_sum, ((0, 62), (0, 0)))], axis=0)

    def feature_cols(array):
        return in_window(array[:HALF], swap(array[HALF:], "col")).T

    out_back = swap(hold(out_send, gnm_back), "row")
    block_out = feature_cols((mid + out_part + out_back.astype(F32)).astype(BF16))
    input_grad = feature_cols(grad)

    def widened(part):
        total = gather_first(part, count, (D, down_sum.shape[1]), (ggain_in,))
        return jnp.concatenate([total[:HALF], total[HALF:]], axis=1)

    down_grad = widened(down_y).T
    up_z = reduce_rest(up_x, count, (ggain_in,))
    gate_grad = widened(gather_rest(gate_z, count, (ggain_in,)))
    up_grad = widened(gather_rest(up_z, count, (last_sum,)))
    out_z = reduce_rest(
        reduce_first(wo_sum, count, (ggain_in,)), count, (last_sum,)
    )
    out_weight_grad = gather_first(gather_rest(out_z, count), count, wo_sum.shape)
    last_z = reduce_rest(reduce_first(last_sum, count), count)
    last = gather_first(gather_rest(last_z, count), count, last_sum.shape)
    return (
        block_out,
        input_grad,
        last[:QUERY].T[:, None, :],
        last[QUERY : QUERY + KEY].T[:, None, :],
        last[QUERY + KEY : D].T[:, None, :],
        out_weight_grad[None],
        gate_grad,
        up_grad,
        down_grad,
        last[D],
        last[D + 1],
    )


def solution(mesh):
    return jax.shard_map(
        functools.partial(per_device, mesh.shape["dp"]),
        mesh=mesh,
        in_specs=(
            P(("dp", "row"), "col"),
            P("col", "row", None),
            P("col", "row", None),
            P("col", "row", None),
            P("row", None, "col"),
            P("col", "row"),
            P("col", "row"),
            P("row", "col"),
            P("col"),
            P("col"),
            P(("dp", "row"), "col"),
            P(("dp", "col")),
        ),
        out_specs=(
            P(("dp", "row"), "col"),
            P(("dp", "row"), "col"),
            P("col", "row", None),
            P("col", "row", None),
            P("col", "row", None),
            P("row", None, "col"),
            P("col", "row"),
            P("col", "row"),
            P("row", "col"),
            P("col"),
            P("col"),
        ),
        check_vma=False,
    )
```

```python
import functools
import math

import jax
import jax.numpy as jnp
from jax import lax
from jax.experimental import pallas as pl
from jax.experimental.pallas import tpu as pltpu
from jax.sharding import PartitionSpec as P

D = 960
HALF = D // 2
HDIM = 64
ROT = HDIM // 2
GROUP = 3
GROUPS = 3
QUERY = GROUPS * GROUP * HDIM
KEY = GROUPS * HDIM
MAXLEN = 1024
BLOCK = MAXLEN // 4
LOCAL = 2 * BLOCK
LIVE = (3, 2)
ROWS = 1024

NORM_EPS = 1e-05
ROPE_BASE = 100000.0
MASKED_SCORE = -1e30
SCALE = 1.0 / math.sqrt(HDIM)
BF16 = jnp.bfloat16
F32 = jnp.float32
VMEM_BYTES = 56 * 1024 * 1024
COST = 0.03

HELD = ((0, 3), (1, 2))
LAID = ((0, 3, 1, 2), (0, 1, 2))
SPANS = ((1, 4), (2, 3))


def dot(left, right, left_dim=1, right_dim=0):
    return lax.dot_general(
        left, right, (((left_dim,), (right_dim,)), ((), ())), preferred_element_type=F32
    )


def shape(dims, dtype=BF16):
    return jax.ShapeDtypeStruct(dims, dtype)


def whole(dims):
    return pl.BlockSpec(dims, lambda *_: (0,) * len(dims))


SMEM_SPEC = pl.BlockSpec(memory_space=pltpu.SMEM)


def run(kernel, ins, outs, flops, grid=None, in_specs=None, out_specs=None, scratch=(), after=()):
    moved = sum(a.size * a.dtype.itemsize for a in ins)
    moved += sum(math.prod(o.shape) * jnp.dtype(o.dtype).itemsize for o in outs)
    if in_specs is None:
        in_specs = [whole(a.shape) for a in ins]
    if out_specs is None:
        out_specs = [whole(o.shape) for o in outs]
    count = len(ins)

    def body(*refs):
        kernel(*refs[:count], *refs[count + len(after) :])

    return pl.pallas_call(
        body,
        grid=grid if grid is not None else (1,),
        in_specs=list(in_specs) + [pl.BlockSpec(memory_space=pl.ANY)] * len(after),
        out_specs=tuple(out_specs),
        out_shape=tuple(outs),
        scratch_shapes=list(scratch),
        compiler_params=pltpu.CompilerParams(vmem_limit_bytes=VMEM_BYTES),
        cost_estimate=pl.CostEstimate(
            flops=int(flops * COST), bytes_accessed=int(moved * COST), transcendentals=0
        ),
    )(*ins, *after)


def level_of(own, got):
    total = jnp.sum(own * own, axis=0, keepdims=True) + jnp.sum(got * got, axis=0, keepdims=True)
    return lax.rsqrt(total / D + NORM_EPS)


def project_heads(nm, cos_ref, sin_ref, own_ref, got_ref, q_ref, kv_ref):
    cosine, sine = cos_ref[...], sin_ref[...]
    joined = dot(own_ref[...], nm[:HALF]) + dot(got_ref[...], nm[HALF:])
    for at in range(0, QUERY + KEY, HDIM):
        low, high = joined[at : at + ROT], joined[at + ROT : at + HDIM]
        parts = (low * cosine - high * sine, high * cosine + low * sine)
        for part, turned in enumerate(parts):
            turned = turned.astype(BF16)
            if at < QUERY:
                turned = (turned.astype(F32) * SCALE).astype(BF16)
                q_ref[at + part * ROT : at + (part + 1) * ROT, :] = turned
            else:
                row = at - QUERY + part * ROT
                kv_ref[row : row + ROT, :] = turned
    kv_ref[KEY:, :] = joined[QUERY + KEY :].astype(BF16)


def project_near_kernel(
    xo_ref, xg_ref, go_ref, gg_ref, cos_ref, sin_ref, own_ref, got_ref, nm_ref, q_ref, kv_ref
):
    own, got = xo_ref[...].astype(F32), xg_ref[...].astype(F32)
    level = level_of(own, got)
    nm_ref[:HALF, :] = (own * level * go_ref[...]).astype(BF16)
    nm_ref[HALF:, :] = (got * level * gg_ref[...]).astype(BF16)
    project_heads(nm_ref[...], cos_ref, sin_ref, own_ref, got_ref, q_ref, kv_ref)


def project_far_kernel(nm_ref, cos_ref, sin_ref, own_ref, got_ref, q_ref, kv_ref):
    project_heads(nm_ref[...], cos_ref, sin_ref, own_ref, got_ref, q_ref, kv_ref)


def laid(core, own, got, axis):
    if core == 0:
        return jnp.concatenate([own, got], axis=axis)
    return jnp.concatenate([lax.slice_in_dim(got, 0, BLOCK, axis=axis), own], axis=axis)


def fill_bias(core, bias_ref, begin_ref):
    for at, block in enumerate(LAID[core]):
        for slot in range(2):
            cols = slice(slot * BLOCK, (slot + 1) * BLOCK)
            key = block * BLOCK + lax.broadcasted_iota(jnp.int32, (BLOCK, BLOCK), 0)
            query = HELD[core][slot] * BLOCK + lax.broadcasted_iota(jnp.int32, (BLOCK, BLOCK), 1)
            allowed = (key >= begin_ref[:, cols]) & (key <= query)
            bias_ref[at * BLOCK : (at + 1) * BLOCK, cols] = jnp.where(allowed, 0.0, MASKED_SCORE)


def attend_kernel(
    where_ref, begin_ref, q_ref, ko_ref, vo_ref, kg_ref, vg_ref, att_ref, lse_ref, bias_ref
):
    group = pl.program_id(0)
    live = group < where_ref[1]

    @pl.when(jnp.logical_not(live))
    def _():
        att_ref[...] = jnp.zeros_like(att_ref)
        lse_ref[...] = jnp.zeros_like(lse_ref)

    for core in range(2):

        @pl.when(live & (where_ref[0] == core))
        def _():
            @pl.when(group == 0)
            def _():
                fill_bias(core, bias_ref, begin_ref)

            keys = laid(core, ko_ref[...], kg_ref[...], 1).T
            values = laid(core, vo_ref[...], vg_ref[...], 1)
            for slot in range(2):
                cols = slice(slot * BLOCK, (slot + 1) * BLOCK)
                span = SPANS[core][slot] * BLOCK
                for j in range(GROUP):
                    heads = slice(j * HDIM, (j + 1) * HDIM)
                    scores = dot(keys[:span], q_ref[heads, cols]) + bias_ref[:span, cols]
                    highest = jnp.max(scores, axis=0, keepdims=True)
                    weights = jnp.exp(scores - highest)
                    total = jnp.sum(weights, axis=0, keepdims=True)
                    mixed = dot(values[:, :span], weights.astype(BF16)) / total
                    att_ref[heads, cols] = mixed.astype(BF16)
                    lse_ref[0, j : j + 1, cols] = highest + jnp.log(total)


def mid_kernel(
    near_ref, far_ref, no_ref, ng_ref, fo_ref, fg_ref, xo_ref, xg_ref, go_ref, gg_ref,
    mid_ref, nm_ref,
):
    near, far = near_ref[...], far_ref[...]
    own = xo_ref[...].astype(F32) + dot(no_ref[...], near, 0, 0) + dot(fo_ref[...], far, 0, 0)
    got = xg_ref[...].astype(F32) + dot(ng_ref[...], near, 0, 0) + dot(fg_ref[...], far, 0, 0)
    mid_ref[:HALF, :] = own
    mid_ref[HALF:, :] = got
    level = level_of(own, got)
    nm_ref[:HALF, :] = (own * level * go_ref[...]).astype(BF16)
    nm_ref[HALF:, :] = (got * level * gg_ref[...]).astype(BF16)


def mlp_kernel(
    nm_ref, og_ref, wgo_ref, wgg_ref, wuo_ref, wug_ref, wdo_ref, wdg_ref,
    out_ref, gnm_ref, act_ref, gg_ref, gu_ref, out_sum, gnm_sum,
):
    step = pl.program_id(0)

    def inward(own_ref, got_ref, rows_ref):
        return dot(own_ref[...], rows_ref[:HALF, :], 0, 0) + dot(
            got_ref[...], rows_ref[HALF:, :], 0, 0
        )

    @pl.when(step == 0)
    def _():
        out_sum[...] = jnp.zeros_like(out_sum)
        gnm_sum[...] = jnp.zeros_like(gnm_sum)

    gate = inward(wgo_ref, wgg_ref, nm_ref)
    up = inward(wuo_ref, wug_ref, nm_ref)
    grad_act = inward(wdo_ref, wdg_ref, og_ref)
    sig = jax.nn.sigmoid(gate)
    silu = gate * sig
    act = (silu * up).astype(BF16)
    grad_gate = (grad_act * up * sig * (1.0 + gate * (1.0 - sig))).astype(BF16)
    grad_up = (grad_act * silu).astype(BF16)
    act_ref[...] = act
    gg_ref[...] = grad_gate
    gu_ref[...] = grad_up
    gnm_sum[:HALF, :] += dot(wgo_ref[...], grad_gate) + dot(wuo_ref[...], grad_up)
    gnm_sum[HALF:, :] += dot(wgg_ref[...], grad_gate) + dot(wug_ref[...], grad_up)
    out_sum[:HALF, :] += dot(wdo_ref[...], act)
    out_sum[HALF:, :] += dot(wdg_ref[...], act)

    @pl.when(step == pl.num_programs(0) - 1)
    def _():
        out_ref[...] = out_sum[...].astype(out_ref.dtype)
        gnm_ref[...] = gnm_sum[...].astype(gnm_ref.dtype)


def grads_kernel(
    nm_ref, nm_far_ref, og_ref, og_far_ref, act_ref, act_far_ref, gg_ref, gg_far_ref, gu_ref,
    gu_far_ref, *out_refs,
):
    sources = (
        (og_ref, og_far_ref, act_ref, act_far_ref), (nm_ref, nm_far_ref, gg_ref, gg_far_ref),
        (nm_ref, nm_far_ref, gu_ref, gu_far_ref),
    )
    for which, (rows_ref, rows_far_ref, cols_ref, cols_far_ref) in enumerate(sources):
        for half in range(2):
            rows = slice(half * HALF, (half + 1) * HALF)
            product = dot(rows_ref[rows, :], cols_ref[...], 1, 1)
            product += dot(rows_far_ref[rows, :], cols_far_ref[...], 1, 1)
            out_refs[2 * which + half][...] = product.astype(BF16)


def gain_rows(product):
    return lax.dot_general(
        jnp.ones((16, product.shape[1]), F32), product, (((1,), (1,)), ((), ())),
        precision=lax.Precision.HIGHEST, preferred_element_type=F32,
    )


def mid_back_kernel(
    og_ref, mid_ref, part_ref, back_ref, go_ref, gg_ref, no_ref, ng_ref, fo_ref, fg_ref,
    gmid_ref, gb_ref, near_ref, far_ref, ggain_ref,
):
    own, got = mid_ref[:HALF, :], mid_ref[HALF:, :]
    level = level_of(own, got)
    gnm = part_ref[...] + back_ref[...].astype(F32)
    scaled_own, scaled_got = gnm[:HALF] * go_ref[...], gnm[HALF:] * gg_ref[...]
    inner = jnp.sum(scaled_own * own, axis=0, keepdims=True)
    inner += jnp.sum(scaled_got * got, axis=0, keepdims=True)
    pull = level**3 * inner / D
    for rows, mid, scaled in (
        (slice(0, HALF), own, scaled_own), (slice(HALF, D), got, scaled_got)
    ):
        ggain_ref[rows.start // HALF] = gain_rows(gnm[rows] * mid * level)
        gmid = og_ref[rows, :].astype(F32) + scaled * level - mid * pull
        gmid_ref[rows, :] = gmid
        gb_ref[rows, :] = gmid.astype(BF16)
    gb_own, gb_got = gb_ref[:HALF, :], gb_ref[HALF:, :]
    near_ref[...] = (dot(no_ref[...], gb_own) + dot(ng_ref[...], gb_got)).astype(BF16)
    far_ref[...] = (dot(fo_ref[...], gb_own) + dot(fg_ref[...], gb_got)).astype(BF16)


def attend_back_kernel(
    where_ref, begin_ref, q_ref, ko_ref, vo_ref, kg_ref, vg_ref, gatt_ref, lse_ref,
    dq_ref, own_ref, got_ref, bias_ref, dk_ref, dv_ref,
):
    group = pl.program_id(0)
    live = group < where_ref[1]

    @pl.when(jnp.logical_not(live))
    def _():
        dq_ref[...] = jnp.zeros_like(dq_ref)
        own_ref[...] = jnp.zeros_like(own_ref)
        got_ref[...] = jnp.zeros_like(got_ref)

    for core in range(2):

        @pl.when(live & (where_ref[0] == core))
        def _():
            @pl.when(group == 0)
            def _():
                fill_bias(core, bias_ref, begin_ref)

            keys_t = laid(core, ko_ref[...], kg_ref[...], 1)
            keys = keys_t.T
            values = laid(core, vo_ref[...], vg_ref[...], 1).T
            dk_ref[...] = jnp.zeros_like(dk_ref)
            dv_ref[...] = jnp.zeros_like(dv_ref)
            for slot in range(2):
                cols = slice(slot * BLOCK, (slot + 1) * BLOCK)
                span = SPANS[core][slot] * BLOCK
                for j in range(GROUP):
                    heads = slice(j * HDIM, (j + 1) * HDIM)
                    queries, grads = q_ref[heads, cols], gatt_ref[heads, cols]
                    scores = dot(keys[:span], queries) + bias_ref[:span, cols]
                    probs = jnp.exp(scores - lse_ref[0, j : j + 1, cols])
                    dprobs = dot(values[:span], grads)
                    inner = jnp.sum(probs * dprobs, axis=0, keepdims=True)
                    dscores = (probs * (dprobs - inner)).astype(BF16)
                    dv_ref[:span, :] += dot(probs.astype(BF16), grads.T)
                    dk_ref[:span, :] += dot(dscores, queries.T)
                    dq_ref[heads, cols] = dot(keys_t[:, :span], dscores) * SCALE
            for kind, grad_ref in enumerate((dk_ref, dv_ref)):
                if core == 0:
                    own_ref[kind, 0] = grad_ref[:LOCAL, :].T
                    got_ref[kind, 0] = grad_ref[LOCAL:, :].T.astype(BF16)
                else:
                    own_ref[kind, 0] = grad_ref[BLOCK : BLOCK + LOCAL, :].T
                    got_ref[kind, 0, :, :BLOCK] = grad_ref[:BLOCK, :].T.astype(BF16)
                    got_ref[kind, 0, :, BLOCK:] = jnp.zeros((HDIM, BLOCK), BF16)


def turn_back(cos_ref, sin_ref, dq_ref, own_ref, got_ref, gj_ref):
    cosine, sine = cos_ref[...], sin_ref[...]

    def back(at, grad):
        low, high = grad[:ROT], grad[ROT:]
        gj_ref[at : at + ROT, :] = (low * cosine + high * sine).astype(BF16)
        gj_ref[at + ROT : at + HDIM, :] = (high * cosine - low * sine).astype(BF16)

    for at in range(0, QUERY, HDIM):
        back(at, dq_ref[at : at + HDIM, :])
    for g in range(GROUPS):
        back(QUERY + g * HDIM, own_ref[0, g] + got_ref[0, g].astype(F32))
        at = QUERY + KEY + g * HDIM
        gj_ref[at : at + HDIM, :] = (own_ref[1, g] + got_ref[1, g].astype(F32)).astype(BF16)


def joined_far_kernel(
    dq_ref, own_ref, got_ref, cos_ref, sin_ref, wo_ref, wg_ref, nm_ref,
    gnm_ref, keep_ref, send_ref, gj_ref,
):
    turn_back(cos_ref, sin_ref, dq_ref, own_ref, got_ref, gj_ref)
    gj = gj_ref[...]
    for half, out_ref in enumerate((keep_ref, send_ref)):
        rows = slice(half * HALF, (half + 1) * HALF)
        out_ref[:D, :] = dot(gj, nm_ref[rows, :], 1, 1).astype(BF16)
        out_ref[D:, :] = jnp.zeros((ROWS - D, HALF), BF16)
    gnm_ref[:HALF, :] = dot(wo_ref[...], gj, 0, 0)
    gnm_ref[HALF:, :] = dot(wg_ref[...], gj, 0, 0)


def joined_near_kernel(
    dq_ref, own_ref, got_ref, cos_ref, sin_ref, wo_ref, wg_ref, nm_ref, part_ref, xo_ref, xg_ref,
    go_ref, gg_ref, gmid_ref, ggain_ref, keep_ref, send_ref, grad_ref, gj_ref,
):
    turn_back(cos_ref, sin_ref, dq_ref, own_ref, got_ref, gj_ref)
    gj = gj_ref[...]
    gnm_own = part_ref[:HALF, :] + dot(wo_ref[...], gj, 0, 0)
    gnm_got = part_ref[HALF:, :] + dot(wg_ref[...], gj, 0, 0)
    own, got = xo_ref[...].astype(F32), xg_ref[...].astype(F32)
    level = level_of(own, got)
    scaled_own, scaled_got = gnm_own * go_ref[...], gnm_got * gg_ref[...]
    inner = jnp.sum(scaled_own * own, axis=0, keepdims=True)
    inner += jnp.sum(scaled_got * got, axis=0, keepdims=True)
    pull = level**3 * inner / D
    for rows, x, gnm, scaled in (
        (slice(0, HALF), own, gnm_own, scaled_own), (slice(HALF, D), got, gnm_got, scaled_got)
    ):
        half = rows.start // HALF
        out_ref = (keep_ref, send_ref)[half]
        out_ref[:D, :] = dot(gj, nm_ref[rows, :], 1, 1).astype(BF16)
        out_ref[D : D + 16, :] = gain_rows(gnm * x * level).astype(BF16)
        out_ref[D + 16 : D + 32, :] = ggain_ref[half].astype(BF16)
        out_ref[D + 32 :, :] = jnp.zeros((ROWS - D - 32, HALF), BF16)
        grad_ref[rows, :] = (gmid_ref[rows, :] + scaled * level - x * pull).astype(BF16)


def per_group(rows, at=0):
    return pl.BlockSpec((rows, LOCAL), lambda g: (g + at, 0))


LSE_SPEC = pl.BlockSpec((1, 8, LOCAL), lambda g: (g, 0, 0))
KV_SPECS = [per_group(HDIM), per_group(HDIM, GROUPS)] * 2
PAIR_SPEC = pl.BlockSpec((2, 1, HDIM, LOCAL), lambda g: (0, g, 0, 0))


def attend(where, begin, q, kv, kv_got, after=()):
    return run(
        attend_kernel,
        (where, begin, q, kv, kv, kv_got, kv_got),
        (shape((QUERY, LOCAL)), shape((GROUPS, 8, LOCAL), F32)),
        6e9,
        grid=(GROUPS,),
        in_specs=[SMEM_SPEC, whole((1, LOCAL)), per_group(GROUP * HDIM)] + KV_SPECS,
        out_specs=(per_group(GROUP * HDIM), LSE_SPEC),
        scratch=[pltpu.VMEM((MAXLEN, LOCAL), F32)],
        after=after,
    )


def attend_back(where, begin, q, kv, kv_got, gatt, lse, after=()):
    return run(
        attend_back_kernel,
        (where, begin, q, kv, kv, kv_got, kv_got, gatt, lse),
        (
            shape((QUERY, LOCAL), F32), shape((2, GROUPS, HDIM, LOCAL), F32),
            shape((2, GROUPS, HDIM, LOCAL)),
        ),
        14e9,
        grid=(GROUPS,),
        in_specs=[SMEM_SPEC, whole((1, LOCAL)), per_group(GROUP * HDIM)]
        + KV_SPECS
        + [per_group(GROUP * HDIM), LSE_SPEC],
        out_specs=(per_group(GROUP * HDIM), PAIR_SPEC, PAIR_SPEC),
        scratch=[
            pltpu.VMEM((MAXLEN, LOCAL), F32), pltpu.VMEM((MAXLEN, HDIM), F32),
            pltpu.VMEM((MAXLEN, HDIM), F32),
        ],
        after=after,
    )


def feed_forward(nm, og, weights, dtype, after=()):
    hidden = weights[0].shape[1]
    chunk = 256
    cols = pl.BlockSpec((HALF, chunk), lambda i: (0, i))
    rows = pl.BlockSpec((chunk, LOCAL), lambda i: (i, 0))
    act = shape((hidden, LOCAL))
    return run(
        mlp_kernel,
        (nm, og) + weights,
        (shape((D, LOCAL), dtype), shape((D, LOCAL), dtype), act, act, act),
        12 * LOCAL * D * hidden,
        grid=(hidden // chunk,),
        in_specs=[whole((D, LOCAL))] * 2 + [cols] * 6,
        out_specs=(whole((D, LOCAL)), whole((D, LOCAL)), rows, rows, rows),
        scratch=[pltpu.VMEM((D, LOCAL), F32)] * 2,
        after=after,
    )


def weight_grads(nm, nm_far, og, og_far, act, act_far, gg, gg_far, gu, gu_far):
    hidden = act.shape[0]
    chunk = 256
    taken = pl.BlockSpec((chunk, LOCAL), lambda i: (i, 0))
    given = pl.BlockSpec((HALF, chunk), lambda i: (0, i))
    return run(
        grads_kernel,
        (nm, nm_far, og, og_far, act, act_far, gg, gg_far, gu, gu_far),
        (shape((HALF, hidden)),) * 6,
        12 * LOCAL * D * hidden,
        grid=(hidden // chunk,),
        in_specs=[whole((D, LOCAL))] * 4 + [taken] * 6,
        out_specs=(given,) * 6,
    )


def swap(array, axis):
    return lax.ppermute(array, axis, [(0, 1), (1, 0)])


def stages(count):
    found, stride = [], 1
    for size in (2,) + (4,) * 16:
        size = min(size, count // stride)
        if size < 2:
            break
        found.append((stride, size))
        stride *= size
    return found


def shift_pairs(count, stride, size, step):
    pairs = []
    for i in range(count):
        digit = i // stride % size
        pairs.append((i, i + ((digit + step) % size - digit) * stride))
    return pairs


def split_rows(array, count):
    rows, cols = array.shape
    return array.reshape(*[size for _, size in stages(count)], rows // count, cols)


def reduce_stage(total, count, stage, held=()):
    stride, size = stages(count)[stage]
    digit = lax.axis_index("dp") // stride % size
    kept = lax.dynamic_index_in_dim(total, digit, 0, keepdims=False).astype(F32)
    found = []
    for step in range(1, size):
        sent = lax.dynamic_index_in_dim(total, (digit + step) % size, 0, keepdims=False)
        found.append(lax.ppermute(sent, "dp", shift_pairs(count, stride, size, step)))
    for got in hold_all(found, held):
        kept = kept + got.astype(F32)
    return kept.astype(BF16)


def gather_stage(part, count, stage, held=()):
    stride, size = stages(count)[stage]
    digit = lax.axis_index("dp") // stride % size
    found = [
        lax.ppermute(part, "dp", shift_pairs(count, stride, size, step)) for step in range(1, size)
    ]
    spread = jnp.zeros((size,) + part.shape, BF16)
    spread = lax.dynamic_update_index_in_dim(spread, part, digit, 0)
    for step, got in enumerate(hold_all(found, held), 1):
        spread = lax.dynamic_update_index_in_dim(spread, got, (digit - step) % size, 0)
    return spread


def reduce_first(array, count, held=()):
    return reduce_stage(split_rows(array, count), count, 0, held)


def reduce_rest(total, count, held=()):
    for stage in range(1, len(stages(count))):
        total = reduce_stage(total, count, stage, held)
    return total


def gather_rest(total, count, held=()):
    for stage in reversed(range(1, len(stages(count)))):
        total = gather_stage(total, count, stage, held)
    return total


def gather_first(total, count, dims, held=()):
    return gather_stage(total, count, 0, held).reshape(dims).astype(F32)


def hold_all(arrays, others):
    if not others:
        return arrays
    return lax.optimization_barrier(tuple(arrays) + tuple(others))[: len(arrays)]


def hold(array, *others):
    return lax.optimization_barrier((array,) + others)[0]


def add(*parts):
    return sum(part.astype(F32) for part in parts).astype(BF16)


def segment_begin(segment):
    index = jnp.arange(segment.shape[0], dtype=jnp.int32)
    is_start = jnp.concatenate([jnp.ones((1,), dtype=bool), segment[1:] != segment[:-1]])
    return lax.cummax(jnp.where(is_start, index, jnp.zeros_like(index)), axis=0)


def rope_tables(position):
    frequency = ROPE_BASE ** (-(jnp.arange(ROT, dtype=F32) * 2.0 / HDIM))
    angles = frequency[:, None] * position.astype(F32)[None, :]
    return jnp.cos(angles), jnp.sin(angles)


def per_device(
    count,
    hidden_in,
    query_weight,
    key_weight,
    value_weight,
    output_weight,
    gate_weight,
    up_weight,
    down_weight,
    attn_gain,
    ffn_gain,
    out_grad,
    segment_ids,
):
    col, row = lax.axis_index("col"), lax.axis_index("row")
    first = col == 0

    def own_tokens(array):
        outer = jnp.concatenate([array[..., :BLOCK], array[..., 3 * BLOCK :]], axis=-1)
        inner = array[..., BLOCK : 3 * BLOCK]
        return jnp.where(first, outer, inner), jnp.where(first, inner, outer)

    def in_window(own, got):
        outer, inner = jnp.where(first, own, got), jnp.where(first, got, own)
        return jnp.concatenate([outer[:, :BLOCK], inner, outer[:, BLOCK:]], axis=1)

    w_near = jnp.concatenate(
        [query_weight[:, 0].T, key_weight[:, 0].T, value_weight[:, 0].T], axis=0
    )
    w_far = swap(w_near, "row")
    x_own, x_other = own_tokens(hidden_in.T)
    x_got = swap(x_other, "col")
    gains = jnp.stack([attn_gain, ffn_gain])
    gains_got = swap(gains, "col").astype(F32)
    gains = gains.astype(F32)
    gin_own, gmid_own = gains[0][:, None], gains[1][:, None]
    gin_got, gmid_got = gains_got[0][:, None], gains_got[1][:, None]
    segment = jnp.where(col == row, segment_ids, swap(segment_ids, "col"))
    begin, _ = own_tokens(segment_begin(segment))
    index, _ = own_tokens(jnp.arange(MAXLEN, dtype=jnp.int32))
    cosine, sine = rope_tables(index - begin)
    begin = begin[None]
    live_near = jnp.where(row == 0, LIVE[0], LIVE[1])
    where_near = jnp.stack([col, live_near]).astype(jnp.int32)
    where_far = jnp.stack([col, LIVE[0] + LIVE[1] - live_near]).astype(jnp.int32)

    w_near_got = swap(w_near, "col")
    heads = (shape((QUERY, LOCAL)), shape((2 * KEY, LOCAL)))
    nm_in, q_near, kv_near = run(
        project_near_kernel,
        (x_own, x_got, gin_own, gin_got, cosine, sine, w_near, w_near_got),
        (shape((D, LOCAL)),) + heads,
        2 * LOCAL * D * D,
    )
    kv_near_got = swap(kv_near, "col")
    wo_near = output_weight[0]
    wo_far = swap(wo_near, "row")
    wo_near_got = swap(wo_near, "col")
    att_near, lse_near = attend(where_near, begin, q_near, kv_near, kv_near_got)
    w_far_got = swap(hold(w_far, lse_near), "col")
    q_far, kv_far = run(
        project_far_kernel,
        (nm_in, cosine, sine, w_far, w_far_got),
        heads,
        2 * LOCAL * D * D,
    )
    kv_far_got = swap(kv_far, "col")
    att_far, lse_far = attend(where_far, begin, q_far, kv_far, kv_far_got, after=(wo_far,))
    wo_far_got = swap(wo_far, "col")
    og_own, og_other = own_tokens(out_grad.T)
    og = jnp.concatenate([og_own, swap(og_other, "col")], axis=0)
    og_far = swap(og, "row")
    mid, nm = run(
        mid_kernel,
        (
            att_near, att_far, wo_near, wo_near_got, wo_far, wo_far_got, x_own, x_got,
            gmid_own, gmid_got,
        ),
        (shape((D, LOCAL), F32), shape((D, LOCAL))),
        2 * LOCAL * D * D,
        after=(og_far,),
    )

    mlp_weights = ()
    for weight in (gate_weight, up_weight, down_weight.T):
        mlp_weights += (weight, swap(weight, "col"))
    nm_far = swap(nm, "row")
    out_part, gnm_part, act, gg, gu = feed_forward(nm, og, mlp_weights, F32)
    out_send, gnm_send, act_far, gg_far, gu_far = feed_forward(
        nm_far, og_far, mlp_weights, BF16, after=(act,)
    )
    gnm_back = swap(gnm_send, "row")
    down_keep, down_send, gate_keep, gate_send, up_keep, up_send = weight_grads(
        nm, nm_far, og, og_far, act, act_far, gg, gg_far, gu, gu_far
    )
    down_sum = add(down_keep, swap(down_send, "col"))
    gate_sum = add(gate_keep, swap(gate_send, "col"))
    up_sum = add(up_keep, swap(up_send, "col"))
    down_grad = lax.psum(down_sum, "dp")

    gmid, gb, gatt_near, gatt_far, ggain_mid = run(
        mid_back_kernel,
        (
            og, mid, gnm_part, gnm_back, gmid_own, gmid_got, wo_near, wo_near_got, wo_far,
            wo_far_got,
        ),
        (
            shape((D, LOCAL), F32), shape((D, LOCAL)), shape((QUERY, LOCAL)),
            shape((QUERY, LOCAL)), shape((2, 16, HALF), F32),
        ),
        2 * LOCAL * D * D,
        after=(up_keep,),
    )

    dq_far, own_far, other_far = attend_back(
        where_far, begin, q_far, kv_far, kv_far_got, gatt_far, lse_far, after=(down_sum, gate_sum, up_sum)
    )
    out_back = hold(swap(hold(out_send, gnm_back), "row"), dq_far)
    block = (mid + out_part + out_back.astype(F32)).astype(BF16)

    def out_grads(att):
        send = dot(att, gb[HALF:], 1, 1).astype(BF16)
        return add(dot(att, gb[:HALF], 1, 1), hold(swap(send, "col"), dq_far))

    wo_far_sum = out_grads(att_far)
    wo_near_sum = out_grads(att_near)
    got_far = swap(other_far, "col")
    joined = shape((ROWS, HALF))
    gnm_in_part, far_keep, far_send = run(
        joined_far_kernel,
        (dq_far, own_far, got_far, cosine, sine, w_far, w_far_got, nm_in),
        (shape((D, LOCAL), F32), joined, joined),
        4 * LOCAL * D * D,
        after=(wo_far_sum, wo_near_sum, block),
        scratch=[pltpu.VMEM((D, LOCAL), BF16)],
    )
    dq_near, own_near, other_near = attend_back(
        where_near, begin, q_near, kv_near, kv_near_got, gatt_near, lse_near, after=(far_keep,)
    )
    far_sum = add(far_keep, hold(swap(far_send, "col"), dq_near))
    wo_sum = add(wo_near_sum, hold(swap(wo_far_sum, "row"), dq_near))
    down_grad = hold(down_grad, dq_near)
    got_near = swap(other_near, "col")
    near_keep, near_send, grad = run(
        joined_near_kernel,
        (
            dq_near, own_near, got_near, cosine, sine, w_near, w_near_got, nm_in, gnm_in_part,
            x_own, x_got, gin_own, gin_got, gmid, ggain_mid,
        ),
        (joined, joined, shape((D, LOCAL))),
        4 * LOCAL * D * D,
        after=(wo_sum, far_sum, down_grad),
        scratch=[pltpu.VMEM((D, LOCAL), BF16)],
    )
    last_sum = add(near_keep, swap(near_send, "col"), swap(far_sum, "row"))

    def feature_cols(array):
        return in_window(array[:HALF], swap(array[HALF:], "col")).T

    block_out = feature_cols(block)
    input_grad = feature_cols(grad)

    gate_grad = lax.psum(hold(gate_sum, down_grad), "dp")
    last_sum = jnp.concatenate([last_sum, wo_sum], axis=0)
    last_z = reduce_rest(reduce_first(last_sum, count), count, (gate_grad,))
    up_grad = lax.psum(hold(up_sum, gate_grad), "dp")
    last = gather_first(gather_rest(last_z, count), count, last_sum.shape)
    gain_grads = jnp.stack([last[D], last[D + 16]])
    gain_grads = gain_grads + swap(gain_grads, "row")
    return (
        block_out,
        input_grad,
        last[:QUERY].T[:, None, :],
        last[QUERY : QUERY + KEY].T[:, None, :],
        last[QUERY + KEY : D].T[:, None, :],
        last[ROWS:][None],
        gate_grad.astype(F32),
        up_grad.astype(F32),
        down_grad.astype(F32).T,
        gain_grads[0],
        gain_grads[1],
    )


def solution(mesh):
    return jax.shard_map(
        functools.partial(per_device, mesh.shape["dp"]),
        mesh=mesh,
        in_specs=(
            P(("dp", "row"), "col"),
            P("col", "row", None),
            P("col", "row", None),
            P("col", "row", None),
            P("row", None, "col"),
            P("col", "row"),
            P("col", "row"),
            P("row", "col"),
            P("col"),
            P("col"),
            P(("dp", "row"), "col"),
            P(("dp", "col")),
        ),
        out_specs=(
            P(("dp", "row"), "col"),
            P(("dp", "row"), "col"),
            P("col", "row", None),
            P("col", "row", None),
            P("col", "row", None),
            P("row", None, "col"),
            P("col", "row"),
            P("col", "row"),
            P("row", "col"),
            P("col"),
            P("col"),
        ),
        check_vma=False,
    )
```

```python
import functools
import math

import jax
import jax.numpy as jnp
from jax import lax
from jax.experimental import pallas as pl
from jax.experimental.pallas import tpu as pltpu
from jax.sharding import PartitionSpec as P

D = 960
HALF = D // 2
HDIM = 64
ROT = HDIM // 2
GROUP = 3
GROUPS = 3
QUERY = GROUPS * GROUP * HDIM
KEY = GROUPS * HDIM
MAXLEN = 1024
BLOCK = MAXLEN // 4
LOCAL = 2 * BLOCK
LANE = 128
LIVE = (3, 2)
ROWS = 1024

NORM_EPS = 1e-05
ROPE_BASE = 100000.0
MASKED_SCORE = -1e30
SCALE = 1.0 / math.sqrt(HDIM)
BF16 = jnp.bfloat16
F32 = jnp.float32
VMEM_BYTES = 56 * 1024 * 1024
COST = 0.03

HELD = ((0, 3), (1, 2))
LAID = ((0, 3, 1, 2), (0, 1, 2))
SPANS = ((1, 4), (2, 3))


def dot(left, right, left_dim=1, right_dim=0):
    return lax.dot_general(
        left, right, (((left_dim,), (right_dim,)), ((), ())), preferred_element_type=F32
    )


def shape(dims, dtype=BF16):
    return jax.ShapeDtypeStruct(dims, dtype)


def whole(dims):
    return pl.BlockSpec(dims, lambda *_: (0,) * len(dims))


SMEM_SPEC = pl.BlockSpec(memory_space=pltpu.SMEM)


def run(kernel, ins, outs, flops, grid=None, in_specs=None, out_specs=None, scratch=(), after=()):
    moved = sum(a.size * a.dtype.itemsize for a in ins)
    moved += sum(math.prod(o.shape) * jnp.dtype(o.dtype).itemsize for o in outs)
    if in_specs is None:
        in_specs = [whole(a.shape) for a in ins]
    if out_specs is None:
        out_specs = [whole(o.shape) for o in outs]
    count = len(ins)

    def body(*refs):
        kernel(*refs[:count], *refs[count + len(after) :])

    return pl.pallas_call(
        body,
        grid=grid if grid is not None else (1,),
        in_specs=list(in_specs) + [pl.BlockSpec(memory_space=pl.ANY)] * len(after),
        out_specs=tuple(out_specs),
        out_shape=tuple(outs),
        scratch_shapes=list(scratch),
        compiler_params=pltpu.CompilerParams(vmem_limit_bytes=VMEM_BYTES),
        cost_estimate=pl.CostEstimate(
            flops=int(flops * COST), bytes_accessed=int(moved * COST), transcendentals=0
        ),
    )(*ins, *after)


def level_of(own, got):
    total = jnp.sum(own * own, axis=0, keepdims=True) + jnp.sum(got * got, axis=0, keepdims=True)
    return lax.rsqrt(total / D + NORM_EPS)


def project_heads(nm, cos_ref, sin_ref, own_ref, got_ref, q_ref, kv_ref):
    cosine, sine = cos_ref[...], sin_ref[...]
    joined = dot(own_ref[...], nm[:HALF]) + dot(got_ref[...], nm[HALF:])
    for at in range(0, QUERY + KEY, HDIM):
        low, high = joined[at : at + ROT], joined[at + ROT : at + HDIM]
        parts = (low * cosine - high * sine, high * cosine + low * sine)
        for part, turned in enumerate(parts):
            turned = turned.astype(BF16)
            if at < QUERY:
                turned = (turned.astype(F32) * SCALE).astype(BF16)
                q_ref[at + part * ROT : at + (part + 1) * ROT, :] = turned
            else:
                row = at - QUERY + part * ROT
                kv_ref[row : row + ROT, :] = turned
    kv_ref[KEY:, :] = joined[QUERY + KEY :].astype(BF16)


def project_near_kernel(
    xo_ref, xg_ref, go_ref, gg_ref, cos_ref, sin_ref, own_ref, got_ref, nm_ref, q_ref, kv_ref
):
    own, got = xo_ref[...].astype(F32), xg_ref[...].astype(F32)
    level = level_of(own, got)
    nm_ref[:HALF, :] = (own * level * go_ref[...]).astype(BF16)
    nm_ref[HALF:, :] = (got * level * gg_ref[...]).astype(BF16)
    project_heads(nm_ref[...], cos_ref, sin_ref, own_ref, got_ref, q_ref, kv_ref)


def project_far_kernel(nm_ref, cos_ref, sin_ref, own_ref, got_ref, q_ref, kv_ref):
    project_heads(nm_ref[...], cos_ref, sin_ref, own_ref, got_ref, q_ref, kv_ref)


def laid(core, own, got, axis):
    if core == 0:
        return jnp.concatenate([own, got], axis=axis)
    return jnp.concatenate([lax.slice_in_dim(got, 0, BLOCK, axis=axis), own], axis=axis)


def fill_bias(core, bias_ref, begin_ref):
    for at, block in enumerate(LAID[core]):
        for slot in range(2):
            cols = slice(slot * BLOCK, (slot + 1) * BLOCK)
            key = block * BLOCK + lax.broadcasted_iota(jnp.int32, (BLOCK, BLOCK), 0)
            query = HELD[core][slot] * BLOCK + lax.broadcasted_iota(jnp.int32, (BLOCK, BLOCK), 1)
            allowed = (key >= begin_ref[:, cols]) & (key <= query)
            bias_ref[at * BLOCK : (at + 1) * BLOCK, cols] = jnp.where(allowed, 0.0, MASKED_SCORE)


def attend_kernel(
    where_ref, begin_ref, q_ref, ko_ref, vo_ref, kg_ref, vg_ref, att_ref, lse_ref, bias_ref
):
    group = pl.program_id(0)
    live = group < where_ref[1]

    @pl.when(jnp.logical_not(live))
    def _():
        att_ref[...] = jnp.zeros_like(att_ref)
        lse_ref[...] = jnp.zeros_like(lse_ref)

    for core in range(2):

        @pl.when(live & (where_ref[0] == core))
        def _():
            @pl.when(group == 0)
            def _():
                fill_bias(core, bias_ref, begin_ref)

            keys = laid(core, ko_ref[...], kg_ref[...], 1).T
            values = laid(core, vo_ref[...], vg_ref[...], 1)
            for slot in range(2):
                cols = slice(slot * BLOCK, (slot + 1) * BLOCK)
                span = SPANS[core][slot] * BLOCK
                for j in range(GROUP):
                    heads = slice(j * HDIM, (j + 1) * HDIM)
                    scores = dot(keys[:span], q_ref[heads, cols]) + bias_ref[:span, cols]
                    highest = jnp.max(scores, axis=0, keepdims=True)
                    weights = jnp.exp(scores - highest)
                    total = jnp.sum(weights, axis=0, keepdims=True)
                    mixed = dot(values[:, :span], weights.astype(BF16)) / total
                    att_ref[heads, cols] = mixed.astype(BF16)
                    lse_ref[0, j : j + 1, cols] = highest + jnp.log(total)


def mid_kernel(
    near_ref, far_ref, no_ref, ng_ref, fo_ref, fg_ref, xo_ref, xg_ref, go_ref, gg_ref,
    mid_ref, nma_ref, nmb_ref,
):
    near, far = near_ref[...], far_ref[...]
    own = xo_ref[...].astype(F32) + dot(no_ref[...], near, 0, 0) + dot(fo_ref[...], far, 0, 0)
    got = xg_ref[...].astype(F32) + dot(ng_ref[...], near, 0, 0) + dot(fg_ref[...], far, 0, 0)
    mid_ref[:HALF, :] = own
    mid_ref[HALF:, :] = got
    level = level_of(own, got)
    for rows, part, gain_ref in ((slice(0, HALF), own, go_ref), (slice(HALF, D), got, gg_ref)):
        normed = (part * level * gain_ref[...]).astype(BF16)
        nma_ref[rows, :] = normed[:, :BLOCK]
        nmb_ref[rows, :] = normed[:, BLOCK:]


def mlp_kernel(pieces, *refs):
    nm_refs = refs[:pieces]
    og_ref, wgo_ref, wgg_ref, wuo_ref, wug_ref, wdo_ref, wdg_ref = refs[pieces : pieces + 7]
    out_ref, gnm_ref, act_ref, gg_ref, gu_ref, out_sum, gnm_sum = refs[pieces + 7 :]
    step = pl.program_id(0)
    nm, og = jnp.concatenate([ref[...] for ref in nm_refs], axis=1), og_ref[...]

    def inward(own_ref, got_ref, rows):
        return dot(own_ref[...], rows[:HALF], 0, 0) + dot(got_ref[...], rows[HALF:], 0, 0)

    @pl.when(step == 0)
    def _():
        out_sum[...] = jnp.zeros_like(out_sum)
        gnm_sum[...] = jnp.zeros_like(gnm_sum)

    gate = inward(wgo_ref, wgg_ref, nm)
    up = inward(wuo_ref, wug_ref, nm)
    grad_act = inward(wdo_ref, wdg_ref, og)
    sig = jax.nn.sigmoid(gate)
    silu = gate * sig
    act = (silu * up).astype(BF16)
    grad_gate = (grad_act * up * sig * (1.0 + gate * (1.0 - sig))).astype(BF16)
    grad_up = (grad_act * silu).astype(BF16)
    act_ref[...] = act
    gg_ref[...] = grad_gate
    gu_ref[...] = grad_up
    gnm_sum[:HALF, :] += dot(wgo_ref[...], grad_gate) + dot(wuo_ref[...], grad_up)
    gnm_sum[HALF:, :] += dot(wgg_ref[...], grad_gate) + dot(wug_ref[...], grad_up)
    out_sum[:HALF, :] += dot(wdo_ref[...], act)
    out_sum[HALF:, :] += dot(wdg_ref[...], act)

    @pl.when(step == pl.num_programs(0) - 1)
    def _():
        out_ref[...] = out_sum[...].astype(out_ref.dtype)
        gnm_ref[...] = gnm_sum[...].astype(gnm_ref.dtype)


def grads_kernel(row_counts, col_counts, rows_of, *refs):
    at = 0

    def whole_tokens(count):
        nonlocal at
        at += count
        return jnp.concatenate([ref[...] for ref in refs[at - count : at]], axis=1)

    rows = [whole_tokens(count) for count in row_counts]
    for kind, count in enumerate(col_counts):
        cols = whole_tokens(count)
        for half in range(2):
            left = rows[rows_of[kind]][half * HALF : (half + 1) * HALF]
            product = dot(left, cols, 1, 1).astype(BF16)
            out_ref = refs[len(refs) - 2 * len(col_counts) + 2 * kind + half]
            out_ref[:HALF, :] = product[:, :LANE]
            out_ref[HALF:, :] = product[:, LANE:]


def gain_rows(product):
    return lax.dot_general(
        jnp.ones((16, product.shape[1]), F32), product, (((1,), (1,)), ((), ())),
        precision=lax.Precision.HIGHEST, preferred_element_type=F32,
    )


def mid_back_kernel(
    og_ref, mid_ref, part_ref, bka_ref, bkb_ref, go_ref, gg_ref, no_ref, ng_ref, fo_ref, fg_ref,
    gmid_ref, gb_ref, near_ref, far_ref, ggain_ref,
):
    own, got = mid_ref[:HALF, :], mid_ref[HALF:, :]
    level = level_of(own, got)
    back = jnp.concatenate([bka_ref[...], bkb_ref[...]], axis=1)
    gnm = part_ref[...] + back.astype(F32)
    scaled_own, scaled_got = gnm[:HALF] * go_ref[...], gnm[HALF:] * gg_ref[...]
    inner = jnp.sum(scaled_own * own, axis=0, keepdims=True)
    inner += jnp.sum(scaled_got * got, axis=0, keepdims=True)
    pull = level**3 * inner / D
    for rows, mid, scaled in (
        (slice(0, HALF), own, scaled_own), (slice(HALF, D), got, scaled_got)
    ):
        ggain_ref[rows.start // HALF] = gain_rows(gnm[rows] * mid * level)
        gmid = og_ref[rows, :].astype(F32) + scaled * level - mid * pull
        gmid_ref[rows, :] = gmid
        gb_ref[rows, :] = gmid.astype(BF16)
    gb_own, gb_got = gb_ref[:HALF, :], gb_ref[HALF:, :]
    near_ref[...] = (dot(no_ref[...], gb_own) + dot(ng_ref[...], gb_got)).astype(BF16)
    far_ref[...] = (dot(fo_ref[...], gb_own) + dot(fg_ref[...], gb_got)).astype(BF16)


def attend_back_kernel(
    where_ref, begin_ref, q_ref, ko_ref, vo_ref, kg_ref, vg_ref, gatt_ref, lse_ref,
    dq_ref, own_ref, got_ref, bias_ref, dk_ref, dv_ref,
):
    group = pl.program_id(0)
    live = group < where_ref[1]

    @pl.when(jnp.logical_not(live))
    def _():
        dq_ref[...] = jnp.zeros_like(dq_ref)
        own_ref[...] = jnp.zeros_like(own_ref)
        got_ref[...] = jnp.zeros_like(got_ref)

    for core in range(2):

        @pl.when(live & (where_ref[0] == core))
        def _():
            @pl.when(group == 0)
            def _():
                fill_bias(core, bias_ref, begin_ref)

            keys_t = laid(core, ko_ref[...], kg_ref[...], 1)
            keys = keys_t.T
            values = laid(core, vo_ref[...], vg_ref[...], 1).T
            dk_ref[...] = jnp.zeros_like(dk_ref)
            dv_ref[...] = jnp.zeros_like(dv_ref)
            for slot in range(2):
                cols = slice(slot * BLOCK, (slot + 1) * BLOCK)
                span = SPANS[core][slot] * BLOCK
                for j in range(GROUP):
                    heads = slice(j * HDIM, (j + 1) * HDIM)
                    queries, grads = q_ref[heads, cols], gatt_ref[heads, cols]
                    scores = dot(keys[:span], queries) + bias_ref[:span, cols]
                    probs = jnp.exp(scores - lse_ref[0, j : j + 1, cols])
                    dprobs = dot(values[:span], grads)
                    inner = jnp.sum(probs * dprobs, axis=0, keepdims=True)
                    dscores = (probs * (dprobs - inner)).astype(BF16)
                    dv_ref[:span, :] += dot(probs.astype(BF16), grads.T)
                    dk_ref[:span, :] += dot(dscores, queries.T)
                    dq_ref[heads, cols] = dot(keys_t[:, :span], dscores) * SCALE
            for kind, grad_ref in enumerate((dk_ref, dv_ref)):
                if core == 0:
                    own_ref[kind, 0] = grad_ref[:LOCAL, :].T
                    got_ref[kind, 0] = grad_ref[LOCAL:, :].T.astype(BF16)
                else:
                    own_ref[kind, 0] = grad_ref[BLOCK : BLOCK + LOCAL, :].T
                    got_ref[kind, 0, :, :BLOCK] = grad_ref[:BLOCK, :].T.astype(BF16)
                    got_ref[kind, 0, :, BLOCK:] = jnp.zeros((HDIM, BLOCK), BF16)


def turn_back(cos_ref, sin_ref, dq_ref, own_ref, got_ref, gj_ref):
    cosine, sine = cos_ref[...], sin_ref[...]

    def back(at, grad):
        low, high = grad[:ROT], grad[ROT:]
        gj_ref[at : at + ROT, :] = (low * cosine + high * sine).astype(BF16)
        gj_ref[at + ROT : at + HDIM, :] = (high * cosine - low * sine).astype(BF16)

    for at in range(0, QUERY, HDIM):
        back(at, dq_ref[at : at + HDIM, :])
    for g in range(GROUPS):
        back(QUERY + g * HDIM, own_ref[0, g] + got_ref[0, g].astype(F32))
        at = QUERY + KEY + g * HDIM
        gj_ref[at : at + HDIM, :] = (own_ref[1, g] + got_ref[1, g].astype(F32)).astype(BF16)


def joined_far_kernel(
    dq_ref, own_ref, got_ref, cos_ref, sin_ref, wo_ref, wg_ref, nm_ref,
    gnm_ref, keep_ref, send_ref, gj_ref,
):
    turn_back(cos_ref, sin_ref, dq_ref, own_ref, got_ref, gj_ref)
    gj = gj_ref[...]
    for half, out_ref in enumerate((keep_ref, send_ref)):
        rows = slice(half * HALF, (half + 1) * HALF)
        out_ref[:D, :] = dot(gj, nm_ref[rows, :], 1, 1).astype(BF16)
        out_ref[D:, :] = jnp.zeros((ROWS - D, HALF), BF16)
    gnm_ref[:HALF, :] = dot(wo_ref[...], gj, 0, 0)
    gnm_ref[HALF:, :] = dot(wg_ref[...], gj, 0, 0)


def joined_near_kernel(
    dq_ref, own_ref, got_ref, cos_ref, sin_ref, wo_ref, wg_ref, nm_ref, part_ref, xo_ref, xg_ref,
    go_ref, gg_ref, gmid_ref, ggain_ref, keep_ref, send_ref, grad_ref, gj_ref,
):
    turn_back(cos_ref, sin_ref, dq_ref, own_ref, got_ref, gj_ref)
    gj = gj_ref[...]
    gnm_own = part_ref[:HALF, :] + dot(wo_ref[...], gj, 0, 0)
    gnm_got = part_ref[HALF:, :] + dot(wg_ref[...], gj, 0, 0)
    own, got = xo_ref[...].astype(F32), xg_ref[...].astype(F32)
    level = level_of(own, got)
    scaled_own, scaled_got = gnm_own * go_ref[...], gnm_got * gg_ref[...]
    inner = jnp.sum(scaled_own * own, axis=0, keepdims=True)
    inner += jnp.sum(scaled_got * got, axis=0, keepdims=True)
    pull = level**3 * inner / D
    for rows, x, gnm, scaled in (
        (slice(0, HALF), own, gnm_own, scaled_own), (slice(HALF, D), got, gnm_got, scaled_got)
    ):
        half = rows.start // HALF
        out_ref = (keep_ref, send_ref)[half]
        out_ref[:D, :] = dot(gj, nm_ref[rows, :], 1, 1).astype(BF16)
        out_ref[D : D + 16, :] = gain_rows(gnm * x * level).astype(BF16)
        out_ref[D + 16 : D + 32, :] = ggain_ref[half].astype(BF16)
        out_ref[D + 32 :, :] = jnp.zeros((ROWS - D - 32, HALF), BF16)
        grad_ref[rows, :] = (gmid_ref[rows, :] + scaled * level - x * pull).astype(BF16)


def per_group(rows, at=0):
    return pl.BlockSpec((rows, LOCAL), lambda g: (g + at, 0))


LSE_SPEC = pl.BlockSpec((1, 8, LOCAL), lambda g: (g, 0, 0))
KV_SPECS = [per_group(HDIM), per_group(HDIM, GROUPS)] * 2
PAIR_SPEC = pl.BlockSpec((2, 1, HDIM, LOCAL), lambda g: (0, g, 0, 0))


def attend(where, begin, q, kv, kv_got, after=()):
    return run(
        attend_kernel,
        (where, begin, q, kv, kv, kv_got, kv_got),
        (shape((QUERY, LOCAL)), shape((GROUPS, 8, LOCAL), F32)),
        6e9,
        grid=(GROUPS,),
        in_specs=[SMEM_SPEC, whole((1, LOCAL)), per_group(GROUP * HDIM)] + KV_SPECS,
        out_specs=(per_group(GROUP * HDIM), LSE_SPEC),
        scratch=[pltpu.VMEM((MAXLEN, LOCAL), F32)],
        after=after,
    )


def attend_back(where, begin, q, kv, kv_got, gatt, lse, after=()):
    return run(
        attend_back_kernel,
        (where, begin, q, kv, kv, kv_got, kv_got, gatt, lse),
        (
            shape((QUERY, LOCAL), F32), shape((2, GROUPS, HDIM, LOCAL), F32),
            shape((2, GROUPS, HDIM, LOCAL)),
        ),
        14e9,
        grid=(GROUPS,),
        in_specs=[SMEM_SPEC, whole((1, LOCAL)), per_group(GROUP * HDIM)]
        + KV_SPECS
        + [per_group(GROUP * HDIM), LSE_SPEC],
        out_specs=(per_group(GROUP * HDIM), PAIR_SPEC, PAIR_SPEC),
        scratch=[
            pltpu.VMEM((MAXLEN, LOCAL), F32), pltpu.VMEM((MAXLEN, HDIM), F32),
            pltpu.VMEM((MAXLEN, HDIM), F32),
        ],
        after=after,
    )


def feed_forward(nms, og, at, weights, dtype, after=()):
    hidden = weights[0].shape[1]
    tokens = sum(nm.shape[1] for nm in nms)
    chunk = 256
    cols = pl.BlockSpec((HALF, chunk), lambda i: (0, i))
    rows = pl.BlockSpec((chunk, tokens), lambda i: (i, 0))
    act = shape((hidden, tokens))
    return run(
        functools.partial(mlp_kernel, len(nms)),
        tuple(nms) + (og,) + weights,
        (shape((D, tokens), dtype), shape((D, tokens), dtype), act, act, act),
        12 * tokens * D * hidden,
        grid=(hidden // chunk,),
        in_specs=[whole(nm.shape) for nm in nms]
        + [pl.BlockSpec((D, tokens), lambda i: (0, at))]
        + [cols] * 6,
        out_specs=(whole((D, tokens)), whole((D, tokens)), rows, rows, rows),
        scratch=[pltpu.VMEM((D, tokens), F32)] * 2,
        after=after,
    )


def weight_grads(rows, cols, rows_of, after=()):
    hidden = cols[0][0].shape[0]
    chunk = 2 * LANE
    all_rows, all_cols = sum(rows, ()), sum(cols, ())
    return run(
        functools.partial(
            grads_kernel, [len(pieces) for pieces in rows], [len(pieces) for pieces in cols], rows_of
        ),
        all_rows + all_cols,
        (shape((hidden // LANE * HALF, LANE)),) * (2 * len(cols)),
        4 * LOCAL * D * hidden * len(cols),
        grid=(hidden // chunk,),
        in_specs=[whole(part.shape) for part in all_rows]
        + [pl.BlockSpec((chunk, part.shape[1]), lambda i: (i, 0)) for part in all_cols],
        out_specs=(pl.BlockSpec((2 * HALF, LANE), lambda i: (i, 0)),) * (2 * len(cols)),
        after=after,
    )


def swap(array, axis):
    return lax.ppermute(array, axis, [(0, 1), (1, 0)])


def stages(count):
    found, stride = [], 1
    for size in (2,) + (4,) * 16:
        size = min(size, count // stride)
        if size < 2:
            break
        found.append((stride, size))
        stride *= size
    return found


def shift_pairs(count, stride, size, step):
    pairs = []
    for i in range(count):
        digit = i // stride % size
        pairs.append((i, i + ((digit + step) % size - digit) * stride))
    return pairs


def split_rows(array, count):
    rows, cols = array.shape
    sizes = [size for _, size in stages(count)]
    return array.reshape(*sizes[::-1], rows // count, cols)


def reduce_stage(total, count, stage, held=()):
    stride, size = stages(count)[stage]
    digit = lax.axis_index("dp") // stride % size
    axis = total.ndim - 3
    kept = lax.dynamic_index_in_dim(total, digit, axis, keepdims=False).astype(F32)
    found = []
    for step in range(1, size):
        sent = lax.dynamic_index_in_dim(total, (digit + step) % size, axis, keepdims=False)
        found.append(lax.ppermute(sent, "dp", shift_pairs(count, stride, size, step)))
    for got in hold_all(found, held):
        kept = kept + got.astype(F32)
    return kept.astype(BF16)


def reduce_first(array, count, held=()):
    return reduce_stage(split_rows(array, count), count, 0, held)


def reduce_rest(total, count, held=()):
    for stage in range(1, len(stages(count))):
        total = reduce_stage(total, count, stage, held)
    return total


def spread(part):
    return lax.all_gather(part, "dp", axis=0, tiled=True)


def hold_all(arrays, others):
    if not others:
        return arrays
    return lax.optimization_barrier(tuple(arrays) + tuple(others))[: len(arrays)]


def hold(array, *others):
    return lax.optimization_barrier((array,) + others)[0]


def add(*parts):
    return sum(part.astype(F32) for part in parts).astype(BF16)


def segment_begin(segment):
    index = jnp.arange(segment.shape[0], dtype=jnp.int32)
    is_start = jnp.concatenate([jnp.ones((1,), dtype=bool), segment[1:] != segment[:-1]])
    return lax.cummax(jnp.where(is_start, index, jnp.zeros_like(index)), axis=0)


def rope_tables(position):
    frequency = ROPE_BASE ** (-(jnp.arange(ROT, dtype=F32) * 2.0 / HDIM))
    angles = frequency[:, None] * position.astype(F32)[None, :]
    return jnp.cos(angles), jnp.sin(angles)


def per_device(
    count,
    hidden_in,
    query_weight,
    key_weight,
    value_weight,
    output_weight,
    gate_weight,
    up_weight,
    down_weight,
    attn_gain,
    ffn_gain,
    out_grad,
    segment_ids,
):
    col, row = lax.axis_index("col"), lax.axis_index("row")
    first = col == 0

    def own_tokens(array):
        outer = jnp.concatenate([array[..., :BLOCK], array[..., 3 * BLOCK :]], axis=-1)
        inner = array[..., BLOCK : 3 * BLOCK]
        return jnp.where(first, outer, inner), jnp.where(first, inner, outer)

    def in_window(own, got):
        outer, inner = jnp.where(first, own, got), jnp.where(first, got, own)
        return jnp.concatenate([outer[:, :BLOCK], inner, outer[:, BLOCK:]], axis=1)

    w_near = jnp.concatenate(
        [query_weight[:, 0].T, key_weight[:, 0].T, value_weight[:, 0].T], axis=0
    )
    w_far = swap(w_near, "row")
    x_own, x_other = own_tokens(hidden_in.T)
    x_got = swap(x_other, "col")
    gains = jnp.stack([attn_gain, ffn_gain])
    gains_got = swap(gains, "col").astype(F32)
    gains = gains.astype(F32)
    gin_own, gmid_own = gains[0][:, None], gains[1][:, None]
    gin_got, gmid_got = gains_got[0][:, None], gains_got[1][:, None]
    segment = jnp.where(col == row, segment_ids, swap(segment_ids, "col"))
    begin, _ = own_tokens(segment_begin(segment))
    index, _ = own_tokens(jnp.arange(MAXLEN, dtype=jnp.int32))
    cosine, sine = rope_tables(index - begin)
    begin = begin[None]
    live_near = jnp.where(row == 0, LIVE[0], LIVE[1])
    where_near = jnp.stack([col, live_near]).astype(jnp.int32)
    where_far = jnp.stack([col, LIVE[0] + LIVE[1] - live_near]).astype(jnp.int32)

    w_near_got = swap(w_near, "col")
    heads = (shape((QUERY, LOCAL)), shape((2 * KEY, LOCAL)))
    nm_in, q_near, kv_near = run(
        project_near_kernel,
        (x_own, x_got, gin_own, gin_got, cosine, sine, w_near, w_near_got),
        (shape((D, LOCAL)),) + heads,
        2 * LOCAL * D * D,
    )
    kv_near_got = swap(kv_near, "col")
    wo_near = output_weight[0]
    wo_far = swap(wo_near, "row")
    wo_near_got = swap(wo_near, "col")
    att_near, lse_near = attend(where_near, begin, q_near, kv_near, kv_near_got)
    w_far_got = swap(hold(w_far, lse_near), "col")
    q_far, kv_far = run(
        project_far_kernel,
        (nm_in, cosine, sine, w_far, w_far_got),
        heads,
        2 * LOCAL * D * D,
    )
    kv_far_got = swap(kv_far, "col")
    att_far, lse_far = attend(where_far, begin, q_far, kv_far, kv_far_got, after=(wo_far,))
    wo_far_got = swap(wo_far, "col")
    og_own, og_other = own_tokens(out_grad.T)
    og = jnp.concatenate([og_own, swap(og_other, "col")], axis=0)
    og_far = swap(og, "row")
    mid, nm_a, nm_b = run(
        mid_kernel,
        (
            att_near, att_far, wo_near, wo_near_got, wo_far, wo_far_got, x_own, x_got,
            gmid_own, gmid_got,
        ),
        (shape((D, LOCAL), F32), shape((D, BLOCK)), shape((D, BLOCK))),
        2 * LOCAL * D * D,
    )

    mlp_weights = ()
    for weight in (gate_weight, up_weight, down_weight.T):
        mlp_weights += (weight, swap(weight, "col"))
    far_a, far_b = swap(nm_a, "row"), swap(nm_b, "row")
    out_part, gnm_part, act, gg, gu = feed_forward(
        (nm_a, nm_b), og, 0, mlp_weights, F32, after=(og_far,)
    )
    out_a, gnm_a, act_a, gg_a, gu_a = feed_forward(
        (far_a,), og_far, 0, mlp_weights, BF16, after=(act,)
    )
    out_b, gnm_b, act_b, gg_b, gu_b = feed_forward(
        (far_b,), og_far, 1, mlp_weights, BF16, after=(act_a,)
    )
    back_a, back_b = hold(swap(gnm_a, "row"), act_b), swap(gnm_b, "row")
    down_keep, down_send, gate_keep, gate_send, up_keep, up_send = weight_grads(
        ((og, og_far), (nm_a, nm_b, far_a, far_b)),
        ((act, act_a, act_b), (gg, gg_a, gg_b), (gu, gu_a, gu_b)),
        (0, 1, 1),
        after=(back_a,),
    )
    down_send, gate_send, up_send = hold_all((down_send, gate_send, up_send), (back_b,))

    gmid, gb, gatt_near, gatt_far, ggain_mid = run(
        mid_back_kernel,
        (
            og, mid, gnm_part, back_a, back_b, gmid_own, gmid_got, wo_near, wo_near_got, wo_far,
            wo_far_got,
        ),
        (
            shape((D, LOCAL), F32), shape((D, LOCAL)), shape((QUERY, LOCAL)),
            shape((QUERY, LOCAL)), shape((2, 16, HALF), F32),
        ),
        2 * LOCAL * D * D,
        after=(up_keep,),
    )
    down_sum = add(down_keep, hold(swap(down_send, "col"), ggain_mid))
    gate_sum = add(gate_keep, hold(swap(gate_send, "col"), ggain_mid))
    up_sum = add(up_keep, hold(swap(up_send, "col"), ggain_mid))

    dq_far, own_far, other_far = attend_back(
        where_far, begin, q_far, kv_far, kv_far_got, gatt_far, lse_far, after=(down_sum, gate_sum, up_sum)
    )
    outs = [hold(swap(hold(out, back_b), "row"), dq_far) for out in (out_a, out_b)]
    block = (mid + out_part + jnp.concatenate(outs, axis=1).astype(F32)).astype(BF16)
    down_x = reduce_first(down_sum, count, (dq_far,))

    def out_grads(att):
        send = dot(att, gb[HALF:], 1, 1).astype(BF16)
        return add(dot(att, gb[:HALF], 1, 1), hold(swap(send, "col"), dq_far))

    wo_far_sum = out_grads(att_far)
    wo_near_sum = out_grads(att_near)
    got_far = swap(other_far, "col")
    joined = shape((ROWS, HALF))
    gnm_in_part, far_keep, far_send = run(
        joined_far_kernel,
        (dq_far, own_far, got_far, cosine, sine, w_far, w_far_got, nm_in),
        (shape((D, LOCAL), F32), joined, joined),
        4 * LOCAL * D * D,
        after=(wo_far_sum, wo_near_sum, block, down_x),
        scratch=[pltpu.VMEM((D, LOCAL), BF16)],
    )
    dq_near, own_near, other_near = attend_back(
        where_near, begin, q_near, kv_near, kv_near_got, gatt_near, lse_near, after=(far_keep,)
    )
    far_sum = add(far_keep, hold(swap(far_send, "col"), dq_near))
    wo_sum = add(wo_near_sum, hold(swap(wo_far_sum, "row"), dq_near))
    gate_x = reduce_first(gate_sum, count, (dq_near,))
    down_z = reduce_rest(down_x, count, (dq_near,))
    got_near = swap(other_near, "col")
    near_keep, near_send, grad = run(
        joined_near_kernel,
        (
            dq_near, own_near, got_near, cosine, sine, w_near, w_near_got, nm_in, gnm_in_part,
            x_own, x_got, gin_own, gin_got, gmid, ggain_mid,
        ),
        (joined, joined, shape((D, LOCAL))),
        4 * LOCAL * D * D,
        after=(wo_sum, far_sum, down_z, gate_x),
        scratch=[pltpu.VMEM((D, LOCAL), BF16)],
    )
    last_sum = add(near_keep, swap(near_send, "col"), swap(far_sum, "row"))

    def feature_cols(array):
        return in_window(array[:HALF], swap(array[HALF:], "col")).T

    block_out = feature_cols(block)
    input_grad = feature_cols(grad)

    last_sum = jnp.concatenate([last_sum, wo_sum], axis=0)

    def widened(part):
        parts = spread(part).reshape(-1, HALF, LANE)
        return parts.transpose(1, 0, 2).reshape(HALF, -1).astype(F32)

    up_x = reduce_first(up_sum, count, (grad,))
    gate_z = reduce_rest(gate_x, count, (grad,))
    up_z = reduce_rest(up_x, count, (grad,))
    last_z = reduce_rest(reduce_first(last_sum, count), count)
    down_grad = widened(down_z)
    gate_grad = widened(gate_z)
    up_grad = widened(up_z)
    last = spread(last_z).astype(F32)
    gain_grads = jnp.stack([last[D], last[D + 16]])
    gain_grads = gain_grads + swap(gain_grads, "row")
    return (
        block_out,
        input_grad,
        last[:QUERY].T[:, None, :],
        last[QUERY : QUERY + KEY].T[:, None, :],
        last[QUERY + KEY : D].T[:, None, :],
        last[ROWS:][None],
        gate_grad,
        up_grad,
        down_grad.T,
        gain_grads[0],
        gain_grads[1],
    )


def solution(mesh):
    return jax.shard_map(
        functools.partial(per_device, mesh.shape["dp"]),
        mesh=mesh,
        in_specs=(
            P(("dp", "row"), "col"),
            P("col", "row", None),
            P("col", "row", None),
            P("col", "row", None),
            P("row", None, "col"),
            P("col", "row"),
            P("col", "row"),
            P("row", "col"),
            P("col"),
            P("col"),
            P(("dp", "row"), "col"),
            P(("dp", "col")),
        ),
        out_specs=(
            P(("dp", "row"), "col"),
            P(("dp", "row"), "col"),
            P("col", "row", None),
            P("col", "row", None),
            P("col", "row", None),
            P("row", None, "col"),
            P("col", "row"),
            P("col", "row"),
            P("row", "col"),
            P("col"),
            P("col"),
        ),
        check_vma=False,
    )
```

```python
import functools
import math

import jax
import jax.numpy as jnp
from jax import lax
from jax.experimental import pallas as pl
from jax.experimental.pallas import tpu as pltpu
from jax.sharding import PartitionSpec as P

D = 960
HALF = D // 2
HDIM = 64
ROT = HDIM // 2
GROUP = 3
GROUPS = 3
QUERY = GROUPS * GROUP * HDIM
KEY = GROUPS * HDIM
MAXLEN = 1024
BLOCK = MAXLEN // 4
LOCAL = 2 * BLOCK
LANE = 128
LIVE = (3, 2)
ROWS = 1024

NORM_EPS = 1e-05
ROPE_BASE = 100000.0
MASKED_SCORE = -1e30
SCALE = 1.0 / math.sqrt(HDIM)
BF16 = jnp.bfloat16
F32 = jnp.float32
VMEM_BYTES = 56 * 1024 * 1024
COST = 0.03

HELD = ((0, 3), (1, 2))
LAID = ((0, 3, 1, 2), (0, 1, 2))
SPANS = ((1, 4), (2, 3))


def dot(left, right, left_dim=1, right_dim=0):
    return lax.dot_general(
        left, right, (((left_dim,), (right_dim,)), ((), ())), preferred_element_type=F32
    )


def shape(dims, dtype=BF16):
    return jax.ShapeDtypeStruct(dims, dtype)


def whole(dims):
    return pl.BlockSpec(dims, lambda *_: (0,) * len(dims))


SMEM_SPEC = pl.BlockSpec(memory_space=pltpu.SMEM)


def run(kernel, ins, outs, flops, grid=None, in_specs=None, out_specs=None, scratch=(), after=()):
    moved = sum(a.size * a.dtype.itemsize for a in ins)
    moved += sum(math.prod(o.shape) * jnp.dtype(o.dtype).itemsize for o in outs)
    if in_specs is None:
        in_specs = [whole(a.shape) for a in ins]
    if out_specs is None:
        out_specs = [whole(o.shape) for o in outs]
    count = len(ins)

    def body(*refs):
        kernel(*refs[:count], *refs[count + len(after) :])

    return pl.pallas_call(
        body,
        grid=grid if grid is not None else (1,),
        in_specs=list(in_specs) + [pl.BlockSpec(memory_space=pl.ANY)] * len(after),
        out_specs=tuple(out_specs),
        out_shape=tuple(outs),
        scratch_shapes=list(scratch),
        compiler_params=pltpu.CompilerParams(vmem_limit_bytes=VMEM_BYTES),
        cost_estimate=pl.CostEstimate(
            flops=int(flops * COST), bytes_accessed=int(moved * COST), transcendentals=0
        ),
    )(*ins, *after)


def level_of(own, got):
    total = jnp.sum(own * own, axis=0, keepdims=True) + jnp.sum(got * got, axis=0, keepdims=True)
    return lax.rsqrt(total / D + NORM_EPS)


def project_heads(nm, cos_ref, sin_ref, own_ref, got_ref, q_ref, kv_ref):
    cosine, sine = cos_ref[...], sin_ref[...]
    joined = dot(own_ref[...], nm[:HALF]) + dot(got_ref[...], nm[HALF:])
    for at in range(0, QUERY + KEY, HDIM):
        low, high = joined[at : at + ROT], joined[at + ROT : at + HDIM]
        parts = (low * cosine - high * sine, high * cosine + low * sine)
        for part, turned in enumerate(parts):
            turned = turned.astype(BF16)
            if at < QUERY:
                turned = (turned.astype(F32) * SCALE).astype(BF16)
                q_ref[at + part * ROT : at + (part + 1) * ROT, :] = turned
            else:
                row = at - QUERY + part * ROT
                kv_ref[row : row + ROT, :] = turned
    kv_ref[KEY:, :] = joined[QUERY + KEY :].astype(BF16)


def project_near_kernel(
    xo_ref, xg_ref, go_ref, gg_ref, cos_ref, sin_ref, own_ref, got_ref, nm_ref, q_ref, kv_ref
):
    own, got = xo_ref[...].astype(F32), xg_ref[...].astype(F32)
    level = level_of(own, got)
    nm_ref[:HALF, :] = (own * level * go_ref[...]).astype(BF16)
    nm_ref[HALF:, :] = (got * level * gg_ref[...]).astype(BF16)
    project_heads(nm_ref[...], cos_ref, sin_ref, own_ref, got_ref, q_ref, kv_ref)


def project_far_kernel(nm_ref, cos_ref, sin_ref, own_ref, got_ref, q_ref, kv_ref):
    project_heads(nm_ref[...], cos_ref, sin_ref, own_ref, got_ref, q_ref, kv_ref)


def laid(core, own, got, axis):
    if core == 0:
        return jnp.concatenate([own, got], axis=axis)
    return jnp.concatenate([lax.slice_in_dim(got, 0, BLOCK, axis=axis), own], axis=axis)


def fill_bias(core, bias_ref, begin_ref):
    for at, block in enumerate(LAID[core]):
        for slot in range(2):
            cols = slice(slot * BLOCK, (slot + 1) * BLOCK)
            key = block * BLOCK + lax.broadcasted_iota(jnp.int32, (BLOCK, BLOCK), 0)
            query = HELD[core][slot] * BLOCK + lax.broadcasted_iota(jnp.int32, (BLOCK, BLOCK), 1)
            allowed = (key >= begin_ref[:, cols]) & (key <= query)
            bias_ref[at * BLOCK : (at + 1) * BLOCK, cols] = jnp.where(allowed, 0.0, MASKED_SCORE)


def attend_kernel(
    where_ref, begin_ref, q_ref, ko_ref, vo_ref, kg_ref, vg_ref, att_ref, lse_ref, bias_ref
):
    group = pl.program_id(0)
    live = group < where_ref[1]

    @pl.when(jnp.logical_not(live))
    def _():
        att_ref[...] = jnp.zeros_like(att_ref)
        lse_ref[...] = jnp.zeros_like(lse_ref)

    for core in range(2):

        @pl.when(live & (where_ref[0] == core))
        def _():
            @pl.when(group == 0)
            def _():
                fill_bias(core, bias_ref, begin_ref)

            keys = laid(core, ko_ref[...], kg_ref[...], 1).T
            values = laid(core, vo_ref[...], vg_ref[...], 1)
            for slot in range(2):
                cols = slice(slot * BLOCK, (slot + 1) * BLOCK)
                span = SPANS[core][slot] * BLOCK
                for j in range(GROUP):
                    heads = slice(j * HDIM, (j + 1) * HDIM)
                    scores = dot(keys[:span], q_ref[heads, cols]) + bias_ref[:span, cols]
                    highest = jnp.max(scores, axis=0, keepdims=True)
                    weights = jnp.exp(scores - highest)
                    total = jnp.sum(weights, axis=0, keepdims=True)
                    mixed = dot(values[:, :span], weights.astype(BF16)) / total
                    att_ref[heads, cols] = mixed.astype(BF16)
                    lse_ref[0, j : j + 1, cols] = highest + jnp.log(total)


def mid_kernel(
    near_ref, far_ref, no_ref, ng_ref, fo_ref, fg_ref, xo_ref, xg_ref, go_ref, gg_ref,
    mid_ref, nm_ref,
):
    near, far = near_ref[...], far_ref[...]
    own = xo_ref[...].astype(F32) + dot(no_ref[...], near, 0, 0) + dot(fo_ref[...], far, 0, 0)
    got = xg_ref[...].astype(F32) + dot(ng_ref[...], near, 0, 0) + dot(fg_ref[...], far, 0, 0)
    mid_ref[:HALF, :] = own
    mid_ref[HALF:, :] = got
    level = level_of(own, got)
    nm_ref[:HALF, :] = (own * level * go_ref[...]).astype(BF16)
    nm_ref[HALF:, :] = (got * level * gg_ref[...]).astype(BF16)


def mlp_kernel(
    nm_ref, og_ref, wgo_ref, wgg_ref, wuo_ref, wug_ref, wdo_ref, wdg_ref,
    out_ref, gnm_ref, act_ref, gg_ref, gu_ref, out_sum, gnm_sum,
):
    step = pl.program_id(0)
    nm, og = nm_ref[...], og_ref[...]

    def inward(own_ref, got_ref, rows):
        return dot(own_ref[...], rows[:HALF], 0, 0) + dot(got_ref[...], rows[HALF:], 0, 0)

    @pl.when(step == 0)
    def _():
        out_sum[...] = jnp.zeros_like(out_sum)
        gnm_sum[...] = jnp.zeros_like(gnm_sum)

    gate = inward(wgo_ref, wgg_ref, nm)
    up = inward(wuo_ref, wug_ref, nm)
    grad_act = inward(wdo_ref, wdg_ref, og)
    sig = jax.nn.sigmoid(gate)
    silu = gate * sig
    act = (silu * up).astype(BF16)
    grad_gate = (grad_act * up * sig * (1.0 + gate * (1.0 - sig))).astype(BF16)
    grad_up = (grad_act * silu).astype(BF16)
    act_ref[...] = act
    gg_ref[...] = grad_gate
    gu_ref[...] = grad_up
    gnm_sum[:HALF, :] += dot(wgo_ref[...], grad_gate) + dot(wuo_ref[...], grad_up)
    gnm_sum[HALF:, :] += dot(wgg_ref[...], grad_gate) + dot(wug_ref[...], grad_up)
    out_sum[:HALF, :] += dot(wdo_ref[...], act)
    out_sum[HALF:, :] += dot(wdg_ref[...], act)

    @pl.when(step == pl.num_programs(0) - 1)
    def _():
        out_ref[...] = out_sum[...].astype(out_ref.dtype)
        gnm_ref[...] = gnm_sum[...].astype(gnm_ref.dtype)


def grads_kernel(row_counts, col_counts, rows_of, *refs):
    at = 0

    def whole_tokens(count):
        nonlocal at
        at += count
        return jnp.concatenate([ref[...] for ref in refs[at - count : at]], axis=1)

    rows = [whole_tokens(count) for count in row_counts]
    for kind, count in enumerate(col_counts):
        cols = whole_tokens(count)
        for half in range(2):
            left = rows[rows_of[kind]][half * HALF : (half + 1) * HALF]
            product = dot(left, cols, 1, 1).astype(BF16)
            out_ref = refs[len(refs) - 2 * len(col_counts) + 2 * kind + half]
            out_ref[:HALF, :] = product[:, :LANE]
            out_ref[HALF:, :] = product[:, LANE:]


def gain_rows(product):
    return lax.dot_general(
        jnp.ones((16, product.shape[1]), F32), product, (((1,), (1,)), ((), ())),
        precision=lax.Precision.HIGHEST, preferred_element_type=F32,
    )


def mid_back_kernel(
    og_ref, mid_ref, part_ref, back_ref, go_ref, gg_ref, no_ref, ng_ref, fo_ref, fg_ref,
    gmid_ref, gb_ref, near_ref, far_ref, ggain_ref,
):
    own, got = mid_ref[:HALF, :], mid_ref[HALF:, :]
    level = level_of(own, got)
    gnm = part_ref[...] + back_ref[...].astype(F32)
    scaled_own, scaled_got = gnm[:HALF] * go_ref[...], gnm[HALF:] * gg_ref[...]
    inner = jnp.sum(scaled_own * own, axis=0, keepdims=True)
    inner += jnp.sum(scaled_got * got, axis=0, keepdims=True)
    pull = level**3 * inner / D
    for rows, mid, scaled in (
        (slice(0, HALF), own, scaled_own), (slice(HALF, D), got, scaled_got)
    ):
        ggain_ref[rows.start // HALF] = gain_rows(gnm[rows] * mid * level)
        gmid = og_ref[rows, :].astype(F32) + scaled * level - mid * pull
        gmid_ref[rows, :] = gmid
        gb_ref[rows, :] = gmid.astype(BF16)
    gb_own, gb_got = gb_ref[:HALF, :], gb_ref[HALF:, :]
    near_ref[...] = (dot(no_ref[...], gb_own) + dot(ng_ref[...], gb_got)).astype(BF16)
    far_ref[...] = (dot(fo_ref[...], gb_own) + dot(fg_ref[...], gb_got)).astype(BF16)


def attend_back_kernel(
    where_ref, begin_ref, q_ref, ko_ref, vo_ref, kg_ref, vg_ref, gatt_ref, lse_ref,
    dq_ref, own_ref, got_ref, bias_ref, dk_ref, dv_ref,
):
    group = pl.program_id(0)
    live = group < where_ref[1]

    @pl.when(jnp.logical_not(live))
    def _():
        dq_ref[...] = jnp.zeros_like(dq_ref)
        own_ref[...] = jnp.zeros_like(own_ref)
        got_ref[...] = jnp.zeros_like(got_ref)

    for core in range(2):

        @pl.when(live & (where_ref[0] == core))
        def _():
            @pl.when(group == 0)
            def _():
                fill_bias(core, bias_ref, begin_ref)

            keys_t = laid(core, ko_ref[...], kg_ref[...], 1)
            keys = keys_t.T
            values = laid(core, vo_ref[...], vg_ref[...], 1).T
            dk_ref[...] = jnp.zeros_like(dk_ref)
            dv_ref[...] = jnp.zeros_like(dv_ref)
            for slot in range(2):
                cols = slice(slot * BLOCK, (slot + 1) * BLOCK)
                span = SPANS[core][slot] * BLOCK
                for j in range(GROUP):
                    heads = slice(j * HDIM, (j + 1) * HDIM)
                    queries, grads = q_ref[heads, cols], gatt_ref[heads, cols]
                    scores = dot(keys[:span], queries) + bias_ref[:span, cols]
                    probs = jnp.exp(scores - lse_ref[0, j : j + 1, cols])
                    dprobs = dot(values[:span], grads)
                    inner = jnp.sum(probs * dprobs, axis=0, keepdims=True)
                    dscores = (probs * (dprobs - inner)).astype(BF16)
                    dv_ref[:span, :] += dot(probs.astype(BF16), grads.T)
                    dk_ref[:span, :] += dot(dscores, queries.T)
                    dq_ref[heads, cols] = dot(keys_t[:, :span], dscores) * SCALE
            for kind, grad_ref in enumerate((dk_ref, dv_ref)):
                if core == 0:
                    own_ref[kind, 0] = grad_ref[:LOCAL, :].T
                    got_ref[kind, 0] = grad_ref[LOCAL:, :].T.astype(BF16)
                else:
                    own_ref[kind, 0] = grad_ref[BLOCK : BLOCK + LOCAL, :].T
                    got_ref[kind, 0, :, :BLOCK] = grad_ref[:BLOCK, :].T.astype(BF16)
                    got_ref[kind, 0, :, BLOCK:] = jnp.zeros((HDIM, BLOCK), BF16)


def turn_back(cos_ref, sin_ref, dq_ref, own_ref, got_ref, gj_ref):
    cosine, sine = cos_ref[...], sin_ref[...]

    def back(at, grad):
        low, high = grad[:ROT], grad[ROT:]
        gj_ref[at : at + ROT, :] = (low * cosine + high * sine).astype(BF16)
        gj_ref[at + ROT : at + HDIM, :] = (high * cosine - low * sine).astype(BF16)

    for at in range(0, QUERY, HDIM):
        back(at, dq_ref[at : at + HDIM, :])
    for g in range(GROUPS):
        back(QUERY + g * HDIM, own_ref[0, g] + got_ref[0, g].astype(F32))
        at = QUERY + KEY + g * HDIM
        gj_ref[at : at + HDIM, :] = (own_ref[1, g] + got_ref[1, g].astype(F32)).astype(BF16)


def joined_far_kernel(
    dq_ref, own_ref, got_ref, cos_ref, sin_ref, wo_ref, wg_ref, nm_ref,
    gnm_ref, keep_ref, send_ref, gj_ref,
):
    turn_back(cos_ref, sin_ref, dq_ref, own_ref, got_ref, gj_ref)
    gj = gj_ref[...]
    for half, out_ref in enumerate((keep_ref, send_ref)):
        rows = slice(half * HALF, (half + 1) * HALF)
        out_ref[:D, :] = dot(gj, nm_ref[rows, :], 1, 1).astype(BF16)
        out_ref[D:, :] = jnp.zeros((ROWS - D, HALF), BF16)
    gnm_ref[:HALF, :] = dot(wo_ref[...], gj, 0, 0)
    gnm_ref[HALF:, :] = dot(wg_ref[...], gj, 0, 0)


def joined_near_kernel(
    dq_ref, own_ref, got_ref, cos_ref, sin_ref, wo_ref, wg_ref, nm_ref, part_ref, xo_ref, xg_ref,
    go_ref, gg_ref, gmid_ref, ggain_ref, keep_ref, send_ref, grad_ref, gj_ref,
):
    turn_back(cos_ref, sin_ref, dq_ref, own_ref, got_ref, gj_ref)
    gj = gj_ref[...]
    gnm_own = part_ref[:HALF, :] + dot(wo_ref[...], gj, 0, 0)
    gnm_got = part_ref[HALF:, :] + dot(wg_ref[...], gj, 0, 0)
    own, got = xo_ref[...].astype(F32), xg_ref[...].astype(F32)
    level = level_of(own, got)
    scaled_own, scaled_got = gnm_own * go_ref[...], gnm_got * gg_ref[...]
    inner = jnp.sum(scaled_own * own, axis=0, keepdims=True)
    inner += jnp.sum(scaled_got * got, axis=0, keepdims=True)
    pull = level**3 * inner / D
    for rows, x, gnm, scaled in (
        (slice(0, HALF), own, gnm_own, scaled_own), (slice(HALF, D), got, gnm_got, scaled_got)
    ):
        half = rows.start // HALF
        out_ref = (keep_ref, send_ref)[half]
        out_ref[:D, :] = dot(gj, nm_ref[rows, :], 1, 1).astype(BF16)
        out_ref[D : D + 16, :] = gain_rows(gnm * x * level).astype(BF16)
        out_ref[D + 16 : D + 32, :] = ggain_ref[half].astype(BF16)
        out_ref[D + 32 :, :] = jnp.zeros((ROWS - D - 32, HALF), BF16)
        grad_ref[rows, :] = (gmid_ref[rows, :] + scaled * level - x * pull).astype(BF16)


def per_group(rows, at=0):
    return pl.BlockSpec((rows, LOCAL), lambda g: (g + at, 0))


LSE_SPEC = pl.BlockSpec((1, 8, LOCAL), lambda g: (g, 0, 0))
KV_SPECS = [per_group(HDIM), per_group(HDIM, GROUPS)] * 2
PAIR_SPEC = pl.BlockSpec((2, 1, HDIM, LOCAL), lambda g: (0, g, 0, 0))


def attend(where, begin, q, kv, kv_got, after=()):
    return run(
        attend_kernel,
        (where, begin, q, kv, kv, kv_got, kv_got),
        (shape((QUERY, LOCAL)), shape((GROUPS, 8, LOCAL), F32)),
        6e9,
        grid=(GROUPS,),
        in_specs=[SMEM_SPEC, whole((1, LOCAL)), per_group(GROUP * HDIM)] + KV_SPECS,
        out_specs=(per_group(GROUP * HDIM), LSE_SPEC),
        scratch=[pltpu.VMEM((MAXLEN, LOCAL), F32)],
        after=after,
    )


def attend_back(where, begin, q, kv, kv_got, gatt, lse, after=()):
    return run(
        attend_back_kernel,
        (where, begin, q, kv, kv, kv_got, kv_got, gatt, lse),
        (
            shape((QUERY, LOCAL), F32), shape((2, GROUPS, HDIM, LOCAL), F32),
            shape((2, GROUPS, HDIM, LOCAL)),
        ),
        14e9,
        grid=(GROUPS,),
        in_specs=[SMEM_SPEC, whole((1, LOCAL)), per_group(GROUP * HDIM)]
        + KV_SPECS
        + [per_group(GROUP * HDIM), LSE_SPEC],
        out_specs=(per_group(GROUP * HDIM), PAIR_SPEC, PAIR_SPEC),
        scratch=[
            pltpu.VMEM((MAXLEN, LOCAL), F32), pltpu.VMEM((MAXLEN, HDIM), F32),
            pltpu.VMEM((MAXLEN, HDIM), F32),
        ],
        after=after,
    )


def feed_forward(nm, og, weights, dtype, after=()):
    hidden = weights[0].shape[1]
    chunk = 256
    cols = pl.BlockSpec((HALF, chunk), lambda i: (0, i))
    rows = pl.BlockSpec((chunk, LOCAL), lambda i: (i, 0))
    act = shape((hidden, LOCAL))
    return run(
        mlp_kernel,
        (nm, og) + weights,
        (shape((D, LOCAL), dtype), shape((D, LOCAL), dtype), act, act, act),
        12 * LOCAL * D * hidden,
        grid=(hidden // chunk,),
        in_specs=[whole((D, LOCAL))] * 2 + [cols] * 6,
        out_specs=(whole((D, LOCAL)), whole((D, LOCAL)), rows, rows, rows),
        scratch=[pltpu.VMEM((D, LOCAL), F32)] * 2,
        after=after,
    )


def weight_grads(rows, cols, rows_of, after=()):
    hidden = cols[0][0].shape[0]
    chunk = 2 * LANE
    all_rows, all_cols = sum(rows, ()), sum(cols, ())
    return run(
        functools.partial(
            grads_kernel, [len(pieces) for pieces in rows], [len(pieces) for pieces in cols], rows_of
        ),
        all_rows + all_cols,
        (shape((hidden // LANE * HALF, LANE)),) * (2 * len(cols)),
        4 * LOCAL * D * hidden * len(cols),
        grid=(hidden // chunk,),
        in_specs=[whole(part.shape) for part in all_rows]
        + [pl.BlockSpec((chunk, part.shape[1]), lambda i: (i, 0)) for part in all_cols],
        out_specs=(pl.BlockSpec((2 * HALF, LANE), lambda i: (i, 0)),) * (2 * len(cols)),
        after=after,
    )


def swap(array, axis):
    return lax.ppermute(array, axis, [(0, 1), (1, 0)])


def stages(count):
    found, stride = [], 1
    for size in (2,) + (4,) * 16:
        size = min(size, count // stride)
        if size < 2:
            break
        found.append((stride, size))
        stride *= size
    return found


def shift_pairs(count, stride, size, step):
    pairs = []
    for i in range(count):
        digit = i // stride % size
        pairs.append((i, i + ((digit + step) % size - digit) * stride))
    return pairs


def split_rows(array, count):
    rows, cols = array.shape
    sizes = [size for _, size in stages(count)]
    return array.reshape(*sizes[::-1], rows // count, cols)


def reduce_stage(total, count, stage, held=()):
    stride, size = stages(count)[stage]
    digit = lax.axis_index("dp") // stride % size
    axis = total.ndim - 3
    kept = lax.dynamic_index_in_dim(total, digit, axis, keepdims=False).astype(F32)
    found = []
    for step in range(1, size):
        sent = lax.dynamic_index_in_dim(total, (digit + step) % size, axis, keepdims=False)
        found.append(lax.ppermute(sent, "dp", shift_pairs(count, stride, size, step)))
    for got in hold_all(found, held):
        kept = kept + got.astype(F32)
    return kept.astype(BF16)


def reduce_first(array, count, held=()):
    return reduce_stage(split_rows(array, count), count, 0, held)


def reduce_rest(total, count, held=()):
    for stage in range(1, len(stages(count))):
        total = reduce_stage(total, count, stage, held)
    return total


def gather_stage(part, count, stage, held=()):
    stride, size = stages(count)[stage]
    digit = lax.axis_index("dp") // stride % size
    axis = part.ndim - 2
    found = [
        lax.ppermute(part, "dp", shift_pairs(count, stride, size, step)) for step in range(1, size)
    ]
    if size == 2:
        got = hold_all(found, held)[0]
        return jnp.stack(
            [jnp.where(digit == 0, part, got), jnp.where(digit == 0, got, part)], axis=axis
        )
    dims = part.shape[:axis] + (size,) + part.shape[axis:]
    whole_parts = lax.dynamic_update_index_in_dim(jnp.zeros(dims, BF16), part, digit, axis)
    for step, got in enumerate(hold_all(found, held), 1):
        whole_parts = lax.dynamic_update_index_in_dim(
            whole_parts, got, (digit - step) % size, axis
        )
    return whole_parts


def gather_rest(part, count, held=()):
    for stage in reversed(range(1, len(stages(count)))):
        part = gather_stage(part, count, stage, held)
    return part


def gather_first(part, count, held=()):
    return gather_stage(part, count, 0, held)


def spread(part):
    return lax.all_gather(part, "dp", axis=0, tiled=True)


def hold_all(arrays, others):
    if not others:
        return arrays
    return lax.optimization_barrier(tuple(arrays) + tuple(others))[: len(arrays)]


def hold(array, *others):
    return lax.optimization_barrier((array,) + others)[0]


def add(*parts):
    return sum(part.astype(F32) for part in parts).astype(BF16)


def segment_begin(segment):
    index = jnp.arange(segment.shape[0], dtype=jnp.int32)
    is_start = jnp.concatenate([jnp.ones((1,), dtype=bool), segment[1:] != segment[:-1]])
    return lax.cummax(jnp.where(is_start, index, jnp.zeros_like(index)), axis=0)


def rope_tables(position):
    frequency = ROPE_BASE ** (-(jnp.arange(ROT, dtype=F32) * 2.0 / HDIM))
    angles = frequency[:, None] * position.astype(F32)[None, :]
    return jnp.cos(angles), jnp.sin(angles)


def per_device(
    count,
    hidden_in,
    query_weight,
    key_weight,
    value_weight,
    output_weight,
    gate_weight,
    up_weight,
    down_weight,
    attn_gain,
    ffn_gain,
    out_grad,
    segment_ids,
):
    col, row = lax.axis_index("col"), lax.axis_index("row")
    first = col == 0

    def own_tokens(array):
        outer = jnp.concatenate([array[..., :BLOCK], array[..., 3 * BLOCK :]], axis=-1)
        inner = array[..., BLOCK : 3 * BLOCK]
        return jnp.where(first, outer, inner), jnp.where(first, inner, outer)

    def in_window(own, got):
        outer, inner = jnp.where(first, own, got), jnp.where(first, got, own)
        return jnp.concatenate([outer[:, :BLOCK], inner, outer[:, BLOCK:]], axis=1)

    w_near = jnp.concatenate(
        [query_weight[:, 0].T, key_weight[:, 0].T, value_weight[:, 0].T], axis=0
    )
    w_far = swap(w_near, "row")
    x_own, x_other = own_tokens(hidden_in.T)
    x_got = swap(x_other, "col")
    gains = jnp.stack([attn_gain, ffn_gain])
    gains_got = swap(gains, "col").astype(F32)
    gains = gains.astype(F32)
    gin_own, gmid_own = gains[0][:, None], gains[1][:, None]
    gin_got, gmid_got = gains_got[0][:, None], gains_got[1][:, None]
    segment = jnp.where(col == row, segment_ids, swap(segment_ids, "col"))
    begin, _ = own_tokens(segment_begin(segment))
    index, _ = own_tokens(jnp.arange(MAXLEN, dtype=jnp.int32))
    cosine, sine = rope_tables(index - begin)
    begin = begin[None]
    live_near = jnp.where(row == 0, LIVE[0], LIVE[1])
    where_near = jnp.stack([col, live_near]).astype(jnp.int32)
    where_far = jnp.stack([col, LIVE[0] + LIVE[1] - live_near]).astype(jnp.int32)

    w_near_got = swap(w_near, "col")
    heads = (shape((QUERY, LOCAL)), shape((2 * KEY, LOCAL)))
    nm_in, q_near, kv_near = run(
        project_near_kernel,
        (x_own, x_got, gin_own, gin_got, cosine, sine, w_near, w_near_got),
        (shape((D, LOCAL)),) + heads,
        2 * LOCAL * D * D,
    )
    kv_near_got = swap(kv_near, "col")
    wo_near = output_weight[0]
    wo_far = swap(wo_near, "row")
    wo_near_got = swap(wo_near, "col")
    att_near, lse_near = attend(where_near, begin, q_near, kv_near, kv_near_got)
    w_far_got = swap(hold(w_far, lse_near), "col")
    q_far, kv_far = run(
        project_far_kernel,
        (nm_in, cosine, sine, w_far, w_far_got),
        heads,
        2 * LOCAL * D * D,
    )
    kv_far_got = swap(kv_far, "col")
    att_far, lse_far = attend(where_far, begin, q_far, kv_far, kv_far_got, after=(wo_far,))
    wo_far_got = swap(wo_far, "col")
    og_own, og_other = own_tokens(out_grad.T)
    og = jnp.concatenate([og_own, swap(og_other, "col")], axis=0)
    og_far = swap(og, "row")
    mid, nm = run(
        mid_kernel,
        (
            att_near, att_far, wo_near, wo_near_got, wo_far, wo_far_got, x_own, x_got,
            gmid_own, gmid_got,
        ),
        (shape((D, LOCAL), F32), shape((D, LOCAL))),
        2 * LOCAL * D * D,
    )

    mlp_weights = ()
    for weight in (gate_weight, up_weight, down_weight.T):
        mlp_weights += (weight, swap(weight, "col"))
    nm_far = swap(nm, "row")
    out_part, gnm_part, act, gg, gu = feed_forward(nm, og, mlp_weights, F32, after=(og_far,))
    out_send, gnm_send, act_far, gg_far, gu_far = feed_forward(
        nm_far, og_far, mlp_weights, BF16, after=(act,)
    )
    gnm_back = swap(gnm_send, "row")
    down_keep, down_send, gate_keep, gate_send, up_keep, up_send = weight_grads(
        ((og, og_far), (nm, nm_far)), ((act, act_far), (gg, gg_far), (gu, gu_far)), (0, 1, 1)
    )
    down_send, gate_send, up_send = hold_all((down_send, gate_send, up_send), (gnm_back,))

    gmid, gb, gatt_near, gatt_far, ggain_mid = run(
        mid_back_kernel,
        (
            og, mid, gnm_part, gnm_back, gmid_own, gmid_got, wo_near, wo_near_got, wo_far,
            wo_far_got,
        ),
        (
            shape((D, LOCAL), F32), shape((D, LOCAL)), shape((QUERY, LOCAL)),
            shape((QUERY, LOCAL)), shape((2, 16, HALF), F32),
        ),
        2 * LOCAL * D * D,
        after=(up_keep,),
    )
    down_sum = add(down_keep, hold(swap(down_send, "col"), ggain_mid))
    gate_sum = add(gate_keep, hold(swap(gate_send, "col"), ggain_mid))
    up_sum = add(up_keep, hold(swap(up_send, "col"), ggain_mid))

    dq_far, own_far, other_far = attend_back(
        where_far, begin, q_far, kv_far, kv_far_got, gatt_far, lse_far, after=(down_sum, gate_sum, up_sum)
    )
    out_back = hold(swap(hold(out_send, gnm_back), "row"), dq_far)
    block = (mid + out_part + out_back.astype(F32)).astype(BF16)
    down_x = reduce_first(down_sum, count, (dq_far,))

    def out_grads(att):
        send = dot(att, gb[HALF:], 1, 1).astype(BF16)
        return add(dot(att, gb[:HALF], 1, 1), hold(swap(send, "col"), dq_far))

    wo_far_sum = out_grads(att_far)
    wo_near_sum = out_grads(att_near)
    got_far = swap(hold(other_far, down_x), "col")
    joined = shape((ROWS, HALF))
    gnm_in_part, far_keep, far_send = run(
        joined_far_kernel,
        (dq_far, own_far, got_far, cosine, sine, w_far, w_far_got, nm_in),
        (shape((D, LOCAL), F32), joined, joined),
        4 * LOCAL * D * D,
        after=(wo_far_sum, wo_near_sum, block, down_x),
        scratch=[pltpu.VMEM((D, LOCAL), BF16)],
    )
    gate_x = reduce_first(gate_sum, count, (far_keep,))
    dq_near, own_near, other_near = attend_back(
        where_near, begin, q_near, kv_near, kv_near_got, gatt_near, lse_near, after=(gate_x,)
    )
    far_sum = add(far_keep, hold(swap(far_send, "col"), dq_near))
    wo_sum = add(wo_near_sum, hold(swap(wo_far_sum, "row"), dq_near))
    down_z = reduce_rest(down_x, count, (dq_near,))
    up_x = reduce_first(hold(up_sum, gate_x), count, (dq_near,))
    got_near = swap(hold(other_near, up_x, down_z, far_sum, wo_sum), "col")
    near_keep, near_send, grad = run(
        joined_near_kernel,
        (
            dq_near, own_near, got_near, cosine, sine, w_near, w_near_got, nm_in, gnm_in_part,
            x_own, x_got, gin_own, gin_got, gmid, ggain_mid,
        ),
        (joined, joined, shape((D, LOCAL))),
        4 * LOCAL * D * D,
        after=(wo_sum, far_sum, down_z, up_x),
        scratch=[pltpu.VMEM((D, LOCAL), BF16)],
    )
    gate_z = reduce_rest(gate_x, count, (grad,))
    near_send = hold(near_send, gate_z)
    last_sum = add(near_keep, swap(near_send, "col"), swap(far_sum, "row"))

    def feature_cols(array):
        return in_window(array[:HALF], swap(array[HALF:], "col")).T

    block_out = feature_cols(block)
    input_grad = feature_cols(grad)


    def widened(whole_sum):
        parts = whole_sum.reshape(-1, HALF, LANE)
        return parts.transpose(1, 0, 2).reshape(HALF, -1).astype(F32)

    up_z = reduce_rest(up_x, count, (grad,))
    down_grad = widened(spread(down_z))
    gate_grad = widened(spread(gate_z))
    up_rest = gather_rest(up_z, count, (last_sum,))
    out_x = reduce_first(wo_sum, count, (grad,))
    last_x = reduce_first(last_sum, count)
    up_grad = widened(gather_first(up_rest, count).reshape(up_sum.shape))
    last_z = reduce_rest(jnp.concatenate([last_x, out_x], axis=-2), count)
    last = gather_first(gather_rest(last_z, count), count)
    last, out_weight_grad = last[..., : ROWS // count, :], last[..., ROWS // count :, :]
    last = last.reshape(last_sum.shape).astype(F32)
    out_weight_grad = out_weight_grad.reshape(wo_sum.shape).astype(F32)
    gain_grads = jnp.stack([last[D], last[D + 16]])
    gain_grads = gain_grads + swap(gain_grads, "row")
    return (
        block_out,
        input_grad,
        last[:QUERY].T[:, None, :],
        last[QUERY : QUERY + KEY].T[:, None, :],
        last[QUERY + KEY : D].T[:, None, :],
        out_weight_grad[None],
        gate_grad,
        up_grad,
        down_grad.T,
        gain_grads[0],
        gain_grads[1],
    )


def solution(mesh):
    return jax.shard_map(
        functools.partial(per_device, mesh.shape["dp"]),
        mesh=mesh,
        in_specs=(
            P(("dp", "row"), "col"),
            P("col", "row", None),
            P("col", "row", None),
            P("col", "row", None),
            P("row", None, "col"),
            P("col", "row"),
            P("col", "row"),
            P("row", "col"),
            P("col"),
            P("col"),
            P(("dp", "row"), "col"),
            P(("dp", "col")),
        ),
        out_specs=(
            P(("dp", "row"), "col"),
            P(("dp", "row"), "col"),
            P("col", "row", None),
            P("col", "row", None),
            P("col", "row", None),
            P("row", None, "col"),
            P("col", "row"),
            P("col", "row"),
            P("row", "col"),
            P("col"),
            P("col"),
        ),
        check_vma=False,
    )
```

```python
import functools
import math

import jax
import jax.numpy as jnp
from jax import lax
from jax.experimental import pallas as pl
from jax.experimental.pallas import tpu as pltpu
from jax.sharding import PartitionSpec as P

D = 960
HALF = D // 2
HDIM = 64
ROT = HDIM // 2
GROUP = 3
GROUPS = 3
QUERY = GROUPS * GROUP * HDIM
KEY = GROUPS * HDIM
MAXLEN = 1024
BLOCK = MAXLEN // 4
LOCAL = 2 * BLOCK
LANE = 128
LIVE = (3, 2)
ROWS = 1024

NORM_EPS = 1e-05
ROPE_BASE = 100000.0
MASKED_SCORE = -1e30
SCALE = 1.0 / math.sqrt(HDIM)
BF16 = jnp.bfloat16
F32 = jnp.float32
VMEM_BYTES = 56 * 1024 * 1024
COST = 0.03

HELD = ((0, 3), (1, 2))
LAID = ((0, 3, 1, 2), (0, 1, 2))
SPANS = ((1, 4), (2, 3))


def dot(left, right, left_dim=1, right_dim=0):
    return lax.dot_general(
        left, right, (((left_dim,), (right_dim,)), ((), ())), preferred_element_type=F32
    )


def shape(dims, dtype=BF16):
    return jax.ShapeDtypeStruct(dims, dtype)


def whole(dims):
    return pl.BlockSpec(dims, lambda *_: (0,) * len(dims))


SMEM_SPEC = pl.BlockSpec(memory_space=pltpu.SMEM)


def run(kernel, ins, outs, flops, grid=None, in_specs=None, out_specs=None, scratch=(), after=()):
    moved = sum(a.size * a.dtype.itemsize for a in ins)
    moved += sum(math.prod(o.shape) * jnp.dtype(o.dtype).itemsize for o in outs)
    if in_specs is None:
        in_specs = [whole(a.shape) for a in ins]
    if out_specs is None:
        out_specs = [whole(o.shape) for o in outs]
    count = len(ins)

    def body(*refs):
        kernel(*refs[:count], *refs[count + len(after) :])

    return pl.pallas_call(
        body,
        grid=grid if grid is not None else (1,),
        in_specs=list(in_specs) + [pl.BlockSpec(memory_space=pl.ANY)] * len(after),
        out_specs=tuple(out_specs),
        out_shape=tuple(outs),
        scratch_shapes=list(scratch),
        compiler_params=pltpu.CompilerParams(vmem_limit_bytes=VMEM_BYTES),
        cost_estimate=pl.CostEstimate(
            flops=int(flops * COST), bytes_accessed=int(moved * COST), transcendentals=0
        ),
    )(*ins, *after)


def level_of(own, got):
    total = jnp.sum(own * own, axis=0, keepdims=True) + jnp.sum(got * got, axis=0, keepdims=True)
    return lax.rsqrt(total / D + NORM_EPS)


def project_heads(nm, cos_ref, sin_ref, own_ref, got_ref, q_ref, kv_ref):
    cosine, sine = cos_ref[...], sin_ref[...]
    joined = dot(own_ref[...], nm[:HALF]) + dot(got_ref[...], nm[HALF:])
    for at in range(0, QUERY + KEY, HDIM):
        low, high = joined[at : at + ROT], joined[at + ROT : at + HDIM]
        parts = (low * cosine - high * sine, high * cosine + low * sine)
        for part, turned in enumerate(parts):
            turned = turned.astype(BF16)
            if at < QUERY:
                turned = (turned.astype(F32) * SCALE).astype(BF16)
                q_ref[at + part * ROT : at + (part + 1) * ROT, :] = turned
            else:
                row = at - QUERY + part * ROT
                kv_ref[row : row + ROT, :] = turned
    kv_ref[KEY:, :] = joined[QUERY + KEY :].astype(BF16)


def project_near_kernel(
    xo_ref, xg_ref, go_ref, gg_ref, cos_ref, sin_ref, own_ref, got_ref, nm_ref, q_ref, kv_ref
):
    own, got = xo_ref[...].astype(F32), xg_ref[...].astype(F32)
    level = level_of(own, got)
    nm_ref[:HALF, :] = (own * level * go_ref[...]).astype(BF16)
    nm_ref[HALF:, :] = (got * level * gg_ref[...]).astype(BF16)
    project_heads(nm_ref[...], cos_ref, sin_ref, own_ref, got_ref, q_ref, kv_ref)


def project_far_kernel(nm_ref, cos_ref, sin_ref, own_ref, got_ref, q_ref, kv_ref):
    project_heads(nm_ref[...], cos_ref, sin_ref, own_ref, got_ref, q_ref, kv_ref)


def laid(core, own, got, axis):
    if core == 0:
        return jnp.concatenate([own, got], axis=axis)
    return jnp.concatenate([lax.slice_in_dim(got, 0, BLOCK, axis=axis), own], axis=axis)


def fill_bias(core, bias_ref, begin_ref):
    for at, block in enumerate(LAID[core]):
        for slot in range(2):
            cols = slice(slot * BLOCK, (slot + 1) * BLOCK)
            key = block * BLOCK + lax.broadcasted_iota(jnp.int32, (BLOCK, BLOCK), 0)
            query = HELD[core][slot] * BLOCK + lax.broadcasted_iota(jnp.int32, (BLOCK, BLOCK), 1)
            allowed = (key >= begin_ref[:, cols]) & (key <= query)
            bias_ref[at * BLOCK : (at + 1) * BLOCK, cols] = jnp.where(allowed, 0.0, MASKED_SCORE)


def attend_kernel(
    where_ref, begin_ref, q_ref, ko_ref, vo_ref, kg_ref, vg_ref, att_ref, lse_ref, bias_ref
):
    group = pl.program_id(0)
    live = group < where_ref[1]

    @pl.when(jnp.logical_not(live))
    def _():
        att_ref[...] = jnp.zeros_like(att_ref)
        lse_ref[...] = jnp.zeros_like(lse_ref)

    for core in range(2):

        @pl.when(live & (where_ref[0] == core))
        def _():
            @pl.when(group == 0)
            def _():
                fill_bias(core, bias_ref, begin_ref)

            keys = laid(core, ko_ref[...], kg_ref[...], 1).T
            values = laid(core, vo_ref[...], vg_ref[...], 1)
            for slot in range(2):
                cols = slice(slot * BLOCK, (slot + 1) * BLOCK)
                span = SPANS[core][slot] * BLOCK
                for j in range(GROUP):
                    heads = slice(j * HDIM, (j + 1) * HDIM)
                    scores = dot(keys[:span], q_ref[heads, cols]) + bias_ref[:span, cols]
                    highest = jnp.max(scores, axis=0, keepdims=True)
                    weights = jnp.exp(scores - highest)
                    total = jnp.sum(weights, axis=0, keepdims=True)
                    mixed = dot(values[:, :span], weights.astype(BF16)) / total
                    att_ref[heads, cols] = mixed.astype(BF16)
                    lse_ref[0, j : j + 1, cols] = highest + jnp.log(total)


def mid_kernel(
    near_ref, far_ref, no_ref, ng_ref, fo_ref, fg_ref, xo_ref, xg_ref, go_ref, gg_ref,
    mid_ref, nm_ref,
):
    near, far = near_ref[...], far_ref[...]
    own = xo_ref[...].astype(F32) + dot(no_ref[...], near, 0, 0) + dot(fo_ref[...], far, 0, 0)
    got = xg_ref[...].astype(F32) + dot(ng_ref[...], near, 0, 0) + dot(fg_ref[...], far, 0, 0)
    mid_ref[:HALF, :] = own
    mid_ref[HALF:, :] = got
    level = level_of(own, got)
    nm_ref[:HALF, :] = (own * level * go_ref[...]).astype(BF16)
    nm_ref[HALF:, :] = (got * level * gg_ref[...]).astype(BF16)


def mlp_kernel(
    nm_ref, og_ref, wgo_ref, wgg_ref, wuo_ref, wug_ref, wdo_ref, wdg_ref,
    out_ref, gnm_ref, act_ref, gg_ref, gu_ref, out_sum, gnm_sum,
):
    step = pl.program_id(0)
    nm, og = nm_ref[...], og_ref[...]

    def inward(own_ref, got_ref, rows):
        return dot(own_ref[...], rows[:HALF], 0, 0) + dot(got_ref[...], rows[HALF:], 0, 0)

    @pl.when(step == 0)
    def _():
        out_sum[...] = jnp.zeros_like(out_sum)
        gnm_sum[...] = jnp.zeros_like(gnm_sum)

    gate = inward(wgo_ref, wgg_ref, nm)
    up = inward(wuo_ref, wug_ref, nm)
    grad_act = inward(wdo_ref, wdg_ref, og)
    sig = jax.nn.sigmoid(gate)
    silu = gate * sig
    act = (silu * up).astype(BF16)
    grad_gate = (grad_act * up * sig * (1.0 + gate * (1.0 - sig))).astype(BF16)
    grad_up = (grad_act * silu).astype(BF16)
    act_ref[...] = act
    gg_ref[...] = grad_gate
    gu_ref[...] = grad_up
    gnm_sum[:HALF, :] += dot(wgo_ref[...], grad_gate) + dot(wuo_ref[...], grad_up)
    gnm_sum[HALF:, :] += dot(wgg_ref[...], grad_gate) + dot(wug_ref[...], grad_up)
    out_sum[:HALF, :] += dot(wdo_ref[...], act)
    out_sum[HALF:, :] += dot(wdg_ref[...], act)

    @pl.when(step == pl.num_programs(0) - 1)
    def _():
        out_ref[...] = out_sum[...].astype(out_ref.dtype)
        gnm_ref[...] = gnm_sum[...].astype(gnm_ref.dtype)


def mlp_far_kernel(*refs):
    og_far_ref, og_ref, act_own_ref, act_ref = refs[1], refs[8], refs[9], refs[12]
    mlp_kernel(*refs[:8], *refs[10:15], *refs[17:])
    for half in range(2):
        rows = slice(half * HALF, (half + 1) * HALF)
        product = dot(og_ref[rows, :], act_own_ref[...], 1, 1)
        product = (product + dot(og_far_ref[rows, :], act_ref[...], 1, 1)).astype(BF16)
        refs[15 + half][:HALF, :] = product[:, :LANE]
        refs[15 + half][HALF:, :] = product[:, LANE:]


def grads_kernel(row_counts, col_counts, rows_of, *refs):
    at = 0

    def whole_tokens(count):
        nonlocal at
        at += count
        return jnp.concatenate([ref[...] for ref in refs[at - count : at]], axis=1)

    rows = [whole_tokens(count) for count in row_counts]
    for kind, count in enumerate(col_counts):
        cols = whole_tokens(count)
        for half in range(2):
            left = rows[rows_of[kind]][half * HALF : (half + 1) * HALF]
            product = dot(left, cols, 1, 1).astype(BF16)
            out_ref = refs[len(refs) - 2 * len(col_counts) + 2 * kind + half]
            out_ref[:HALF, :] = product[:, :LANE]
            out_ref[HALF:, :] = product[:, LANE:]


def gain_rows(product):
    return lax.dot_general(
        jnp.ones((16, product.shape[1]), F32), product, (((1,), (1,)), ((), ())),
        precision=lax.Precision.HIGHEST, preferred_element_type=F32,
    )


def mid_back_kernel(
    og_ref, mid_ref, part_ref, back_ref, go_ref, gg_ref, no_ref, ng_ref, fo_ref, fg_ref,
    gmid_ref, gb_ref, near_ref, far_ref, ggain_ref,
):
    own, got = mid_ref[:HALF, :], mid_ref[HALF:, :]
    level = level_of(own, got)
    gnm = part_ref[...] + back_ref[...].astype(F32)
    scaled_own, scaled_got = gnm[:HALF] * go_ref[...], gnm[HALF:] * gg_ref[...]
    inner = jnp.sum(scaled_own * own, axis=0, keepdims=True)
    inner += jnp.sum(scaled_got * got, axis=0, keepdims=True)
    pull = level**3 * inner / D
    for rows, mid, scaled in (
        (slice(0, HALF), own, scaled_own), (slice(HALF, D), got, scaled_got)
    ):
        ggain_ref[rows.start // HALF] = gain_rows(gnm[rows] * mid * level)
        gmid = og_ref[rows, :].astype(F32) + scaled * level - mid * pull
        gmid_ref[rows, :] = gmid
        gb_ref[rows, :] = gmid.astype(BF16)
    gb_own, gb_got = gb_ref[:HALF, :], gb_ref[HALF:, :]
    near_ref[...] = (dot(no_ref[...], gb_own) + dot(ng_ref[...], gb_got)).astype(BF16)
    far_ref[...] = (dot(fo_ref[...], gb_own) + dot(fg_ref[...], gb_got)).astype(BF16)


def attend_back_kernel(
    where_ref, begin_ref, q_ref, ko_ref, vo_ref, kg_ref, vg_ref, gatt_ref, lse_ref,
    dq_ref, own_ref, got_ref, bias_ref, dk_ref, dv_ref,
):
    group = pl.program_id(0)
    live = group < where_ref[1]

    @pl.when(jnp.logical_not(live))
    def _():
        dq_ref[...] = jnp.zeros_like(dq_ref)
        own_ref[...] = jnp.zeros_like(own_ref)
        got_ref[...] = jnp.zeros_like(got_ref)

    for core in range(2):

        @pl.when(live & (where_ref[0] == core))
        def _():
            @pl.when(group == 0)
            def _():
                fill_bias(core, bias_ref, begin_ref)

            keys_t = laid(core, ko_ref[...], kg_ref[...], 1)
            keys = keys_t.T
            values = laid(core, vo_ref[...], vg_ref[...], 1).T
            dk_ref[...] = jnp.zeros_like(dk_ref)
            dv_ref[...] = jnp.zeros_like(dv_ref)
            for slot in range(2):
                cols = slice(slot * BLOCK, (slot + 1) * BLOCK)
                span = SPANS[core][slot] * BLOCK
                for j in range(GROUP):
                    heads = slice(j * HDIM, (j + 1) * HDIM)
                    queries, grads = q_ref[heads, cols], gatt_ref[heads, cols]
                    scores = dot(keys[:span], queries) + bias_ref[:span, cols]
                    probs = jnp.exp(scores - lse_ref[0, j : j + 1, cols])
                    dprobs = dot(values[:span], grads)
                    inner = jnp.sum(probs * dprobs, axis=0, keepdims=True)
                    dscores = (probs * (dprobs - inner)).astype(BF16)
                    dv_ref[:span, :] += dot(probs.astype(BF16), grads.T)
                    dk_ref[:span, :] += dot(dscores, queries.T)
                    dq_ref[heads, cols] = dot(keys_t[:, :span], dscores) * SCALE
            for kind, grad_ref in enumerate((dk_ref, dv_ref)):
                if core == 0:
                    own_ref[kind, 0] = grad_ref[:LOCAL, :].T
                    got_ref[kind, 0] = grad_ref[LOCAL:, :].T.astype(BF16)
                else:
                    own_ref[kind, 0] = grad_ref[BLOCK : BLOCK + LOCAL, :].T
                    got_ref[kind, 0, :, :BLOCK] = grad_ref[:BLOCK, :].T.astype(BF16)
                    got_ref[kind, 0, :, BLOCK:] = jnp.zeros((HDIM, BLOCK), BF16)


def turn_back(cos_ref, sin_ref, dq_ref, own_ref, got_ref, gj_ref):
    cosine, sine = cos_ref[...], sin_ref[...]

    def back(at, grad):
        low, high = grad[:ROT], grad[ROT:]
        gj_ref[at : at + ROT, :] = (low * cosine + high * sine).astype(BF16)
        gj_ref[at + ROT : at + HDIM, :] = (high * cosine - low * sine).astype(BF16)

    for at in range(0, QUERY, HDIM):
        back(at, dq_ref[at : at + HDIM, :])
    for g in range(GROUPS):
        back(QUERY + g * HDIM, own_ref[0, g] + got_ref[0, g].astype(F32))
        at = QUERY + KEY + g * HDIM
        gj_ref[at : at + HDIM, :] = (own_ref[1, g] + got_ref[1, g].astype(F32)).astype(BF16)


def joined_far_kernel(
    dq_ref, own_ref, got_ref, cos_ref, sin_ref, wo_ref, wg_ref, nm_ref,
    gnm_ref, keep_ref, send_ref, gj_ref,
):
    turn_back(cos_ref, sin_ref, dq_ref, own_ref, got_ref, gj_ref)
    gj = gj_ref[...]
    for half, out_ref in enumerate((keep_ref, send_ref)):
        rows = slice(half * HALF, (half + 1) * HALF)
        out_ref[:D, :] = dot(gj, nm_ref[rows, :], 1, 1).astype(BF16)
        out_ref[D:, :] = jnp.zeros((ROWS - D, HALF), BF16)
    gnm_ref[:HALF, :] = dot(wo_ref[...], gj, 0, 0)
    gnm_ref[HALF:, :] = dot(wg_ref[...], gj, 0, 0)


def joined_near_kernel(
    dq_ref, own_ref, got_ref, cos_ref, sin_ref, wo_ref, wg_ref, nm_ref, part_ref, xo_ref, xg_ref,
    go_ref, gg_ref, gmid_ref, ggain_ref, keep_ref, send_ref, grad_ref, gj_ref,
):
    turn_back(cos_ref, sin_ref, dq_ref, own_ref, got_ref, gj_ref)
    gj = gj_ref[...]
    gnm_own = part_ref[:HALF, :] + dot(wo_ref[...], gj, 0, 0)
    gnm_got = part_ref[HALF:, :] + dot(wg_ref[...], gj, 0, 0)
    own, got = xo_ref[...].astype(F32), xg_ref[...].astype(F32)
    level = level_of(own, got)
    scaled_own, scaled_got = gnm_own * go_ref[...], gnm_got * gg_ref[...]
    inner = jnp.sum(scaled_own * own, axis=0, keepdims=True)
    inner += jnp.sum(scaled_got * got, axis=0, keepdims=True)
    pull = level**3 * inner / D
    for rows, x, gnm, scaled in (
        (slice(0, HALF), own, gnm_own, scaled_own), (slice(HALF, D), got, gnm_got, scaled_got)
    ):
        half = rows.start // HALF
        out_ref = (keep_ref, send_ref)[half]
        out_ref[:D, :] = dot(gj, nm_ref[rows, :], 1, 1).astype(BF16)
        out_ref[D : D + 16, :] = gain_rows(gnm * x * level).astype(BF16)
        out_ref[D + 16 : D + 32, :] = ggain_ref[half].astype(BF16)
        out_ref[D + 32 :, :] = jnp.zeros((ROWS - D - 32, HALF), BF16)
        grad_ref[rows, :] = (gmid_ref[rows, :] + scaled * level - x * pull).astype(BF16)


def per_group(rows, at=0):
    return pl.BlockSpec((rows, LOCAL), lambda g: (g + at, 0))


LSE_SPEC = pl.BlockSpec((1, 8, LOCAL), lambda g: (g, 0, 0))
KV_SPECS = [per_group(HDIM), per_group(HDIM, GROUPS)] * 2
PAIR_SPEC = pl.BlockSpec((2, 1, HDIM, LOCAL), lambda g: (0, g, 0, 0))


def attend(where, begin, q, kv, kv_got, after=()):
    return run(
        attend_kernel,
        (where, begin, q, kv, kv, kv_got, kv_got),
        (shape((QUERY, LOCAL)), shape((GROUPS, 8, LOCAL), F32)),
        6e9,
        grid=(GROUPS,),
        in_specs=[SMEM_SPEC, whole((1, LOCAL)), per_group(GROUP * HDIM)] + KV_SPECS,
        out_specs=(per_group(GROUP * HDIM), LSE_SPEC),
        scratch=[pltpu.VMEM((MAXLEN, LOCAL), F32)],
        after=after,
    )


def attend_back(where, begin, q, kv, kv_got, gatt, lse, after=()):
    return run(
        attend_back_kernel,
        (where, begin, q, kv, kv, kv_got, kv_got, gatt, lse),
        (
            shape((QUERY, LOCAL), F32), shape((2, GROUPS, HDIM, LOCAL), F32),
            shape((2, GROUPS, HDIM, LOCAL)),
        ),
        14e9,
        grid=(GROUPS,),
        in_specs=[SMEM_SPEC, whole((1, LOCAL)), per_group(GROUP * HDIM)]
        + KV_SPECS
        + [per_group(GROUP * HDIM), LSE_SPEC],
        out_specs=(per_group(GROUP * HDIM), PAIR_SPEC, PAIR_SPEC),
        scratch=[
            pltpu.VMEM((MAXLEN, LOCAL), F32), pltpu.VMEM((MAXLEN, HDIM), F32),
            pltpu.VMEM((MAXLEN, HDIM), F32),
        ],
        after=after,
    )


def feed_forward(nm, og, weights, dtype, own=(), after=()):
    hidden = weights[0].shape[1]
    chunk = 2 * LANE
    cols = pl.BlockSpec((HALF, chunk), lambda i: (0, i))
    rows = pl.BlockSpec((chunk, LOCAL), lambda i: (i, 0))
    grads = pl.BlockSpec((2 * HALF, LANE), lambda i: (i, 0))
    act = shape((hidden, LOCAL))
    outs = (shape((D, LOCAL), dtype), shape((D, LOCAL), dtype), act, act, act)
    in_specs = [whole((D, LOCAL))] * 2 + [cols] * 6
    out_specs = (whole((D, LOCAL)), whole((D, LOCAL)), rows, rows, rows)
    if own:
        outs += (shape((hidden // LANE * HALF, LANE)),) * 2
        in_specs += [whole((D, LOCAL)), rows]
        out_specs += (grads, grads)
    return run(
        mlp_far_kernel if own else mlp_kernel,
        (nm, og) + weights + own,
        outs,
        12 * LOCAL * D * hidden,
        grid=(hidden // chunk,),
        in_specs=in_specs,
        out_specs=out_specs,
        scratch=[pltpu.VMEM((D, LOCAL), F32)] * 2,
        after=after,
    )


def weight_grads(rows, cols, rows_of, after=()):
    hidden = cols[0][0].shape[0]
    chunk = 2 * LANE
    all_rows, all_cols = sum(rows, ()), sum(cols, ())
    return run(
        functools.partial(
            grads_kernel, [len(pieces) for pieces in rows], [len(pieces) for pieces in cols], rows_of
        ),
        all_rows + all_cols,
        (shape((hidden // LANE * HALF, LANE)),) * (2 * len(cols)),
        4 * LOCAL * D * hidden * len(cols),
        grid=(hidden // chunk,),
        in_specs=[whole(part.shape) for part in all_rows]
        + [pl.BlockSpec((chunk, part.shape[1]), lambda i: (i, 0)) for part in all_cols],
        out_specs=(pl.BlockSpec((2 * HALF, LANE), lambda i: (i, 0)),) * (2 * len(cols)),
        after=after,
    )


def swap(array, axis):
    return lax.ppermute(array, axis, [(0, 1), (1, 0)])


def stages(count):
    found, stride = [], 1
    for size in (2,) + (4,) * 16:
        size = min(size, count // stride)
        if size < 2:
            break
        found.append((stride, size))
        stride *= size
    return found


def shift_pairs(count, stride, size, step):
    pairs = []
    for i in range(count):
        digit = i // stride % size
        pairs.append((i, i + ((digit + step) % size - digit) * stride))
    return pairs


def split_rows(array, count):
    rows, cols = array.shape
    sizes = [size for _, size in stages(count)]
    return array.reshape(*sizes[::-1], rows // count, cols)


def reduce_stage(total, count, stage, held=()):
    stride, size = stages(count)[stage]
    digit = lax.axis_index("dp") // stride % size
    axis = total.ndim - 3
    kept = lax.dynamic_index_in_dim(total, digit, axis, keepdims=False).astype(F32)
    found = []
    for step in range(1, size):
        sent = lax.dynamic_index_in_dim(total, (digit + step) % size, axis, keepdims=False)
        found.append(lax.ppermute(sent, "dp", shift_pairs(count, stride, size, step)))
    for got in hold_all(found, held):
        kept = kept + got.astype(F32)
    return kept.astype(BF16)


def reduce_first(array, count, held=()):
    return reduce_stage(split_rows(array, count), count, 0, held)


def reduce_rest(total, count, held=()):
    for stage in range(1, len(stages(count))):
        total = reduce_stage(total, count, stage, held)
    return total


def gather_stage(part, count, stage, held=()):
    stride, size = stages(count)[stage]
    digit = lax.axis_index("dp") // stride % size
    axis = part.ndim - 2
    found = [
        lax.ppermute(part, "dp", shift_pairs(count, stride, size, step)) for step in range(1, size)
    ]
    if size == 2:
        got = hold_all(found, held)[0]
        return jnp.stack(
            [jnp.where(digit == 0, part, got), jnp.where(digit == 0, got, part)], axis=axis
        )
    dims = part.shape[:axis] + (size,) + part.shape[axis:]
    whole_parts = lax.dynamic_update_index_in_dim(jnp.zeros(dims, BF16), part, digit, axis)
    for step, got in enumerate(hold_all(found, held), 1):
        whole_parts = lax.dynamic_update_index_in_dim(
            whole_parts, got, (digit - step) % size, axis
        )
    return whole_parts


def gather_rest(part, count, held=()):
    for stage in reversed(range(1, len(stages(count)))):
        part = gather_stage(part, count, stage, held)
    return part


def gather_first(part, count, held=()):
    return gather_stage(part, count, 0, held)


def spread(part):
    return lax.all_gather(part, "dp", axis=0, tiled=True)


def hold_all(arrays, others):
    if not others:
        return arrays
    return lax.optimization_barrier(tuple(arrays) + tuple(others))[: len(arrays)]


def hold(array, *others):
    return lax.optimization_barrier((array,) + others)[0]


def add(*parts):
    return sum(part.astype(F32) for part in parts).astype(BF16)


def segment_begin(segment):
    index = jnp.arange(segment.shape[0], dtype=jnp.int32)
    is_start = jnp.concatenate([jnp.ones((1,), dtype=bool), segment[1:] != segment[:-1]])
    return lax.cummax(jnp.where(is_start, index, jnp.zeros_like(index)), axis=0)


def rope_tables(position):
    frequency = ROPE_BASE ** (-(jnp.arange(ROT, dtype=F32) * 2.0 / HDIM))
    angles = frequency[:, None] * position.astype(F32)[None, :]
    return jnp.cos(angles), jnp.sin(angles)


def per_device(
    count,
    hidden_in,
    query_weight,
    key_weight,
    value_weight,
    output_weight,
    gate_weight,
    up_weight,
    down_weight,
    attn_gain,
    ffn_gain,
    out_grad,
    segment_ids,
):
    col, row = lax.axis_index("col"), lax.axis_index("row")
    first = col == 0

    def own_tokens(array):
        outer = jnp.concatenate([array[..., :BLOCK], array[..., 3 * BLOCK :]], axis=-1)
        inner = array[..., BLOCK : 3 * BLOCK]
        return jnp.where(first, outer, inner), jnp.where(first, inner, outer)

    def in_window(own, got):
        outer, inner = jnp.where(first, own, got), jnp.where(first, got, own)
        return jnp.concatenate([outer[:, :BLOCK], inner, outer[:, BLOCK:]], axis=1)

    w_near = jnp.concatenate(
        [query_weight[:, 0].T, key_weight[:, 0].T, value_weight[:, 0].T], axis=0
    )
    wo_near = output_weight[0]
    weights_far = swap(jnp.concatenate([w_near, wo_near], axis=0), "row")
    x_own, x_other = own_tokens(hidden_in.T)
    x_got = swap(x_other, "col")
    gains = jnp.stack([attn_gain, ffn_gain])
    gains_got = swap(gains, "col").astype(F32)
    gains = gains.astype(F32)
    gin_own, gmid_own = gains[0][:, None], gains[1][:, None]
    gin_got, gmid_got = gains_got[0][:, None], gains_got[1][:, None]
    segment = jnp.where(col == row, segment_ids, swap(segment_ids, "col"))
    begin, _ = own_tokens(segment_begin(segment))
    index, _ = own_tokens(jnp.arange(MAXLEN, dtype=jnp.int32))
    cosine, sine = rope_tables(index - begin)
    begin = begin[None]
    live_near = jnp.where(row == 0, LIVE[0], LIVE[1])
    where_near = jnp.stack([col, live_near]).astype(jnp.int32)
    where_far = jnp.stack([col, LIVE[0] + LIVE[1] - live_near]).astype(jnp.int32)

    w_near_got = swap(w_near, "col")
    heads = (shape((QUERY, LOCAL)), shape((2 * KEY, LOCAL)))
    nm_in, q_near, kv_near = run(
        project_near_kernel,
        (x_own, x_got, gin_own, gin_got, cosine, sine, w_near, w_near_got),
        (shape((D, LOCAL)),) + heads,
        2 * LOCAL * D * D,
    )
    kv_near_got = swap(kv_near, "col")
    wo_near_got = swap(wo_near, "col")
    att_near, lse_near = attend(where_near, begin, q_near, kv_near, kv_near_got)
    w_far, wo_far = weights_far[:D], weights_far[D:]
    weights_far_got = swap(hold(weights_far, lse_near), "col")
    w_far_got, wo_far_got = weights_far_got[:D], weights_far_got[D:]
    q_far, kv_far = run(
        project_far_kernel,
        (nm_in, cosine, sine, w_far, w_far_got),
        heads,
        2 * LOCAL * D * D,
    )
    kv_far_got = swap(kv_far, "col")
    att_far, lse_far = attend(where_far, begin, q_far, kv_far, kv_far_got)
    og_own, og_other = own_tokens(out_grad.T)
    og = jnp.concatenate([og_own, swap(og_other, "col")], axis=0)
    og_far = swap(og, "row")
    mid, nm = run(
        mid_kernel,
        (
            att_near, att_far, wo_near, wo_near_got, wo_far, wo_far_got, x_own, x_got,
            gmid_own, gmid_got,
        ),
        (shape((D, LOCAL), F32), shape((D, LOCAL))),
        2 * LOCAL * D * D,
        after=(og_far,),
    )

    mlp_weights = ()
    for weight in (gate_weight, up_weight, down_weight.T):
        mlp_weights += (weight, swap(weight, "col"))
    nm_far = swap(nm, "row")
    out_part, gnm_part, act, gg, gu = feed_forward(nm, og, mlp_weights, F32)
    out_send, gnm_send, act_far, gg_far, gu_far, down_keep, down_send = feed_forward(
        nm_far, og_far, mlp_weights, BF16, own=(og, act)
    )
    gnm_back = swap(gnm_send, "row")
    down_got = swap(down_send, "col")
    gate_keep, gate_send, up_keep, up_send = weight_grads(
        ((nm, nm_far),), ((gg, gg_far), (gu, gu_far)), (0, 0)
    )
    down_sum = add(down_keep, hold(down_got, gate_keep))
    gate_send, up_send = hold_all((gate_send, up_send), (gnm_back,))

    gmid, gb, gatt_near, gatt_far, ggain_mid = run(
        mid_back_kernel,
        (
            og, mid, gnm_part, gnm_back, gmid_own, gmid_got, wo_near, wo_near_got, wo_far,
            wo_far_got,
        ),
        (
            shape((D, LOCAL), F32), shape((D, LOCAL)), shape((QUERY, LOCAL)),
            shape((QUERY, LOCAL)), shape((2, 16, HALF), F32),
        ),
        2 * LOCAL * D * D,
        after=(down_sum,),
    )
    down_x = reduce_first(down_sum, count, (ggain_mid,))
    gate_sum = add(gate_keep, hold(swap(gate_send, "col"), ggain_mid))
    up_sum = add(up_keep, hold(swap(up_send, "col"), ggain_mid))

    dq_far, own_far, other_far = attend_back(
        where_far, begin, q_far, kv_far, kv_far_got, gatt_far, lse_far, after=(down_x, gate_sum, up_sum)
    )
    gate_x = reduce_first(gate_sum, count, (dq_far,))

    def out_grads(att):
        send = dot(att, gb[HALF:], 1, 1).astype(BF16)
        return add(dot(att, gb[:HALF], 1, 1), swap(send, "col"))

    wo_far_sum = out_grads(att_far)
    wo_near_sum = out_grads(att_near)
    got_far = swap(hold(other_far, gate_x), "col")
    joined = shape((ROWS, HALF))
    gnm_in_part, far_keep, far_send = run(
        joined_far_kernel,
        (dq_far, own_far, got_far, cosine, sine, w_far, w_far_got, nm_in),
        (shape((D, LOCAL), F32), joined, joined),
        4 * LOCAL * D * D,
        after=(gate_x,),
        scratch=[pltpu.VMEM((D, LOCAL), BF16)],
    )
    down_z = reduce_rest(down_x, count, (far_keep,))
    dq_near, own_near, other_near = attend_back(
        where_near, begin, q_near, kv_near, kv_near_got, gatt_near, lse_near, after=(down_z,)
    )
    wo_sum = add(wo_near_sum, swap(wo_far_sum, "row"))
    far_sum = add(far_keep, hold(swap(hold(far_send, down_z), "col"), dq_near))
    up_x = reduce_first(hold(up_sum, gate_x), count, (dq_near,))
    got_near = swap(hold(other_near, up_x, far_sum), "col")
    near_keep, near_send, grad = run(
        joined_near_kernel,
        (
            dq_near, own_near, got_near, cosine, sine, w_near, w_near_got, nm_in, gnm_in_part,
            x_own, x_got, gin_own, gin_got, gmid, ggain_mid,
        ),
        (joined, joined, shape((D, LOCAL))),
        4 * LOCAL * D * D,
        scratch=[pltpu.VMEM((D, LOCAL), BF16)],
    )
    far_back = swap(far_sum, "row")
    last_sum = add(near_keep, swap(hold(near_send, far_back), "col"), far_back)

    def feature_cols(array):
        return in_window(array[:HALF], swap(array[HALF:], "col")).T

    input_grad = feature_cols(grad)


    def widened(whole_sum):
        parts = whole_sum.reshape(-1, HALF, LANE)
        return parts.transpose(1, 0, 2).reshape(HALF, -1).astype(F32)

    gate_z = reduce_rest(gate_x, count, (grad,))
    up_z = reduce_rest(up_x, count, (last_sum,))
    out_back = hold(swap(hold(out_send, gnm_back), "row"), last_sum)
    block = (mid + out_part + out_back.astype(F32)).astype(BF16)
    down_grad = widened(spread(down_z))
    gate_grad = widened(spread(gate_z))
    block_out = feature_cols(block)
    up_rest = gather_rest(up_z, count, (last_sum,))
    out_x = reduce_first(wo_sum, count)
    last_x = reduce_first(last_sum, count)
    up_grad = widened(gather_first(up_rest, count).reshape(up_sum.shape))
    last_z = reduce_rest(jnp.concatenate([last_x, out_x], axis=-2), count)
    last = gather_first(gather_rest(last_z, count), count)
    last, out_weight_grad = last[..., : ROWS // count, :], last[..., ROWS // count :, :]
    last = last.reshape(last_sum.shape).astype(F32)
    out_weight_grad = out_weight_grad.reshape(wo_sum.shape).astype(F32)
    gain_grads = jnp.stack([last[D], last[D + 16]])
    gain_grads = gain_grads + swap(gain_grads, "row")
    return (
        block_out,
        input_grad,
        last[:QUERY].T[:, None, :],
        last[QUERY : QUERY + KEY].T[:, None, :],
        last[QUERY + KEY : D].T[:, None, :],
        out_weight_grad[None],
        gate_grad,
        up_grad,
        down_grad.T,
        gain_grads[0],
        gain_grads[1],
    )


def solution(mesh):
    return jax.shard_map(
        functools.partial(per_device, mesh.shape["dp"]),
        mesh=mesh,
        in_specs=(
            P(("dp", "row"), "col"),
            P("col", "row", None),
            P("col", "row", None),
            P("col", "row", None),
            P("row", None, "col"),
            P("col", "row"),
            P("col", "row"),
            P("row", "col"),
            P("col"),
            P("col"),
            P(("dp", "row"), "col"),
            P(("dp", "col")),
        ),
        out_specs=(
            P(("dp", "row"), "col"),
            P(("dp", "row"), "col"),
            P("col", "row", None),
            P("col", "row", None),
            P("col", "row", None),
            P("row", None, "col"),
            P("col", "row"),
            P("col", "row"),
            P("row", "col"),
            P("col"),
            P("col"),
        ),
        check_vma=False,
    )
```

```python
import functools
import math

import jax
import jax.numpy as jnp
from jax import lax
from jax.experimental import pallas as pl
from jax.experimental.pallas import tpu as pltpu
from jax.sharding import PartitionSpec as P

D = 960
HALF = D // 2
HDIM = 64
ROT = HDIM // 2
GROUP = 3
GROUPS = 3
QUERY = GROUPS * GROUP * HDIM
KEY = GROUPS * HDIM
MAXLEN = 1024
BLOCK = MAXLEN // 4
LOCAL = 2 * BLOCK
LANE = 128
LIVE = (3, 2)
ROWS = 1024

NORM_EPS = 1e-05
ROPE_BASE = 100000.0
MASKED_SCORE = -1e30
SCALE = 1.0 / math.sqrt(HDIM)
BF16 = jnp.bfloat16
F32 = jnp.float32
VMEM_BYTES = 56 * 1024 * 1024
COST = 0.03

HELD = ((0, 3), (1, 2))
LAID = ((0, 3, 1, 2), (0, 1, 2))
SPANS = ((1, 4), (2, 3))


def dot(left, right, left_dim=1, right_dim=0):
    return lax.dot_general(
        left, right, (((left_dim,), (right_dim,)), ((), ())), preferred_element_type=F32
    )


def shape(dims, dtype=BF16):
    return jax.ShapeDtypeStruct(dims, dtype)


def whole(dims):
    return pl.BlockSpec(dims, lambda *_: (0,) * len(dims))


SMEM_SPEC = pl.BlockSpec(memory_space=pltpu.SMEM)


def run(kernel, ins, outs, flops, grid=None, in_specs=None, out_specs=None, scratch=(), after=()):
    moved = sum(a.size * a.dtype.itemsize for a in ins)
    moved += sum(math.prod(o.shape) * jnp.dtype(o.dtype).itemsize for o in outs)
    if in_specs is None:
        in_specs = [whole(a.shape) for a in ins]
    if out_specs is None:
        out_specs = [whole(o.shape) for o in outs]
    count = len(ins)

    def body(*refs):
        kernel(*refs[:count], *refs[count + len(after) :])

    return pl.pallas_call(
        body,
        grid=grid if grid is not None else (1,),
        in_specs=list(in_specs) + [pl.BlockSpec(memory_space=pl.ANY)] * len(after),
        out_specs=tuple(out_specs),
        out_shape=tuple(outs),
        scratch_shapes=list(scratch),
        compiler_params=pltpu.CompilerParams(vmem_limit_bytes=VMEM_BYTES),
        cost_estimate=pl.CostEstimate(
            flops=int(flops * COST), bytes_accessed=int(moved * COST), transcendentals=0
        ),
    )(*ins, *after)


def level_of(own, got):
    total = jnp.sum(own * own, axis=0, keepdims=True) + jnp.sum(got * got, axis=0, keepdims=True)
    return lax.rsqrt(total / D + NORM_EPS)


def project_heads(nm, cos_ref, sin_ref, own_ref, got_ref, q_ref, kv_ref):
    cosine, sine = cos_ref[...], sin_ref[...]
    joined = dot(own_ref[...], nm[:HALF]) + dot(got_ref[...], nm[HALF:])
    for at in range(0, QUERY + KEY, HDIM):
        low, high = joined[at : at + ROT], joined[at + ROT : at + HDIM]
        parts = (low * cosine - high * sine, high * cosine + low * sine)
        for part, turned in enumerate(parts):
            turned = turned.astype(BF16)
            if at < QUERY:
                turned = (turned.astype(F32) * SCALE).astype(BF16)
                q_ref[at + part * ROT : at + (part + 1) * ROT, :] = turned
            else:
                row = at - QUERY + part * ROT
                kv_ref[row : row + ROT, :] = turned
    kv_ref[KEY:, :] = joined[QUERY + KEY :].astype(BF16)


def project_near_kernel(
    xo_ref, xg_ref, go_ref, gg_ref, cos_ref, sin_ref, own_ref, got_ref, nm_ref, q_ref, kv_ref
):
    own, got = xo_ref[...].astype(F32), xg_ref[...].astype(F32)
    level = level_of(own, got)
    nm_ref[:HALF, :] = (own * level * go_ref[...]).astype(BF16)
    nm_ref[HALF:, :] = (got * level * gg_ref[...]).astype(BF16)
    project_heads(nm_ref[...], cos_ref, sin_ref, own_ref, got_ref, q_ref, kv_ref)


def project_far_kernel(nm_ref, cos_ref, sin_ref, own_ref, got_ref, q_ref, kv_ref):
    project_heads(nm_ref[...], cos_ref, sin_ref, own_ref, got_ref, q_ref, kv_ref)


def laid(core, own, got, axis):
    if core == 0:
        return jnp.concatenate([own, got], axis=axis)
    return jnp.concatenate([lax.slice_in_dim(got, 0, BLOCK, axis=axis), own], axis=axis)


def fill_bias(core, bias_ref, begin_ref):
    for at, block in enumerate(LAID[core]):
        for slot in range(2):
            cols = slice(slot * BLOCK, (slot + 1) * BLOCK)
            key = block * BLOCK + lax.broadcasted_iota(jnp.int32, (BLOCK, BLOCK), 0)
            query = HELD[core][slot] * BLOCK + lax.broadcasted_iota(jnp.int32, (BLOCK, BLOCK), 1)
            allowed = (key >= begin_ref[:, cols]) & (key <= query)
            bias_ref[at * BLOCK : (at + 1) * BLOCK, cols] = jnp.where(allowed, 0.0, MASKED_SCORE)


def attend_kernel(
    where_ref, begin_ref, q_ref, ko_ref, vo_ref, kg_ref, vg_ref, att_ref, lse_ref, bias_ref
):
    group = pl.program_id(0)
    live = group < where_ref[1]

    @pl.when(jnp.logical_not(live))
    def _():
        att_ref[...] = jnp.zeros_like(att_ref)
        lse_ref[...] = jnp.zeros_like(lse_ref)

    for core in range(2):

        @pl.when(live & (where_ref[0] == core))
        def _():
            @pl.when(group == 0)
            def _():
                fill_bias(core, bias_ref, begin_ref)

            keys = laid(core, ko_ref[...], kg_ref[...], 1).T
            values = laid(core, vo_ref[...], vg_ref[...], 1)
            for slot in range(2):
                cols = slice(slot * BLOCK, (slot + 1) * BLOCK)
                span = SPANS[core][slot] * BLOCK
                for j in range(GROUP):
                    heads = slice(j * HDIM, (j + 1) * HDIM)
                    scores = dot(keys[:span], q_ref[heads, cols]) + bias_ref[:span, cols]
                    highest = jnp.max(scores, axis=0, keepdims=True)
                    weights = jnp.exp(scores - highest)
                    total = jnp.sum(weights, axis=0, keepdims=True)
                    mixed = dot(values[:, :span], weights.astype(BF16)) / total
                    att_ref[heads, cols] = mixed.astype(BF16)
                    lse_ref[0, j : j + 1, cols] = highest + jnp.log(total)


def mid_kernel(
    near_ref, far_ref, no_ref, ng_ref, fo_ref, fg_ref, xo_ref, xg_ref, go_ref, gg_ref,
    mid_ref, nm_ref,
):
    near, far = near_ref[...], far_ref[...]
    own = xo_ref[...].astype(F32) + dot(no_ref[...], near, 0, 0) + dot(fo_ref[...], far, 0, 0)
    got = xg_ref[...].astype(F32) + dot(ng_ref[...], near, 0, 0) + dot(fg_ref[...], far, 0, 0)
    mid_ref[:HALF, :] = own
    mid_ref[HALF:, :] = got
    level = level_of(own, got)
    nm_ref[:HALF, :] = (own * level * go_ref[...]).astype(BF16)
    nm_ref[HALF:, :] = (got * level * gg_ref[...]).astype(BF16)


def mlp_kernel(
    nm_ref, og_ref, wgo_ref, wgg_ref, wuo_ref, wug_ref, wdo_ref, wdg_ref,
    out_ref, gnm_ref, act_ref, gg_ref, gu_ref, out_sum, gnm_sum,
):
    step = pl.program_id(0)
    nm, og = nm_ref[...], og_ref[...]

    def inward(own_ref, got_ref, rows):
        return dot(own_ref[...], rows[:HALF], 0, 0) + dot(got_ref[...], rows[HALF:], 0, 0)

    @pl.when(step == 0)
    def _():
        out_sum[...] = jnp.zeros_like(out_sum)
        gnm_sum[...] = jnp.zeros_like(gnm_sum)

    gate = inward(wgo_ref, wgg_ref, nm)
    up = inward(wuo_ref, wug_ref, nm)
    grad_act = inward(wdo_ref, wdg_ref, og)
    sig = jax.nn.sigmoid(gate)
    silu = gate * sig
    act = (silu * up).astype(BF16)
    grad_gate = (grad_act * up * sig * (1.0 + gate * (1.0 - sig))).astype(BF16)
    grad_up = (grad_act * silu).astype(BF16)
    act_ref[...] = act
    gg_ref[...] = grad_gate
    gu_ref[...] = grad_up
    gnm_sum[:HALF, :] += dot(wgo_ref[...], grad_gate) + dot(wuo_ref[...], grad_up)
    gnm_sum[HALF:, :] += dot(wgg_ref[...], grad_gate) + dot(wug_ref[...], grad_up)
    out_sum[:HALF, :] += dot(wdo_ref[...], act)
    out_sum[HALF:, :] += dot(wdg_ref[...], act)

    @pl.when(step == pl.num_programs(0) - 1)
    def _():
        out_ref[...] = out_sum[...].astype(out_ref.dtype)
        gnm_ref[...] = gnm_sum[...].astype(gnm_ref.dtype)


def grads_kernel(row_counts, col_counts, rows_of, *refs):
    at = 0

    def whole_tokens(count):
        nonlocal at
        at += count
        return jnp.concatenate([ref[...] for ref in refs[at - count : at]], axis=1)

    rows = [whole_tokens(count) for count in row_counts]
    for kind, count in enumerate(col_counts):
        cols = whole_tokens(count)
        for half in range(2):
            left = rows[rows_of[kind]][half * HALF : (half + 1) * HALF]
            product = dot(left, cols, 1, 1).astype(BF16)
            out_ref = refs[len(refs) - 2 * len(col_counts) + 2 * kind + half]
            out_ref[:HALF, :] = product[:, :LANE]
            out_ref[HALF:, :] = product[:, LANE:]


def gain_rows(product):
    return lax.dot_general(
        jnp.ones((16, product.shape[1]), F32), product, (((1,), (1,)), ((), ())),
        precision=lax.Precision.HIGHEST, preferred_element_type=F32,
    )


def mid_back_kernel(
    og_ref, mid_ref, part_ref, back_ref, go_ref, gg_ref, no_ref, ng_ref, fo_ref, fg_ref,
    gmid_ref, gb_ref, near_ref, far_ref, ggain_ref,
):
    own, got = mid_ref[:HALF, :], mid_ref[HALF:, :]
    level = level_of(own, got)
    gnm = part_ref[...] + back_ref[...].astype(F32)
    scaled_own, scaled_got = gnm[:HALF] * go_ref[...], gnm[HALF:] * gg_ref[...]
    inner = jnp.sum(scaled_own * own, axis=0, keepdims=True)
    inner += jnp.sum(scaled_got * got, axis=0, keepdims=True)
    pull = level**3 * inner / D
    for rows, mid, scaled in (
        (slice(0, HALF), own, scaled_own), (slice(HALF, D), got, scaled_got)
    ):
        ggain_ref[rows.start // HALF] = gain_rows(gnm[rows] * mid * level)
        gmid = og_ref[rows, :].astype(F32) + scaled * level - mid * pull
        gmid_ref[rows, :] = gmid
        gb_ref[rows, :] = gmid.astype(BF16)
    gb_own, gb_got = gb_ref[:HALF, :], gb_ref[HALF:, :]
    near_ref[...] = (dot(no_ref[...], gb_own) + dot(ng_ref[...], gb_got)).astype(BF16)
    far_ref[...] = (dot(fo_ref[...], gb_own) + dot(fg_ref[...], gb_got)).astype(BF16)


def attend_back_kernel(
    where_ref, begin_ref, q_ref, ko_ref, vo_ref, kg_ref, vg_ref, gatt_ref, lse_ref,
    dq_ref, own_ref, got_ref, bias_ref, dk_ref, dv_ref,
):
    group = pl.program_id(0)
    live = group < where_ref[1]

    @pl.when(jnp.logical_not(live))
    def _():
        dq_ref[...] = jnp.zeros_like(dq_ref)
        own_ref[...] = jnp.zeros_like(own_ref)
        got_ref[...] = jnp.zeros_like(got_ref)

    for core in range(2):

        @pl.when(live & (where_ref[0] == core))
        def _():
            @pl.when(group == 0)
            def _():
                fill_bias(core, bias_ref, begin_ref)

            keys_t = laid(core, ko_ref[...], kg_ref[...], 1)
            keys = keys_t.T
            values = laid(core, vo_ref[...], vg_ref[...], 1).T
            dk_ref[...] = jnp.zeros_like(dk_ref)
            dv_ref[...] = jnp.zeros_like(dv_ref)
            for slot in range(2):
                cols = slice(slot * BLOCK, (slot + 1) * BLOCK)
                span = SPANS[core][slot] * BLOCK
                for j in range(GROUP):
                    heads = slice(j * HDIM, (j + 1) * HDIM)
                    queries, grads = q_ref[heads, cols], gatt_ref[heads, cols]
                    scores = dot(keys[:span], queries) + bias_ref[:span, cols]
                    probs = jnp.exp(scores - lse_ref[0, j : j + 1, cols])
                    dprobs = dot(values[:span], grads)
                    inner = jnp.sum(probs * dprobs, axis=0, keepdims=True)
                    dscores = (probs * (dprobs - inner)).astype(BF16)
                    dv_ref[:span, :] += dot(probs.astype(BF16), grads.T)
                    dk_ref[:span, :] += dot(dscores, queries.T)
                    dq_ref[heads, cols] = dot(keys_t[:, :span], dscores) * SCALE
            for kind, grad_ref in enumerate((dk_ref, dv_ref)):
                if core == 0:
                    own_ref[kind, 0] = grad_ref[:LOCAL, :].T
                    got_ref[kind, 0] = grad_ref[LOCAL:, :].T.astype(BF16)
                else:
                    own_ref[kind, 0] = grad_ref[BLOCK : BLOCK + LOCAL, :].T
                    got_ref[kind, 0, :, :BLOCK] = grad_ref[:BLOCK, :].T.astype(BF16)
                    got_ref[kind, 0, :, BLOCK:] = jnp.zeros((HDIM, BLOCK), BF16)


def turn_back(cos_ref, sin_ref, dq_ref, own_ref, got_ref, gj_ref):
    cosine, sine = cos_ref[...], sin_ref[...]

    def back(at, grad):
        low, high = grad[:ROT], grad[ROT:]
        gj_ref[at : at + ROT, :] = (low * cosine + high * sine).astype(BF16)
        gj_ref[at + ROT : at + HDIM, :] = (high * cosine - low * sine).astype(BF16)

    for at in range(0, QUERY, HDIM):
        back(at, dq_ref[at : at + HDIM, :])
    for g in range(GROUPS):
        back(QUERY + g * HDIM, own_ref[0, g] + got_ref[0, g].astype(F32))
        at = QUERY + KEY + g * HDIM
        gj_ref[at : at + HDIM, :] = (own_ref[1, g] + got_ref[1, g].astype(F32)).astype(BF16)


def joined_far_kernel(
    dq_ref, own_ref, got_ref, cos_ref, sin_ref, wo_ref, wg_ref, nm_ref,
    gnm_ref, keep_ref, send_ref, gj_ref,
):
    turn_back(cos_ref, sin_ref, dq_ref, own_ref, got_ref, gj_ref)
    gj = gj_ref[...]
    for half, out_ref in enumerate((keep_ref, send_ref)):
        rows = slice(half * HALF, (half + 1) * HALF)
        out_ref[:D, :] = dot(gj, nm_ref[rows, :], 1, 1).astype(BF16)
        out_ref[D:, :] = jnp.zeros((ROWS - D, HALF), BF16)
    gnm_ref[:HALF, :] = dot(wo_ref[...], gj, 0, 0)
    gnm_ref[HALF:, :] = dot(wg_ref[...], gj, 0, 0)


def joined_near_kernel(
    dq_ref, own_ref, got_ref, cos_ref, sin_ref, wo_ref, wg_ref, nm_ref, part_ref, xo_ref, xg_ref,
    go_ref, gg_ref, gmid_ref, ggain_ref, keep_ref, send_ref, grad_ref, gj_ref,
):
    turn_back(cos_ref, sin_ref, dq_ref, own_ref, got_ref, gj_ref)
    gj = gj_ref[...]
    gnm_own = part_ref[:HALF, :] + dot(wo_ref[...], gj, 0, 0)
    gnm_got = part_ref[HALF:, :] + dot(wg_ref[...], gj, 0, 0)
    own, got = xo_ref[...].astype(F32), xg_ref[...].astype(F32)
    level = level_of(own, got)
    scaled_own, scaled_got = gnm_own * go_ref[...], gnm_got * gg_ref[...]
    inner = jnp.sum(scaled_own * own, axis=0, keepdims=True)
    inner += jnp.sum(scaled_got * got, axis=0, keepdims=True)
    pull = level**3 * inner / D
    for rows, x, gnm, scaled in (
        (slice(0, HALF), own, gnm_own, scaled_own), (slice(HALF, D), got, gnm_got, scaled_got)
    ):
        half = rows.start // HALF
        out_ref = (keep_ref, send_ref)[half]
        out_ref[:D, :] = dot(gj, nm_ref[rows, :], 1, 1).astype(BF16)
        out_ref[D : D + 16, :] = gain_rows(gnm * x * level).astype(BF16)
        out_ref[D + 16 : D + 32, :] = ggain_ref[half].astype(BF16)
        out_ref[D + 32 :, :] = jnp.zeros((ROWS - D - 32, HALF), BF16)
        grad_ref[rows, :] = (gmid_ref[rows, :] + scaled * level - x * pull).astype(BF16)


def per_group(rows, at=0):
    return pl.BlockSpec((rows, LOCAL), lambda g: (g + at, 0))


LSE_SPEC = pl.BlockSpec((1, 8, LOCAL), lambda g: (g, 0, 0))
KV_SPECS = [per_group(HDIM), per_group(HDIM, GROUPS)] * 2
PAIR_SPEC = pl.BlockSpec((2, 1, HDIM, LOCAL), lambda g: (0, g, 0, 0))


def attend(where, begin, q, kv, kv_got, after=()):
    return run(
        attend_kernel,
        (where, begin, q, kv, kv, kv_got, kv_got),
        (shape((QUERY, LOCAL)), shape((GROUPS, 8, LOCAL), F32)),
        6e9,
        grid=(GROUPS,),
        in_specs=[SMEM_SPEC, whole((1, LOCAL)), per_group(GROUP * HDIM)] + KV_SPECS,
        out_specs=(per_group(GROUP * HDIM), LSE_SPEC),
        scratch=[pltpu.VMEM((MAXLEN, LOCAL), F32)],
        after=after,
    )


def attend_back(where, begin, q, kv, kv_got, gatt, lse, after=()):
    return run(
        attend_back_kernel,
        (where, begin, q, kv, kv, kv_got, kv_got, gatt, lse),
        (
            shape((QUERY, LOCAL), F32), shape((2, GROUPS, HDIM, LOCAL), F32),
            shape((2, GROUPS, HDIM, LOCAL)),
        ),
        14e9,
        grid=(GROUPS,),
        in_specs=[SMEM_SPEC, whole((1, LOCAL)), per_group(GROUP * HDIM)]
        + KV_SPECS
        + [per_group(GROUP * HDIM), LSE_SPEC],
        out_specs=(per_group(GROUP * HDIM), PAIR_SPEC, PAIR_SPEC),
        scratch=[
            pltpu.VMEM((MAXLEN, LOCAL), F32), pltpu.VMEM((MAXLEN, HDIM), F32),
            pltpu.VMEM((MAXLEN, HDIM), F32),
        ],
        after=after,
    )


def feed_forward(nm, og, weights, dtype, after=()):
    hidden = weights[0].shape[1]
    chunk = 2 * LANE
    cols = pl.BlockSpec((HALF, chunk), lambda i: (0, i))
    rows = pl.BlockSpec((chunk, LOCAL), lambda i: (i, 0))
    act = shape((hidden, LOCAL))
    return run(
        mlp_kernel,
        (nm, og) + weights,
        (shape((D, LOCAL), dtype), shape((D, LOCAL), dtype), act, act, act),
        12 * LOCAL * D * hidden,
        grid=(hidden // chunk,),
        in_specs=[whole((D, LOCAL))] * 2 + [cols] * 6,
        out_specs=(whole((D, LOCAL)), whole((D, LOCAL)), rows, rows, rows),
        scratch=[pltpu.VMEM((D, LOCAL), F32)] * 2,
        after=after,
    )


def weight_grads(rows, cols, rows_of, after=()):
    hidden = cols[0][0].shape[0]
    chunk = 2 * LANE
    all_rows, all_cols = sum(rows, ()), sum(cols, ())
    return run(
        functools.partial(
            grads_kernel, [len(pieces) for pieces in rows], [len(pieces) for pieces in cols], rows_of
        ),
        all_rows + all_cols,
        (shape((hidden // LANE * HALF, LANE)),) * (2 * len(cols)),
        4 * LOCAL * D * hidden * len(cols),
        grid=(hidden // chunk,),
        in_specs=[whole(part.shape) for part in all_rows]
        + [pl.BlockSpec((chunk, part.shape[1]), lambda i: (i, 0)) for part in all_cols],
        out_specs=(pl.BlockSpec((2 * HALF, LANE), lambda i: (i, 0)),) * (2 * len(cols)),
        after=after,
    )


def swap(array, axis):
    return lax.ppermute(array, axis, [(0, 1), (1, 0)])


def stages(count):
    found, stride = [], 1
    for size in (2,) + (4,) * 16:
        size = min(size, count // stride)
        if size < 2:
            break
        found.append((stride, size))
        stride *= size
    return found


def shift_pairs(count, stride, size, step):
    pairs = []
    for i in range(count):
        digit = i // stride % size
        pairs.append((i, i + ((digit + step) % size - digit) * stride))
    return pairs


def split_rows(array, count):
    rows, cols = array.shape
    sizes = [size for _, size in stages(count)]
    return array.reshape(*sizes[::-1], rows // count, cols)


def reduce_stage(total, count, stage, held=()):
    stride, size = stages(count)[stage]
    digit = lax.axis_index("dp") // stride % size
    axis = total.ndim - 3
    kept = lax.dynamic_index_in_dim(total, digit, axis, keepdims=False).astype(F32)
    found = []
    for step in range(1, size):
        sent = lax.dynamic_index_in_dim(total, (digit + step) % size, axis, keepdims=False)
        found.append(lax.ppermute(sent, "dp", shift_pairs(count, stride, size, step)))
    for got in hold_all(found, held):
        kept = kept + got.astype(F32)
    return kept.astype(BF16)


def reduce_first(array, count, held=()):
    return reduce_stage(split_rows(array, count), count, 0, held)


def reduce_rest(total, count, held=()):
    for stage in range(1, len(stages(count))):
        total = reduce_stage(total, count, stage, held)
    return total


def gather_stage(part, count, stage, held=()):
    stride, size = stages(count)[stage]
    digit = lax.axis_index("dp") // stride % size
    axis = part.ndim - 2
    found = [
        lax.ppermute(part, "dp", shift_pairs(count, stride, size, step)) for step in range(1, size)
    ]
    if size == 2:
        got = hold_all(found, held)[0]
        return jnp.stack(
            [jnp.where(digit == 0, part, got), jnp.where(digit == 0, got, part)], axis=axis
        )
    dims = part.shape[:axis] + (size,) + part.shape[axis:]
    whole_parts = lax.dynamic_update_index_in_dim(jnp.zeros(dims, BF16), part, digit, axis)
    for step, got in enumerate(hold_all(found, held), 1):
        whole_parts = lax.dynamic_update_index_in_dim(
            whole_parts, got, (digit - step) % size, axis
        )
    return whole_parts


def gather_rest(part, count, held=()):
    for stage in reversed(range(1, len(stages(count)))):
        part = gather_stage(part, count, stage, held)
    return part


def gather_first(part, count, held=()):
    return gather_stage(part, count, 0, held)


def spread(part):
    return lax.all_gather(part, "dp", axis=0, tiled=True)


def hold_all(arrays, others):
    if not others:
        return arrays
    return lax.optimization_barrier(tuple(arrays) + tuple(others))[: len(arrays)]


def hold(array, *others):
    return lax.optimization_barrier((array,) + others)[0]


def add(*parts):
    return sum(part.astype(F32) for part in parts).astype(BF16)


def segment_begin(segment):
    index = jnp.arange(segment.shape[0], dtype=jnp.int32)
    is_start = jnp.concatenate([jnp.ones((1,), dtype=bool), segment[1:] != segment[:-1]])
    return lax.cummax(jnp.where(is_start, index, jnp.zeros_like(index)), axis=0)


def rope_tables(position):
    frequency = ROPE_BASE ** (-(jnp.arange(ROT, dtype=F32) * 2.0 / HDIM))
    angles = frequency[:, None] * position.astype(F32)[None, :]
    return jnp.cos(angles), jnp.sin(angles)


def per_device(
    count,
    hidden_in,
    query_weight,
    key_weight,
    value_weight,
    output_weight,
    gate_weight,
    up_weight,
    down_weight,
    attn_gain,
    ffn_gain,
    out_grad,
    segment_ids,
):
    col, row = lax.axis_index("col"), lax.axis_index("row")
    first = col == 0

    def own_tokens(array):
        outer = jnp.concatenate([array[..., :BLOCK], array[..., 3 * BLOCK :]], axis=-1)
        inner = array[..., BLOCK : 3 * BLOCK]
        return jnp.where(first, outer, inner), jnp.where(first, inner, outer)

    def in_window(own, got):
        outer, inner = jnp.where(first, own, got), jnp.where(first, got, own)
        return jnp.concatenate([outer[:, :BLOCK], inner, outer[:, BLOCK:]], axis=1)

    w_near = jnp.concatenate(
        [query_weight[:, 0].T, key_weight[:, 0].T, value_weight[:, 0].T], axis=0
    )
    w_far = swap(w_near, "row")
    wo_near = output_weight[0]
    wo_far = swap(wo_near, "row")
    x_own, x_other = own_tokens(hidden_in.T)
    x_got = swap(x_other, "col")
    gains = jnp.stack([attn_gain, ffn_gain])
    gains_got = swap(gains, "col").astype(F32)
    gains = gains.astype(F32)
    gin_own, gmid_own = gains[0][:, None], gains[1][:, None]
    gin_got, gmid_got = gains_got[0][:, None], gains_got[1][:, None]
    segment = jnp.where(col == row, segment_ids, swap(segment_ids, "col"))
    begin, _ = own_tokens(segment_begin(segment))
    index, _ = own_tokens(jnp.arange(MAXLEN, dtype=jnp.int32))
    cosine, sine = rope_tables(index - begin)
    begin = begin[None]
    live_near = jnp.where(row == 0, LIVE[0], LIVE[1])
    where_near = jnp.stack([col, live_near]).astype(jnp.int32)
    where_far = jnp.stack([col, LIVE[0] + LIVE[1] - live_near]).astype(jnp.int32)

    w_near_got = swap(w_near, "col")
    heads = (shape((QUERY, LOCAL)), shape((2 * KEY, LOCAL)))
    nm_in, q_near, kv_near = run(
        project_near_kernel,
        (x_own, x_got, gin_own, gin_got, cosine, sine, w_near, w_near_got),
        (shape((D, LOCAL)),) + heads,
        2 * LOCAL * D * D,
    )
    kv_near_got = swap(kv_near, "col")
    wo_near_got = swap(wo_near, "col")
    att_near, lse_near = attend(where_near, begin, q_near, kv_near, kv_near_got)
    w_far_got = swap(hold(w_far, lse_near), "col")
    q_far, kv_far = run(
        project_far_kernel,
        (nm_in, cosine, sine, w_far, w_far_got),
        heads,
        2 * LOCAL * D * D,
    )
    kv_far_got = swap(kv_far, "col")
    att_far, lse_far = attend(where_far, begin, q_far, kv_far, kv_far_got)
    wo_far_got = swap(hold(wo_far, kv_far), "col")
    og_own, og_other = own_tokens(out_grad.T)
    og = jnp.concatenate([og_own, swap(og_other, "col")], axis=0)
    og_far = swap(og, "row")
    mid, nm = run(
        mid_kernel,
        (
            att_near, att_far, wo_near, wo_near_got, wo_far, wo_far_got, x_own, x_got,
            gmid_own, gmid_got,
        ),
        (shape((D, LOCAL), F32), shape((D, LOCAL))),
        2 * LOCAL * D * D,
    )

    mlp_weights = ()
    for weight in (gate_weight, up_weight, down_weight.T):
        mlp_weights += (weight, swap(weight, "col"))
    nm_far = swap(nm, "row")
    out_part, gnm_part, act, gg, gu = feed_forward(nm, og, mlp_weights, F32, after=(og_far,))
    out_send, gnm_send, act_far, gg_far, gu_far = feed_forward(
        nm_far, og_far, mlp_weights, BF16, after=(act,)
    )
    gnm_back = swap(gnm_send, "row")
    down_keep, down_send = weight_grads(((og, og_far),), ((act, act_far),), (0,))
    down_got = swap(down_send, "col")
    gate_keep, gate_send, up_keep, up_send = weight_grads(
        ((nm, nm_far),), ((gg, gg_far), (gu, gu_far)), (0, 0), after=(down_keep,)
    )
    down_sum = add(down_keep, hold(down_got, gate_keep))
    gate_send, up_send = hold_all((gate_send, up_send), (gnm_back,))

    gmid, gb, gatt_near, gatt_far, ggain_mid = run(
        mid_back_kernel,
        (
            og, mid, gnm_part, gnm_back, gmid_own, gmid_got, wo_near, wo_near_got, wo_far,
            wo_far_got,
        ),
        (
            shape((D, LOCAL), F32), shape((D, LOCAL)), shape((QUERY, LOCAL)),
            shape((QUERY, LOCAL)), shape((2, 16, HALF), F32),
        ),
        2 * LOCAL * D * D,
        after=(down_sum,),
    )
    down_x = reduce_first(down_sum, count, (ggain_mid,))
    gate_sum = add(gate_keep, hold(swap(gate_send, "col"), ggain_mid))
    up_sum = add(up_keep, hold(swap(up_send, "col"), ggain_mid))

    dq_far, own_far, other_far = attend_back(
        where_far, begin, q_far, kv_far, kv_far_got, gatt_far, lse_far, after=(down_x, gate_sum, up_sum)
    )
    gate_x = reduce_first(gate_sum, count, (dq_far,))

    def out_grads(att):
        send = dot(att, gb[HALF:], 1, 1).astype(BF16)
        return add(dot(att, gb[:HALF], 1, 1), swap(send, "col"))

    wo_far_sum = out_grads(att_far)
    wo_near_sum = out_grads(att_near)
    got_far = swap(hold(other_far, gate_x), "col")
    joined = shape((ROWS, HALF))
    gnm_in_part, far_keep, far_send = run(
        joined_far_kernel,
        (dq_far, own_far, got_far, cosine, sine, w_far, w_far_got, nm_in),
        (shape((D, LOCAL), F32), joined, joined),
        4 * LOCAL * D * D,
        after=(gate_x,),
        scratch=[pltpu.VMEM((D, LOCAL), BF16)],
    )
    down_z = reduce_rest(down_x, count, (far_keep,))
    up_x = reduce_first(hold(up_sum, gate_x), count, (far_keep,))
    dq_near, own_near, other_near = attend_back(
        where_near, begin, q_near, kv_near, kv_near_got, gatt_near, lse_near, after=(down_z, up_x, wo_far_sum, wo_near_sum)
    )
    wo_sum = add(wo_near_sum, swap(wo_far_sum, "row"))
    far_sum = add(far_keep, hold(swap(hold(far_send, down_z, up_x), "col"), dq_near))
    got_near = swap(hold(other_near, far_sum, wo_sum), "col")
    near_keep, near_send, grad = run(
        joined_near_kernel,
        (
            dq_near, own_near, got_near, cosine, sine, w_near, w_near_got, nm_in, gnm_in_part,
            x_own, x_got, gin_own, gin_got, gmid, ggain_mid,
        ),
        (joined, joined, shape((D, LOCAL))),
        4 * LOCAL * D * D,
        scratch=[pltpu.VMEM((D, LOCAL), BF16)],
    )
    gate_z = reduce_rest(gate_x, count, (grad,))
    far_back = swap(far_sum, "row")
    last_sum = add(near_keep, swap(hold(near_send, far_back, gate_z), "col"), far_back)

    def feature_cols(array):
        return in_window(array[:HALF], swap(array[HALF:], "col")).T


    def widened(whole_sum):
        parts = whole_sum.reshape(-1, HALF, LANE)
        return parts.transpose(1, 0, 2).reshape(HALF, -1).astype(F32)

    last_x = reduce_first(last_sum, count)
    out_x = reduce_first(wo_sum, count)
    up_z = reduce_rest(up_x, count, (last_x,))
    last_z = reduce_rest(jnp.concatenate([last_x, out_x], axis=-2), count)
    out_back = hold(swap(hold(out_send, gnm_back), "row"), last_z)
    block_out = feature_cols((mid + out_part + out_back.astype(F32)).astype(BF16))
    input_grad = feature_cols(hold(grad, last_x))
    down_grad = widened(hold(spread(down_z), last_x))
    gate_grad = widened(hold(spread(gate_z), last_x))
    up_rest = gather_rest(up_z, count, (last_z,))
    up_grad = widened(gather_first(up_rest, count).reshape(up_sum.shape))
    last = gather_first(gather_rest(last_z, count), count)
    last, out_weight_grad = last[..., : ROWS // count, :], last[..., ROWS // count :, :]
    last = last.reshape(last_sum.shape).astype(F32)
    out_weight_grad = out_weight_grad.reshape(wo_sum.shape).astype(F32)
    gain_grads = jnp.stack([last[D], last[D + 16]])
    gain_grads = gain_grads + swap(gain_grads, "row")
    return (
        block_out,
        input_grad,
        last[:QUERY].T[:, None, :],
        last[QUERY : QUERY + KEY].T[:, None, :],
        last[QUERY + KEY : D].T[:, None, :],
        out_weight_grad[None],
        gate_grad,
        up_grad,
        down_grad.T,
        gain_grads[0],
        gain_grads[1],
    )


def solution(mesh):
    return jax.shard_map(
        functools.partial(per_device, mesh.shape["dp"]),
        mesh=mesh,
        in_specs=(
            P(("dp", "row"), "col"),
            P("col", "row", None),
            P("col", "row", None),
            P("col", "row", None),
            P("row", None, "col"),
            P("col", "row"),
            P("col", "row"),
            P("row", "col"),
            P("col"),
            P("col"),
            P(("dp", "row"), "col"),
            P(("dp", "col")),
        ),
        out_specs=(
            P(("dp", "row"), "col"),
            P(("dp", "row"), "col"),
            P("col", "row", None),
            P("col", "row", None),
            P("col", "row", None),
            P("row", None, "col"),
            P("col", "row"),
            P("col", "row"),
            P("row", "col"),
            P("col"),
            P("col"),
        ),
        check_vma=False,
    )
```

```python
import functools
import math

import jax
import jax.numpy as jnp
from jax import lax
from jax.experimental import pallas as pl
from jax.experimental.pallas import tpu as pltpu
from jax.sharding import PartitionSpec as P

D = 960
HALF = D // 2
HDIM = 64
ROT = HDIM // 2
GROUP = 3
GROUPS = 3
QUERY = GROUPS * GROUP * HDIM
KEY = GROUPS * HDIM
MAXLEN = 1024
BLOCK = MAXLEN // 4
LOCAL = 2 * BLOCK
LANE = 128
LIVE = (3, 2)
ROWS = 1024
WIDE = 512

NORM_EPS = 1e-05
ROPE_BASE = 100000.0
MASKED_SCORE = -1e30
SCALE = 1.0 / math.sqrt(HDIM)
BF16 = jnp.bfloat16
F32 = jnp.float32
VMEM_BYTES = 56 * 1024 * 1024
COST = 0.03

HELD = ((0, 3), (1, 2))
LAID = ((0, 3, 1, 2), (0, 1, 2))
SPANS = ((1, 4), (2, 3))


def dot(left, right, left_dim=1, right_dim=0):
    return lax.dot_general(
        left, right, (((left_dim,), (right_dim,)), ((), ())), preferred_element_type=F32
    )


def shape(dims, dtype=BF16):
    return jax.ShapeDtypeStruct(dims, dtype)


def whole(dims):
    return pl.BlockSpec(dims, lambda *_: (0,) * len(dims))


SMEM_SPEC = pl.BlockSpec(memory_space=pltpu.SMEM)


def run(kernel, ins, outs, flops, grid=None, in_specs=None, out_specs=None, scratch=(), after=()):
    moved = sum(a.size * a.dtype.itemsize for a in ins)
    moved += sum(math.prod(o.shape) * jnp.dtype(o.dtype).itemsize for o in outs)
    if in_specs is None:
        in_specs = [whole(a.shape) for a in ins]
    if out_specs is None:
        out_specs = [whole(o.shape) for o in outs]
    count = len(ins)

    def body(*refs):
        kernel(*refs[:count], *refs[count + len(after) :])

    return pl.pallas_call(
        body,
        grid=grid if grid is not None else (1,),
        in_specs=list(in_specs) + [pl.BlockSpec(memory_space=pl.ANY)] * len(after),
        out_specs=tuple(out_specs),
        out_shape=tuple(outs),
        scratch_shapes=list(scratch),
        compiler_params=pltpu.CompilerParams(vmem_limit_bytes=VMEM_BYTES),
        cost_estimate=pl.CostEstimate(
            flops=int(flops * COST), bytes_accessed=int(moved * COST), transcendentals=0
        ),
    )(*ins, *after)


def level_of(own, got):
    total = jnp.sum(own * own, axis=0, keepdims=True) + jnp.sum(got * got, axis=0, keepdims=True)
    return lax.rsqrt(total / D + NORM_EPS)


def project_heads(nm, cos_ref, sin_ref, own_ref, got_ref, q_ref, kv_ref):
    cosine, sine = cos_ref[...], sin_ref[...]
    joined = dot(own_ref[...], nm[:HALF]) + dot(got_ref[...], nm[HALF:])
    for at in range(0, QUERY + KEY, HDIM):
        low, high = joined[at : at + ROT], joined[at + ROT : at + HDIM]
        parts = (low * cosine - high * sine, high * cosine + low * sine)
        for part, turned in enumerate(parts):
            turned = turned.astype(BF16)
            if at < QUERY:
                turned = (turned.astype(F32) * SCALE).astype(BF16)
                q_ref[at + part * ROT : at + (part + 1) * ROT, :] = turned
            else:
                row = at - QUERY + part * ROT
                kv_ref[row : row + ROT, :] = turned
    kv_ref[KEY:, :] = joined[QUERY + KEY :].astype(BF16)


def project_near_kernel(
    xo_ref, xg_ref, go_ref, gg_ref, cos_ref, sin_ref, own_ref, got_ref, nm_ref, q_ref, kv_ref
):
    own, got = xo_ref[...].astype(F32), xg_ref[...].astype(F32)
    level = level_of(own, got)
    nm_ref[:HALF, :] = (own * level * go_ref[...]).astype(BF16)
    nm_ref[HALF:, :] = (got * level * gg_ref[...]).astype(BF16)
    project_heads(nm_ref[...], cos_ref, sin_ref, own_ref, got_ref, q_ref, kv_ref)


def project_far_kernel(nm_ref, cos_ref, sin_ref, own_ref, got_ref, q_ref, kv_ref):
    project_heads(nm_ref[...], cos_ref, sin_ref, own_ref, got_ref, q_ref, kv_ref)


def laid(core, own, got, axis):
    if core == 0:
        return jnp.concatenate([own, got], axis=axis)
    return jnp.concatenate([lax.slice_in_dim(got, 0, BLOCK, axis=axis), own], axis=axis)


def fill_bias(core, bias_ref, begin_ref):
    for at, block in enumerate(LAID[core]):
        for slot in range(2):
            cols = slice(slot * BLOCK, (slot + 1) * BLOCK)
            key = block * BLOCK + lax.broadcasted_iota(jnp.int32, (BLOCK, BLOCK), 0)
            query = HELD[core][slot] * BLOCK + lax.broadcasted_iota(jnp.int32, (BLOCK, BLOCK), 1)
            allowed = (key >= begin_ref[:, cols]) & (key <= query)
            bias_ref[at * BLOCK : (at + 1) * BLOCK, cols] = jnp.where(allowed, 0.0, MASKED_SCORE)


def attend_kernel(
    where_ref, begin_ref, q_ref, ko_ref, vo_ref, kg_ref, vg_ref, att_ref, lse_ref, bias_ref
):
    group = pl.program_id(0)
    live = group < where_ref[1]

    @pl.when(jnp.logical_not(live))
    def _():
        att_ref[...] = jnp.zeros_like(att_ref)
        lse_ref[...] = jnp.zeros_like(lse_ref)

    for core in range(2):

        @pl.when(live & (where_ref[0] == core))
        def _():
            @pl.when(group == 0)
            def _():
                fill_bias(core, bias_ref, begin_ref)

            keys = laid(core, ko_ref[...], kg_ref[...], 1).T
            values = laid(core, vo_ref[...], vg_ref[...], 1)
            for slot in range(2):
                cols = slice(slot * BLOCK, (slot + 1) * BLOCK)
                span = SPANS[core][slot] * BLOCK
                for j in range(GROUP):
                    heads = slice(j * HDIM, (j + 1) * HDIM)
                    scores = dot(keys[:span], q_ref[heads, cols]) + bias_ref[:span, cols]
                    highest = jnp.max(scores, axis=0, keepdims=True)
                    weights = jnp.exp(scores - highest)
                    total = jnp.sum(weights, axis=0, keepdims=True)
                    mixed = dot(values[:, :span], weights.astype(BF16)) / total
                    att_ref[heads, cols] = mixed.astype(BF16)
                    lse_ref[0, j : j + 1, cols] = highest + jnp.log(total)


def mid_kernel(
    near_ref, far_ref, no_ref, ng_ref, fo_ref, fg_ref, xo_ref, xg_ref, go_ref, gg_ref,
    mid_ref, nm_ref,
):
    near, far = near_ref[...], far_ref[...]
    own = xo_ref[...].astype(F32) + dot(no_ref[...], near, 0, 0) + dot(fo_ref[...], far, 0, 0)
    got = xg_ref[...].astype(F32) + dot(ng_ref[...], near, 0, 0) + dot(fg_ref[...], far, 0, 0)
    mid_ref[:HALF, :] = own
    mid_ref[HALF:, :] = got
    level = level_of(own, got)
    nm_ref[:HALF, :] = (own * level * go_ref[...]).astype(BF16)
    nm_ref[HALF:, :] = (got * level * gg_ref[...]).astype(BF16)


def mlp_kernel(
    nm_ref, og_ref, wgo_ref, wgg_ref, wuo_ref, wug_ref, wdo_ref, wdg_ref,
    out_ref, gnm_ref, act_ref, gg_ref, gu_ref, out_sum, gnm_sum,
):
    step = pl.program_id(0)
    nm, og = nm_ref[...], og_ref[...]

    def inward(own_ref, got_ref, rows):
        return dot(own_ref[...], rows[:HALF], 0, 0) + dot(got_ref[...], rows[HALF:], 0, 0)

    @pl.when(step == 0)
    def _():
        out_sum[...] = jnp.zeros_like(out_sum)
        gnm_sum[...] = jnp.zeros_like(gnm_sum)

    gate = inward(wgo_ref, wgg_ref, nm)
    up = inward(wuo_ref, wug_ref, nm)
    grad_act = inward(wdo_ref, wdg_ref, og)
    sig = jax.nn.sigmoid(gate)
    silu = gate * sig
    act = (silu * up).astype(BF16)
    grad_gate = (grad_act * up * sig * (1.0 + gate * (1.0 - sig))).astype(BF16)
    grad_up = (grad_act * silu).astype(BF16)
    act_ref[...] = act
    gg_ref[...] = grad_gate
    gu_ref[...] = grad_up
    gnm_sum[:HALF, :] += dot(wgo_ref[...], grad_gate) + dot(wuo_ref[...], grad_up)
    gnm_sum[HALF:, :] += dot(wgg_ref[...], grad_gate) + dot(wug_ref[...], grad_up)
    out_sum[:HALF, :] += dot(wdo_ref[...], act)
    out_sum[HALF:, :] += dot(wdg_ref[...], act)

    @pl.when(step == pl.num_programs(0) - 1)
    def _():
        out_ref[...] = out_sum[...].astype(out_ref.dtype)
        gnm_ref[...] = gnm_sum[...].astype(gnm_ref.dtype)


def grads_kernel(row_counts, col_counts, rows_of, *refs):
    at = 0

    def whole_tokens(count):
        nonlocal at
        at += count
        return jnp.concatenate([ref[...] for ref in refs[at - count : at]], axis=1)

    rows = [whole_tokens(count) for count in row_counts]
    for kind, count in enumerate(col_counts):
        cols = whole_tokens(count)
        for half in range(2):
            left = rows[rows_of[kind]][half * HALF : (half + 1) * HALF]
            product = dot(left, cols, 1, 1).astype(BF16)
            out_ref = refs[len(refs) - 2 * len(col_counts) + 2 * kind + half]
            out_ref[:HALF, :] = product[:, :LANE]
            out_ref[HALF:, :] = product[:, LANE:]


def gain_rows(product):
    return lax.dot_general(
        jnp.ones((16, product.shape[1]), F32), product, (((1,), (1,)), ((), ())),
        precision=lax.Precision.HIGHEST, preferred_element_type=F32,
    )


def mid_back_kernel(
    og_ref, mid_ref, part_ref, back_ref, go_ref, gg_ref, no_ref, ng_ref, fo_ref, fg_ref,
    gmid_ref, gb_ref, near_ref, far_ref, ggain_ref,
):
    own, got = mid_ref[:HALF, :], mid_ref[HALF:, :]
    level = level_of(own, got)
    gnm = part_ref[...] + back_ref[...].astype(F32)
    scaled_own, scaled_got = gnm[:HALF] * go_ref[...], gnm[HALF:] * gg_ref[...]
    inner = jnp.sum(scaled_own * own, axis=0, keepdims=True)
    inner += jnp.sum(scaled_got * got, axis=0, keepdims=True)
    pull = level**3 * inner / D
    for rows, mid, scaled in (
        (slice(0, HALF), own, scaled_own), (slice(HALF, D), got, scaled_got)
    ):
        ggain_ref[rows.start // HALF] = gain_rows(gnm[rows] * mid * level)
        gmid = og_ref[rows, :].astype(F32) + scaled * level - mid * pull
        gmid_ref[rows, :] = gmid
        gb_ref[rows, :] = gmid.astype(BF16)
    gb_own, gb_got = gb_ref[:HALF, :], gb_ref[HALF:, :]
    near_ref[...] = (dot(no_ref[...], gb_own) + dot(ng_ref[...], gb_got)).astype(BF16)
    far_ref[...] = (dot(fo_ref[...], gb_own) + dot(fg_ref[...], gb_got)).astype(BF16)


def attend_back_kernel(
    where_ref, begin_ref, q_ref, ko_ref, vo_ref, kg_ref, vg_ref, gatt_ref, lse_ref,
    dq_ref, own_ref, got_ref, bias_ref, dk_ref, dv_ref,
):
    group = pl.program_id(0)
    live = group < where_ref[1]

    @pl.when(jnp.logical_not(live))
    def _():
        dq_ref[...] = jnp.zeros_like(dq_ref)
        own_ref[...] = jnp.zeros_like(own_ref)
        got_ref[...] = jnp.zeros_like(got_ref)

    for core in range(2):

        @pl.when(live & (where_ref[0] == core))
        def _():
            @pl.when(group == 0)
            def _():
                fill_bias(core, bias_ref, begin_ref)

            keys_t = laid(core, ko_ref[...], kg_ref[...], 1)
            keys = keys_t.T
            values = laid(core, vo_ref[...], vg_ref[...], 1).T
            dk_ref[...] = jnp.zeros_like(dk_ref)
            dv_ref[...] = jnp.zeros_like(dv_ref)
            for slot in range(2):
                cols = slice(slot * BLOCK, (slot + 1) * BLOCK)
                span = SPANS[core][slot] * BLOCK
                for j in range(GROUP):
                    heads = slice(j * HDIM, (j + 1) * HDIM)
                    queries, grads = q_ref[heads, cols], gatt_ref[heads, cols]
                    scores = dot(keys[:span], queries) + bias_ref[:span, cols]
                    probs = jnp.exp(scores - lse_ref[0, j : j + 1, cols])
                    dprobs = dot(values[:span], grads)
                    inner = jnp.sum(probs * dprobs, axis=0, keepdims=True)
                    dscores = (probs * (dprobs - inner)).astype(BF16)
                    dv_ref[:span, :] += dot(probs.astype(BF16), grads.T)
                    dk_ref[:span, :] += dot(dscores, queries.T)
                    dq_ref[heads, cols] = dot(keys_t[:, :span], dscores) * SCALE
            for kind, grad_ref in enumerate((dk_ref, dv_ref)):
                if core == 0:
                    own_ref[kind, 0] = grad_ref[:LOCAL, :].T
                    got_ref[kind, 0] = grad_ref[LOCAL:, :].T.astype(BF16)
                else:
                    own_ref[kind, 0] = grad_ref[BLOCK : BLOCK + LOCAL, :].T
                    got_ref[kind, 0, :, :BLOCK] = grad_ref[:BLOCK, :].T.astype(BF16)
                    got_ref[kind, 0, :, BLOCK:] = jnp.zeros((HDIM, BLOCK), BF16)


def turn_back(cos_ref, sin_ref, dq_ref, own_ref, got_ref, gj_ref):
    cosine, sine = cos_ref[...], sin_ref[...]

    def back(at, grad):
        low, high = grad[:ROT], grad[ROT:]
        gj_ref[at : at + ROT, :] = (low * cosine + high * sine).astype(BF16)
        gj_ref[at + ROT : at + HDIM, :] = (high * cosine - low * sine).astype(BF16)

    for at in range(0, QUERY, HDIM):
        back(at, dq_ref[at : at + HDIM, :])
    for g in range(GROUPS):
        back(QUERY + g * HDIM, own_ref[0, g] + got_ref[0, g].astype(F32))
        at = QUERY + KEY + g * HDIM
        gj_ref[at : at + HDIM, :] = (own_ref[1, g] + got_ref[1, g].astype(F32)).astype(BF16)


def joined_far_kernel(
    dq_ref, own_ref, got_ref, cos_ref, sin_ref, wo_ref, wg_ref, nm_ref,
    gnm_ref, keep_ref, send_ref, gj_ref,
):
    turn_back(cos_ref, sin_ref, dq_ref, own_ref, got_ref, gj_ref)
    gj = gj_ref[...]
    for half, out_ref in enumerate((keep_ref, send_ref)):
        rows = slice(half * HALF, (half + 1) * HALF)
        out_ref[:D, :HALF] = dot(gj, nm_ref[rows, :], 1, 1).astype(BF16)
        out_ref[D:, :] = jnp.zeros((ROWS - D, WIDE), BF16)
        out_ref[:D, HALF:] = jnp.zeros((D, WIDE - HALF), BF16)
    gnm_ref[:HALF, :] = dot(wo_ref[...], gj, 0, 0)
    gnm_ref[HALF:, :] = dot(wg_ref[...], gj, 0, 0)


def joined_near_kernel(
    dq_ref, own_ref, got_ref, cos_ref, sin_ref, wo_ref, wg_ref, nm_ref, part_ref, xo_ref, xg_ref,
    go_ref, gg_ref, gmid_ref, ggain_ref, keep_ref, send_ref, grad_ref, gj_ref,
):
    turn_back(cos_ref, sin_ref, dq_ref, own_ref, got_ref, gj_ref)
    gj = gj_ref[...]
    gnm_own = part_ref[:HALF, :] + dot(wo_ref[...], gj, 0, 0)
    gnm_got = part_ref[HALF:, :] + dot(wg_ref[...], gj, 0, 0)
    own, got = xo_ref[...].astype(F32), xg_ref[...].astype(F32)
    level = level_of(own, got)
    scaled_own, scaled_got = gnm_own * go_ref[...], gnm_got * gg_ref[...]
    inner = jnp.sum(scaled_own * own, axis=0, keepdims=True)
    inner += jnp.sum(scaled_got * got, axis=0, keepdims=True)
    pull = level**3 * inner / D
    for rows, x, gnm, scaled in (
        (slice(0, HALF), own, gnm_own, scaled_own), (slice(HALF, D), got, gnm_got, scaled_got)
    ):
        half = rows.start // HALF
        out_ref = (keep_ref, send_ref)[half]
        out_ref[:D, :HALF] = dot(gj, nm_ref[rows, :], 1, 1).astype(BF16)
        out_ref[D : D + 16, :HALF] = gain_rows(gnm * x * level).astype(BF16)
        out_ref[D + 16 : D + 32, :HALF] = ggain_ref[half].astype(BF16)
        out_ref[D + 32 :, :HALF] = jnp.zeros((ROWS - D - 32, HALF), BF16)
        out_ref[:, HALF:] = jnp.zeros((ROWS, WIDE - HALF), BF16)
        grad_ref[rows, :] = (gmid_ref[rows, :] + scaled * level - x * pull).astype(BF16)


def per_group(rows, at=0):
    return pl.BlockSpec((rows, LOCAL), lambda g: (g + at, 0))


LSE_SPEC = pl.BlockSpec((1, 8, LOCAL), lambda g: (g, 0, 0))
KV_SPECS = [per_group(HDIM), per_group(HDIM, GROUPS)] * 2
PAIR_SPEC = pl.BlockSpec((2, 1, HDIM, LOCAL), lambda g: (0, g, 0, 0))


def attend(where, begin, q, kv, kv_got, after=()):
    return run(
        attend_kernel,
        (where, begin, q, kv, kv, kv_got, kv_got),
        (shape((QUERY, LOCAL)), shape((GROUPS, 8, LOCAL), F32)),
        6e9,
        grid=(GROUPS,),
        in_specs=[SMEM_SPEC, whole((1, LOCAL)), per_group(GROUP * HDIM)] + KV_SPECS,
        out_specs=(per_group(GROUP * HDIM), LSE_SPEC),
        scratch=[pltpu.VMEM((MAXLEN, LOCAL), F32)],
        after=after,
    )


def attend_back(where, begin, q, kv, kv_got, gatt, lse, after=()):
    return run(
        attend_back_kernel,
        (where, begin, q, kv, kv, kv_got, kv_got, gatt, lse),
        (
            shape((QUERY, LOCAL), F32), shape((2, GROUPS, HDIM, LOCAL), F32),
            shape((2, GROUPS, HDIM, LOCAL)),
        ),
        14e9,
        grid=(GROUPS,),
        in_specs=[SMEM_SPEC, whole((1, LOCAL)), per_group(GROUP * HDIM)]
        + KV_SPECS
        + [per_group(GROUP * HDIM), LSE_SPEC],
        out_specs=(per_group(GROUP * HDIM), PAIR_SPEC, PAIR_SPEC),
        scratch=[
            pltpu.VMEM((MAXLEN, LOCAL), F32), pltpu.VMEM((MAXLEN, HDIM), F32),
            pltpu.VMEM((MAXLEN, HDIM), F32),
        ],
        after=after,
    )


def feed_forward(nm, og, weights, dtype, after=()):
    hidden = weights[0].shape[1]
    chunk = 2 * LANE
    cols = pl.BlockSpec((HALF, chunk), lambda i: (0, i))
    rows = pl.BlockSpec((chunk, LOCAL), lambda i: (i, 0))
    act = shape((hidden, LOCAL))
    return run(
        mlp_kernel,
        (nm, og) + weights,
        (shape((D, LOCAL), dtype), shape((D, LOCAL), dtype), act, act, act),
        12 * LOCAL * D * hidden,
        grid=(hidden // chunk,),
        in_specs=[whole((D, LOCAL))] * 2 + [cols] * 6,
        out_specs=(whole((D, LOCAL)), whole((D, LOCAL)), rows, rows, rows),
        scratch=[pltpu.VMEM((D, LOCAL), F32)] * 2,
        after=after,
    )


def weight_grads(rows, cols, rows_of, after=()):
    hidden = cols[0][0].shape[0]
    chunk = 2 * LANE
    all_rows, all_cols = sum(rows, ()), sum(cols, ())
    return run(
        functools.partial(
            grads_kernel, [len(pieces) for pieces in rows], [len(pieces) for pieces in cols], rows_of
        ),
        all_rows + all_cols,
        (shape((hidden // LANE * HALF, LANE)),) * (2 * len(cols)),
        4 * LOCAL * D * hidden * len(cols),
        grid=(hidden // chunk,),
        in_specs=[whole(part.shape) for part in all_rows]
        + [pl.BlockSpec((chunk, part.shape[1]), lambda i: (i, 0)) for part in all_cols],
        out_specs=(pl.BlockSpec((2 * HALF, LANE), lambda i: (i, 0)),) * (2 * len(cols)),
        after=after,
    )


def swap(array, axis):
    return lax.ppermute(array, axis, [(0, 1), (1, 0)])


def stages(count):
    found, stride = [], 1
    for size in (2,) + (4,) * 16:
        size = min(size, count // stride)
        if size < 2:
            break
        found.append((stride, size))
        stride *= size
    return found


def shift_pairs(count, stride, size, step):
    pairs = []
    for i in range(count):
        digit = i // stride % size
        pairs.append((i, i + ((digit + step) % size - digit) * stride))
    return pairs


def split_rows(array, count):
    rows, cols = array.shape
    sizes = [size for _, size in stages(count)]
    return array.reshape(*sizes[::-1], rows // count, cols)


def reduce_stage(total, count, stage, held=()):
    stride, size = stages(count)[stage]
    digit = lax.axis_index("dp") // stride % size
    axis = total.ndim - 3
    kept = lax.dynamic_index_in_dim(total, digit, axis, keepdims=False).astype(F32)
    found = []
    for step in range(1, size):
        sent = lax.dynamic_index_in_dim(total, (digit + step) % size, axis, keepdims=False)
        found.append(lax.ppermute(sent, "dp", shift_pairs(count, stride, size, step)))
    for got in hold_all(found, held):
        kept = kept + got.astype(F32)
    return kept.astype(BF16)


def reduce_first(array, count, held=()):
    return reduce_stage(split_rows(array, count), count, 0, held)


def reduce_rest(total, count, held=()):
    for stage in range(1, len(stages(count))):
        total = reduce_stage(total, count, stage, held)
    return total


def gather_stage(part, count, stage, held=()):
    stride, size = stages(count)[stage]
    digit = lax.axis_index("dp") // stride % size
    axis = part.ndim - 2
    found = [
        lax.ppermute(part, "dp", shift_pairs(count, stride, size, step)) for step in range(1, size)
    ]
    if size == 2:
        got = hold_all(found, held)[0]
        return jnp.stack(
            [jnp.where(digit == 0, part, got), jnp.where(digit == 0, got, part)], axis=axis
        )
    dims = part.shape[:axis] + (size,) + part.shape[axis:]
    whole_parts = lax.dynamic_update_index_in_dim(jnp.zeros(dims, BF16), part, digit, axis)
    for step, got in enumerate(hold_all(found, held), 1):
        whole_parts = lax.dynamic_update_index_in_dim(
            whole_parts, got, (digit - step) % size, axis
        )
    return whole_parts


def gather_rest(part, count, held=()):
    for stage in reversed(range(1, len(stages(count)))):
        part = gather_stage(part, count, stage, held)
    return part


def gather_first(part, count, held=()):
    return gather_stage(part, count, 0, held)


def spread(part):
    return lax.all_gather(part, "dp", axis=0, tiled=True)


def hold_all(arrays, others):
    if not others:
        return arrays
    return lax.optimization_barrier(tuple(arrays) + tuple(others))[: len(arrays)]


def hold(array, *others):
    return lax.optimization_barrier((array,) + others)[0]


def add(*parts):
    return sum(part.astype(F32) for part in parts).astype(BF16)


def segment_begin(segment):
    index = jnp.arange(segment.shape[0], dtype=jnp.int32)
    is_start = jnp.concatenate([jnp.ones((1,), dtype=bool), segment[1:] != segment[:-1]])
    return lax.cummax(jnp.where(is_start, index, jnp.zeros_like(index)), axis=0)


def rope_tables(position):
    frequency = ROPE_BASE ** (-(jnp.arange(ROT, dtype=F32) * 2.0 / HDIM))
    angles = frequency[:, None] * position.astype(F32)[None, :]
    return jnp.cos(angles), jnp.sin(angles)


def per_device(
    count,
    hidden_in,
    query_weight,
    key_weight,
    value_weight,
    output_weight,
    gate_weight,
    up_weight,
    down_weight,
    attn_gain,
    ffn_gain,
    out_grad,
    segment_ids,
):
    col, row = lax.axis_index("col"), lax.axis_index("row")
    first = col == 0

    def own_tokens(array):
        outer = jnp.concatenate([array[..., :BLOCK], array[..., 3 * BLOCK :]], axis=-1)
        inner = array[..., BLOCK : 3 * BLOCK]
        return jnp.where(first, outer, inner), jnp.where(first, inner, outer)

    def in_window(own, got):
        outer, inner = jnp.where(first, own, got), jnp.where(first, got, own)
        return jnp.concatenate([outer[:, :BLOCK], inner, outer[:, BLOCK:]], axis=1)

    w_near = jnp.concatenate(
        [query_weight[:, 0].T, key_weight[:, 0].T, value_weight[:, 0].T], axis=0
    )
    w_far = swap(w_near, "row")
    wo_near = output_weight[0]
    wo_far = swap(wo_near, "row")
    x_own, x_other = own_tokens(hidden_in.T)
    x_got = swap(x_other, "col")
    gains = jnp.stack([attn_gain, ffn_gain])
    gains_got = swap(gains, "col").astype(F32)
    gains = gains.astype(F32)
    gin_own, gmid_own = gains[0][:, None], gains[1][:, None]
    gin_got, gmid_got = gains_got[0][:, None], gains_got[1][:, None]
    segment = jnp.where(col == row, segment_ids, swap(segment_ids, "col"))
    begin, _ = own_tokens(segment_begin(segment))
    index, _ = own_tokens(jnp.arange(MAXLEN, dtype=jnp.int32))
    cosine, sine = rope_tables(index - begin)
    begin = begin[None]
    live_near = jnp.where(row == 0, LIVE[0], LIVE[1])
    where_near = jnp.stack([col, live_near]).astype(jnp.int32)
    where_far = jnp.stack([col, LIVE[0] + LIVE[1] - live_near]).astype(jnp.int32)

    w_near_got = swap(w_near, "col")
    heads = (shape((QUERY, LOCAL)), shape((2 * KEY, LOCAL)))
    nm_in, q_near, kv_near = run(
        project_near_kernel,
        (x_own, x_got, gin_own, gin_got, cosine, sine, w_near, w_near_got),
        (shape((D, LOCAL)),) + heads,
        2 * LOCAL * D * D,
    )
    kv_near_got = swap(kv_near, "col")
    wo_near_got = swap(wo_near, "col")
    att_near, lse_near = attend(where_near, begin, q_near, kv_near, kv_near_got)
    w_far_got = swap(hold(w_far, lse_near), "col")
    q_far, kv_far = run(
        project_far_kernel,
        (nm_in, cosine, sine, w_far, w_far_got),
        heads,
        2 * LOCAL * D * D,
    )
    kv_far_got = swap(kv_far, "col")
    att_far, lse_far = attend(where_far, begin, q_far, kv_far, kv_far_got)
    wo_far_got = swap(hold(wo_far, kv_far), "col")
    og_own, og_other = own_tokens(out_grad.T)
    og = jnp.concatenate([og_own, swap(og_other, "col")], axis=0)
    og_far = swap(og, "row")
    mid, nm = run(
        mid_kernel,
        (
            att_near, att_far, wo_near, wo_near_got, wo_far, wo_far_got, x_own, x_got,
            gmid_own, gmid_got,
        ),
        (shape((D, LOCAL), F32), shape((D, LOCAL))),
        2 * LOCAL * D * D,
    )

    mlp_weights = ()
    for weight in (gate_weight, up_weight, down_weight.T):
        mlp_weights += (weight, swap(weight, "col"))
    nm_far = swap(nm, "row")
    out_part, gnm_part, act, gg, gu = feed_forward(nm, og, mlp_weights, F32, after=(og_far,))
    out_send, gnm_send, act_far, gg_far, gu_far = feed_forward(
        nm_far, og_far, mlp_weights, BF16, after=(act,)
    )
    gnm_back = swap(gnm_send, "row")
    down_keep, down_send = weight_grads(((og, og_far),), ((act, act_far),), (0,))
    down_got = swap(down_send, "col")
    gate_keep, gate_send, up_keep, up_send = weight_grads(
        ((nm, nm_far),), ((gg, gg_far), (gu, gu_far)), (0, 0), after=(down_keep,)
    )
    down_sum = add(down_keep, hold(down_got, gate_keep))
    gate_send, up_send = hold_all((gate_send, up_send), (gnm_back,))

    gmid, gb, gatt_near, gatt_far, ggain_mid = run(
        mid_back_kernel,
        (
            og, mid, gnm_part, gnm_back, gmid_own, gmid_got, wo_near, wo_near_got, wo_far,
            wo_far_got,
        ),
        (
            shape((D, LOCAL), F32), shape((D, LOCAL)), shape((QUERY, LOCAL)),
            shape((QUERY, LOCAL)), shape((2, 16, HALF), F32),
        ),
        2 * LOCAL * D * D,
        after=(down_sum,),
    )
    down_x = reduce_first(down_sum, count, (ggain_mid,))
    gate_sum = add(gate_keep, hold(swap(gate_send, "col"), ggain_mid))
    up_sum = add(up_keep, hold(swap(up_send, "col"), ggain_mid))

    def out_grads(att):
        send = dot(att, gb[HALF:], 1, 1).astype(BF16)
        return add(dot(att, gb[:HALF], 1, 1), swap(send, "col"))

    wo_far_sum = out_grads(att_far)
    wo_near_sum = out_grads(att_near)

    dq_far, own_far, other_far = attend_back(
        where_far, begin, q_far, kv_far, kv_far_got, gatt_far, lse_far, after=(down_x, gate_sum, up_sum)
    )
    gate_x = reduce_first(gate_sum, count, (dq_far,))
    down_z = reduce_rest(down_x, count, (dq_far,))

    got_far = swap(hold(other_far, gate_x, down_z), "col")
    joined = shape((ROWS, WIDE))
    gnm_in_part, far_keep, far_send = run(
        joined_far_kernel,
        (dq_far, own_far, got_far, cosine, sine, w_far, w_far_got, nm_in),
        (shape((D, LOCAL), F32), joined, joined),
        4 * LOCAL * D * D,
        after=(gate_x,),
        scratch=[pltpu.VMEM((D, LOCAL), BF16)],
    )
    gate_z = reduce_rest(gate_x, count, (far_keep,))
    up_x = reduce_first(hold(up_sum, gate_x), count, (far_keep,))
    wo_sum = add(wo_near_sum, swap(wo_far_sum, "row"))
    wo_sum = jnp.pad(wo_sum, ((0, 0), (0, WIDE - HALF)))
    dq_near, own_near, other_near = attend_back(
        where_near, begin, q_near, kv_near, kv_near_got, gatt_near, lse_near, after=(gate_z, up_x, wo_far_sum, wo_near_sum)
    )
    far_sum = add(far_keep, hold(swap(hold(far_send, gate_z, up_x), "col"), dq_near))
    got_near = swap(hold(other_near, far_sum, wo_sum), "col")
    near_keep, near_send, grad = run(
        joined_near_kernel,
        (
            dq_near, own_near, got_near, cosine, sine, w_near, w_near_got, nm_in, gnm_in_part,
            x_own, x_got, gin_own, gin_got, gmid, ggain_mid,
        ),
        (joined, joined, shape((D, LOCAL))),
        4 * LOCAL * D * D,
        scratch=[pltpu.VMEM((D, LOCAL), BF16)],
    )
    up_z = reduce_rest(up_x, count, (grad,))
    far_back = swap(far_sum, "row")
    last_sum = add(near_keep, swap(hold(near_send, far_back, up_z), "col"), far_back)

    def feature_cols(array):
        return in_window(array[:HALF], swap(array[HALF:], "col")).T


    def widened(whole_sum):
        parts = whole_sum.reshape(-1, HALF, LANE)
        return parts.transpose(1, 0, 2).reshape(HALF, -1).astype(F32)

    last_x = reduce_first(last_sum, count)
    out_x = reduce_first(wo_sum, count)
    last_z = reduce_rest(jnp.concatenate([last_x, out_x], axis=-2), count)
    out_back = hold(swap(hold(out_send, gnm_back), "row"), last_z)
    block_out = feature_cols((mid + out_part + out_back.astype(F32)).astype(BF16))
    input_grad = feature_cols(hold(grad, last_x))
    down_grad = widened(hold(spread(down_z), last_x))
    gate_grad = widened(hold(spread(gate_z), last_x))
    up_rest = gather_rest(up_z, count, (last_x,))
    up_grad = widened(gather_first(up_rest, count, (last_z,)).reshape(up_sum.shape))
    last = gather_first(gather_rest(last_z, count), count)
    last, out_weight_grad = last[..., : ROWS // count, :], last[..., ROWS // count :, :]
    last = last.reshape(last_sum.shape)[:, :HALF].astype(F32)
    out_weight_grad = out_weight_grad.reshape(wo_sum.shape)[:, :HALF].astype(F32)
    gain_grads = jnp.stack([last[D], last[D + 16]])
    gain_grads = gain_grads + swap(gain_grads, "row")
    return (
        block_out,
        input_grad,
        last[:QUERY].T[:, None, :],
        last[QUERY : QUERY + KEY].T[:, None, :],
        last[QUERY + KEY : D].T[:, None, :],
        out_weight_grad[None],
        gate_grad,
        up_grad,
        down_grad.T,
        gain_grads[0],
        gain_grads[1],
    )


def solution(mesh):
    return jax.shard_map(
        functools.partial(per_device, mesh.shape["dp"]),
        mesh=mesh,
        in_specs=(
            P(("dp", "row"), "col"),
            P("col", "row", None),
            P("col", "row", None),
            P("col", "row", None),
            P("row", None, "col"),
            P("col", "row"),
            P("col", "row"),
            P("row", "col"),
            P("col"),
            P("col"),
            P(("dp", "row"), "col"),
            P(("dp", "col")),
        ),
        out_specs=(
            P(("dp", "row"), "col"),
            P(("dp", "row"), "col"),
            P("col", "row", None),
            P("col", "row", None),
            P("col", "row", None),
            P("row", None, "col"),
            P("col", "row"),
            P("col", "row"),
            P("row", "col"),
            P("col"),
            P("col"),
        ),
        check_vma=False,
    )
```

```python
import functools
import math

import jax
import jax.numpy as jnp
from jax import lax
from jax.experimental import pallas as pl
from jax.experimental.pallas import tpu as pltpu
from jax.sharding import PartitionSpec as P

D = 960
HALF = D // 2
HDIM = 64
ROT = HDIM // 2
GROUP = 3
GROUPS = 3
QUERY = GROUPS * GROUP * HDIM
KEY = GROUPS * HDIM
MAXLEN = 1024
BLOCK = MAXLEN // 4
LOCAL = 2 * BLOCK
LANE = 128
LIVE = (3, 2)
ROWS = 1024
WIDE = 512

NORM_EPS = 1e-05
ROPE_BASE = 100000.0
MASKED_SCORE = -1e30
SCALE = 1.0 / math.sqrt(HDIM)
BF16 = jnp.bfloat16
F32 = jnp.float32
VMEM_BYTES = 56 * 1024 * 1024
COST = 0.03

HELD = ((0, 3), (1, 2))
LAID = ((0, 3, 1, 2), (0, 1, 2))
SPANS = ((1, 4), (2, 3))


def dot(left, right, left_dim=1, right_dim=0):
    return lax.dot_general(
        left, right, (((left_dim,), (right_dim,)), ((), ())), preferred_element_type=F32
    )


def shape(dims, dtype=BF16):
    return jax.ShapeDtypeStruct(dims, dtype)


def whole(dims):
    return pl.BlockSpec(dims, lambda *_: (0,) * len(dims))


SMEM_SPEC = pl.BlockSpec(memory_space=pltpu.SMEM)


def run(kernel, ins, outs, flops, grid=None, in_specs=None, out_specs=None, scratch=(), after=()):
    moved = sum(a.size * a.dtype.itemsize for a in ins)
    moved += sum(math.prod(o.shape) * jnp.dtype(o.dtype).itemsize for o in outs)
    if in_specs is None:
        in_specs = [whole(a.shape) for a in ins]
    if out_specs is None:
        out_specs = [whole(o.shape) for o in outs]
    count = len(ins)

    def body(*refs):
        kernel(*refs[:count], *refs[count + len(after) :])

    return pl.pallas_call(
        body,
        grid=grid if grid is not None else (1,),
        in_specs=list(in_specs) + [pl.BlockSpec(memory_space=pl.ANY)] * len(after),
        out_specs=tuple(out_specs),
        out_shape=tuple(outs),
        scratch_shapes=list(scratch),
        compiler_params=pltpu.CompilerParams(vmem_limit_bytes=VMEM_BYTES),
        cost_estimate=pl.CostEstimate(
            flops=int(flops * COST), bytes_accessed=int(moved * COST), transcendentals=0
        ),
    )(*ins, *after)


def level_of(own, got):
    total = jnp.sum(own * own, axis=0, keepdims=True) + jnp.sum(got * got, axis=0, keepdims=True)
    return lax.rsqrt(total / D + NORM_EPS)


def project_heads(nm, cos_ref, sin_ref, own_ref, got_ref, q_ref, kv_ref):
    cosine, sine = cos_ref[...], sin_ref[...]
    joined = dot(own_ref[...], nm[:HALF]) + dot(got_ref[...], nm[HALF:])
    for at in range(0, QUERY + KEY, HDIM):
        low, high = joined[at : at + ROT], joined[at + ROT : at + HDIM]
        parts = (low * cosine - high * sine, high * cosine + low * sine)
        for part, turned in enumerate(parts):
            turned = turned.astype(BF16)
            if at < QUERY:
                turned = (turned.astype(F32) * SCALE).astype(BF16)
                q_ref[at + part * ROT : at + (part + 1) * ROT, :] = turned
            else:
                row = at - QUERY + part * ROT
                kv_ref[row : row + ROT, :] = turned
    kv_ref[KEY:, :] = joined[QUERY + KEY :].astype(BF16)


def project_near_kernel(
    xo_ref, xg_ref, go_ref, gg_ref, cos_ref, sin_ref, own_ref, got_ref, nm_ref, q_ref, kv_ref
):
    own, got = xo_ref[...].astype(F32), xg_ref[...].astype(F32)
    level = level_of(own, got)
    nm_ref[:HALF, :] = (own * level * go_ref[...]).astype(BF16)
    nm_ref[HALF:, :] = (got * level * gg_ref[...]).astype(BF16)
    project_heads(nm_ref[...], cos_ref, sin_ref, own_ref, got_ref, q_ref, kv_ref)


def project_far_kernel(nm_ref, cos_ref, sin_ref, own_ref, got_ref, q_ref, kv_ref):
    project_heads(nm_ref[...], cos_ref, sin_ref, own_ref, got_ref, q_ref, kv_ref)


def laid(core, own, got, axis):
    if core == 0:
        return jnp.concatenate([own, got], axis=axis)
    return jnp.concatenate([lax.slice_in_dim(got, 0, BLOCK, axis=axis), own], axis=axis)


def fill_bias(core, bias_ref, begin_ref):
    for at, block in enumerate(LAID[core]):
        for slot in range(2):
            cols = slice(slot * BLOCK, (slot + 1) * BLOCK)
            key = block * BLOCK + lax.broadcasted_iota(jnp.int32, (BLOCK, BLOCK), 0)
            query = HELD[core][slot] * BLOCK + lax.broadcasted_iota(jnp.int32, (BLOCK, BLOCK), 1)
            allowed = (key >= begin_ref[:, cols]) & (key <= query)
            bias_ref[at * BLOCK : (at + 1) * BLOCK, cols] = jnp.where(allowed, 0.0, MASKED_SCORE)


def attend_kernel(
    where_ref, begin_ref, q_ref, ko_ref, vo_ref, kg_ref, vg_ref, att_ref, lse_ref, bias_ref
):
    group = pl.program_id(0)
    live = group < where_ref[1]

    @pl.when(jnp.logical_not(live))
    def _():
        att_ref[...] = jnp.zeros_like(att_ref)
        lse_ref[...] = jnp.zeros_like(lse_ref)

    for core in range(2):

        @pl.when(live & (where_ref[0] == core))
        def _():
            @pl.when(group == 0)
            def _():
                fill_bias(core, bias_ref, begin_ref)

            keys = laid(core, ko_ref[...], kg_ref[...], 1).T
            values = laid(core, vo_ref[...], vg_ref[...], 1)
            for slot in range(2):
                cols = slice(slot * BLOCK, (slot + 1) * BLOCK)
                span = SPANS[core][slot] * BLOCK
                for j in range(GROUP):
                    heads = slice(j * HDIM, (j + 1) * HDIM)
                    scores = dot(keys[:span], q_ref[heads, cols]) + bias_ref[:span, cols]
                    highest = jnp.max(scores, axis=0, keepdims=True)
                    weights = jnp.exp(scores - highest)
                    total = jnp.sum(weights, axis=0, keepdims=True)
                    mixed = dot(values[:, :span], weights.astype(BF16)) / total
                    att_ref[heads, cols] = mixed.astype(BF16)
                    lse_ref[0, j : j + 1, cols] = highest + jnp.log(total)


def mid_kernel(
    near_ref, far_ref, no_ref, ng_ref, fo_ref, fg_ref, xo_ref, xg_ref, go_ref, gg_ref,
    mid_ref, nm_ref,
):
    near, far = near_ref[...], far_ref[...]
    own = xo_ref[...].astype(F32) + dot(no_ref[...], near, 0, 0) + dot(fo_ref[...], far, 0, 0)
    got = xg_ref[...].astype(F32) + dot(ng_ref[...], near, 0, 0) + dot(fg_ref[...], far, 0, 0)
    mid_ref[:HALF, :] = own
    mid_ref[HALF:, :] = got
    level = level_of(own, got)
    nm_ref[:HALF, :] = (own * level * go_ref[...]).astype(BF16)
    nm_ref[HALF:, :] = (got * level * gg_ref[...]).astype(BF16)


def mlp_kernel(
    nm_ref, og_ref, wgo_ref, wgg_ref, wuo_ref, wug_ref, wdo_ref, wdg_ref,
    out_ref, gnm_ref, act_ref, gg_ref, gu_ref, out_sum, gnm_sum,
):
    step = pl.program_id(0)
    nm, og = nm_ref[...], og_ref[...]

    def inward(own_ref, got_ref, rows):
        return dot(own_ref[...], rows[:HALF], 0, 0) + dot(got_ref[...], rows[HALF:], 0, 0)

    @pl.when(step == 0)
    def _():
        out_sum[...] = jnp.zeros_like(out_sum)
        gnm_sum[...] = jnp.zeros_like(gnm_sum)

    gate = inward(wgo_ref, wgg_ref, nm)
    up = inward(wuo_ref, wug_ref, nm)
    grad_act = inward(wdo_ref, wdg_ref, og)
    sig = jax.nn.sigmoid(gate)
    silu = gate * sig
    act = (silu * up).astype(BF16)
    grad_gate = (grad_act * up * sig * (1.0 + gate * (1.0 - sig))).astype(BF16)
    grad_up = (grad_act * silu).astype(BF16)
    act_ref[...] = act
    gg_ref[...] = grad_gate
    gu_ref[...] = grad_up
    gnm_sum[:HALF, :] += dot(wgo_ref[...], grad_gate) + dot(wuo_ref[...], grad_up)
    gnm_sum[HALF:, :] += dot(wgg_ref[...], grad_gate) + dot(wug_ref[...], grad_up)
    out_sum[:HALF, :] += dot(wdo_ref[...], act)
    out_sum[HALF:, :] += dot(wdg_ref[...], act)

    @pl.when(step == pl.num_programs(0) - 1)
    def _():
        out_ref[...] = out_sum[...].astype(out_ref.dtype)
        gnm_ref[...] = gnm_sum[...].astype(gnm_ref.dtype)


def grads_kernel(row_counts, col_counts, rows_of, *refs):
    at = 0

    def whole_tokens(count):
        nonlocal at
        at += count
        return jnp.concatenate([ref[...] for ref in refs[at - count : at]], axis=1)

    rows = [whole_tokens(count) for count in row_counts]
    for kind, count in enumerate(col_counts):
        cols = whole_tokens(count)
        for half in range(2):
            left = rows[rows_of[kind]][half * HALF : (half + 1) * HALF]
            product = dot(left, cols, 1, 1).astype(BF16)
            out_ref = refs[len(refs) - 2 * len(col_counts) + 2 * kind + half]
            out_ref[:HALF, :] = product[:, :LANE]
            out_ref[HALF:, :] = product[:, LANE:]


def gain_rows(product):
    return lax.dot_general(
        jnp.ones((16, product.shape[1]), F32), product, (((1,), (1,)), ((), ())),
        precision=lax.Precision.HIGHEST, preferred_element_type=F32,
    )


def mid_back_kernel(
    og_ref, mid_ref, part_ref, back_ref, go_ref, gg_ref, no_ref, ng_ref, fo_ref, fg_ref,
    gmid_ref, gb_ref, near_ref, far_ref, ggain_ref,
):
    own, got = mid_ref[:HALF, :], mid_ref[HALF:, :]
    level = level_of(own, got)
    gnm = part_ref[...] + back_ref[...].astype(F32)
    scaled_own, scaled_got = gnm[:HALF] * go_ref[...], gnm[HALF:] * gg_ref[...]
    inner = jnp.sum(scaled_own * own, axis=0, keepdims=True)
    inner += jnp.sum(scaled_got * got, axis=0, keepdims=True)
    pull = level**3 * inner / D
    for rows, mid, scaled in (
        (slice(0, HALF), own, scaled_own), (slice(HALF, D), got, scaled_got)
    ):
        ggain_ref[rows.start // HALF] = gain_rows(gnm[rows] * mid * level)
        gmid = og_ref[rows, :].astype(F32) + scaled * level - mid * pull
        gmid_ref[rows, :] = gmid
        gb_ref[rows, :] = gmid.astype(BF16)
    gb_own, gb_got = gb_ref[:HALF, :], gb_ref[HALF:, :]
    near_ref[...] = (dot(no_ref[...], gb_own) + dot(ng_ref[...], gb_got)).astype(BF16)
    far_ref[...] = (dot(fo_ref[...], gb_own) + dot(fg_ref[...], gb_got)).astype(BF16)


def attend_back_kernel(
    where_ref, begin_ref, q_ref, ko_ref, vo_ref, kg_ref, vg_ref, gatt_ref, lse_ref,
    dq_ref, own_ref, got_ref, bias_ref, dk_ref, dv_ref,
):
    group = pl.program_id(0)
    live = group < where_ref[1]

    @pl.when(jnp.logical_not(live))
    def _():
        dq_ref[...] = jnp.zeros_like(dq_ref)
        own_ref[...] = jnp.zeros_like(own_ref)
        got_ref[...] = jnp.zeros_like(got_ref)

    for core in range(2):

        @pl.when(live & (where_ref[0] == core))
        def _():
            @pl.when(group == 0)
            def _():
                fill_bias(core, bias_ref, begin_ref)

            keys_t = laid(core, ko_ref[...], kg_ref[...], 1)
            keys = keys_t.T
            values = laid(core, vo_ref[...], vg_ref[...], 1).T
            dk_ref[...] = jnp.zeros_like(dk_ref)
            dv_ref[...] = jnp.zeros_like(dv_ref)
            for slot in range(2):
                cols = slice(slot * BLOCK, (slot + 1) * BLOCK)
                span = SPANS[core][slot] * BLOCK
                for j in range(GROUP):
                    heads = slice(j * HDIM, (j + 1) * HDIM)
                    queries, grads = q_ref[heads, cols], gatt_ref[heads, cols]
                    scores = dot(keys[:span], queries) + bias_ref[:span, cols]
                    probs = jnp.exp(scores - lse_ref[0, j : j + 1, cols])
                    dprobs = dot(values[:span], grads)
                    inner = jnp.sum(probs * dprobs, axis=0, keepdims=True)
                    dscores = (probs * (dprobs - inner)).astype(BF16)
                    dv_ref[:span, :] += dot(probs.astype(BF16), grads.T)
                    dk_ref[:span, :] += dot(dscores, queries.T)
                    dq_ref[heads, cols] = dot(keys_t[:, :span], dscores) * SCALE
            for kind, grad_ref in enumerate((dk_ref, dv_ref)):
                if core == 0:
                    own_ref[kind, 0] = grad_ref[:LOCAL, :].T
                    got_ref[kind, 0] = grad_ref[LOCAL:, :].T.astype(BF16)
                else:
                    own_ref[kind, 0] = grad_ref[BLOCK : BLOCK + LOCAL, :].T
                    got_ref[kind, 0, :, :BLOCK] = grad_ref[:BLOCK, :].T.astype(BF16)
                    got_ref[kind, 0, :, BLOCK:] = jnp.zeros((HDIM, BLOCK), BF16)


def turn_back(cos_ref, sin_ref, dq_ref, own_ref, got_ref, gj_ref):
    cosine, sine = cos_ref[...], sin_ref[...]

    def back(at, grad):
        low, high = grad[:ROT], grad[ROT:]
        gj_ref[at : at + ROT, :] = (low * cosine + high * sine).astype(BF16)
        gj_ref[at + ROT : at + HDIM, :] = (high * cosine - low * sine).astype(BF16)

    for at in range(0, QUERY, HDIM):
        back(at, dq_ref[at : at + HDIM, :])
    for g in range(GROUPS):
        back(QUERY + g * HDIM, own_ref[0, g] + got_ref[0, g].astype(F32))
        at = QUERY + KEY + g * HDIM
        gj_ref[at : at + HDIM, :] = (own_ref[1, g] + got_ref[1, g].astype(F32)).astype(BF16)


def joined_far_kernel(
    dq_ref, own_ref, got_ref, cos_ref, sin_ref, wo_ref, wg_ref, nm_ref,
    gnm_ref, keep_ref, send_ref, gj_ref,
):
    turn_back(cos_ref, sin_ref, dq_ref, own_ref, got_ref, gj_ref)
    gj = gj_ref[...]
    for half, out_ref in enumerate((keep_ref, send_ref)):
        rows = slice(half * HALF, (half + 1) * HALF)
        out_ref[:D, :HALF] = dot(gj, nm_ref[rows, :], 1, 1).astype(BF16)
        out_ref[D:, :] = jnp.zeros((ROWS - D, WIDE), BF16)
        out_ref[:D, HALF:] = jnp.zeros((D, WIDE - HALF), BF16)
    gnm_ref[:HALF, :] = dot(wo_ref[...], gj, 0, 0)
    gnm_ref[HALF:, :] = dot(wg_ref[...], gj, 0, 0)


def joined_near_kernel(
    dq_ref, own_ref, got_ref, cos_ref, sin_ref, wo_ref, wg_ref, nm_ref, part_ref, xo_ref, xg_ref,
    go_ref, gg_ref, gmid_ref, ggain_ref, keep_ref, send_ref, grad_ref, gj_ref,
):
    turn_back(cos_ref, sin_ref, dq_ref, own_ref, got_ref, gj_ref)
    gj = gj_ref[...]
    gnm_own = part_ref[:HALF, :] + dot(wo_ref[...], gj, 0, 0)
    gnm_got = part_ref[HALF:, :] + dot(wg_ref[...], gj, 0, 0)
    own, got = xo_ref[...].astype(F32), xg_ref[...].astype(F32)
    level = level_of(own, got)
    scaled_own, scaled_got = gnm_own * go_ref[...], gnm_got * gg_ref[...]
    inner = jnp.sum(scaled_own * own, axis=0, keepdims=True)
    inner += jnp.sum(scaled_got * got, axis=0, keepdims=True)
    pull = level**3 * inner / D
    for rows, x, gnm, scaled in (
        (slice(0, HALF), own, gnm_own, scaled_own), (slice(HALF, D), got, gnm_got, scaled_got)
    ):
        half = rows.start // HALF
        out_ref = (keep_ref, send_ref)[half]
        out_ref[:D, :HALF] = dot(gj, nm_ref[rows, :], 1, 1).astype(BF16)
        out_ref[D : D + 16, :HALF] = gain_rows(gnm * x * level).astype(BF16)
        out_ref[D + 16 : D + 32, :HALF] = ggain_ref[half].astype(BF16)
        out_ref[D + 32 :, :HALF] = jnp.zeros((ROWS - D - 32, HALF), BF16)
        out_ref[:, HALF:] = jnp.zeros((ROWS, WIDE - HALF), BF16)
        grad_ref[rows, :] = (gmid_ref[rows, :] + scaled * level - x * pull).astype(BF16)


def per_group(rows, at=0):
    return pl.BlockSpec((rows, LOCAL), lambda g: (g + at, 0))


LSE_SPEC = pl.BlockSpec((1, 8, LOCAL), lambda g: (g, 0, 0))
KV_SPECS = [per_group(HDIM), per_group(HDIM, GROUPS)] * 2
PAIR_SPEC = pl.BlockSpec((2, 1, HDIM, LOCAL), lambda g: (0, g, 0, 0))


def attend(where, begin, q, kv, kv_got, after=()):
    return run(
        attend_kernel,
        (where, begin, q, kv, kv, kv_got, kv_got),
        (shape((QUERY, LOCAL)), shape((GROUPS, 8, LOCAL), F32)),
        6e9,
        grid=(GROUPS,),
        in_specs=[SMEM_SPEC, whole((1, LOCAL)), per_group(GROUP * HDIM)] + KV_SPECS,
        out_specs=(per_group(GROUP * HDIM), LSE_SPEC),
        scratch=[pltpu.VMEM((MAXLEN, LOCAL), F32)],
        after=after,
    )


def attend_back(where, begin, q, kv, kv_got, gatt, lse, after=()):
    return run(
        attend_back_kernel,
        (where, begin, q, kv, kv, kv_got, kv_got, gatt, lse),
        (
            shape((QUERY, LOCAL), F32), shape((2, GROUPS, HDIM, LOCAL), F32),
            shape((2, GROUPS, HDIM, LOCAL)),
        ),
        14e9,
        grid=(GROUPS,),
        in_specs=[SMEM_SPEC, whole((1, LOCAL)), per_group(GROUP * HDIM)]
        + KV_SPECS
        + [per_group(GROUP * HDIM), LSE_SPEC],
        out_specs=(per_group(GROUP * HDIM), PAIR_SPEC, PAIR_SPEC),
        scratch=[
            pltpu.VMEM((MAXLEN, LOCAL), F32), pltpu.VMEM((MAXLEN, HDIM), F32),
            pltpu.VMEM((MAXLEN, HDIM), F32),
        ],
        after=after,
    )


def feed_forward(nm, og, weights, dtype, after=()):
    hidden = weights[0].shape[1]
    chunk = 2 * LANE
    cols = pl.BlockSpec((HALF, chunk), lambda i: (0, i))
    rows = pl.BlockSpec((chunk, LOCAL), lambda i: (i, 0))
    act = shape((hidden, LOCAL))
    return run(
        mlp_kernel,
        (nm, og) + weights,
        (shape((D, LOCAL), dtype), shape((D, LOCAL), dtype), act, act, act),
        12 * LOCAL * D * hidden,
        grid=(hidden // chunk,),
        in_specs=[whole((D, LOCAL))] * 2 + [cols] * 6,
        out_specs=(whole((D, LOCAL)), whole((D, LOCAL)), rows, rows, rows),
        scratch=[pltpu.VMEM((D, LOCAL), F32)] * 2,
        after=after,
    )


def weight_grads(rows, cols, rows_of, after=()):
    hidden = cols[0][0].shape[0]
    chunk = 2 * LANE
    all_rows, all_cols = sum(rows, ()), sum(cols, ())
    return run(
        functools.partial(
            grads_kernel, [len(pieces) for pieces in rows], [len(pieces) for pieces in cols], rows_of
        ),
        all_rows + all_cols,
        (shape((hidden // LANE * HALF, LANE)),) * (2 * len(cols)),
        4 * LOCAL * D * hidden * len(cols),
        grid=(hidden // chunk,),
        in_specs=[whole(part.shape) for part in all_rows]
        + [pl.BlockSpec((chunk, part.shape[1]), lambda i: (i, 0)) for part in all_cols],
        out_specs=(pl.BlockSpec((2 * HALF, LANE), lambda i: (i, 0)),) * (2 * len(cols)),
        after=after,
    )


def swap(array, axis):
    return lax.ppermute(array, axis, [(0, 1), (1, 0)])


def stages(count):
    found, stride = [], 1
    for size in (2,) + (4,) * 16:
        size = min(size, count // stride)
        if size < 2:
            break
        found.append((stride, size))
        stride *= size
    return found


def shift_pairs(count, stride, size, step):
    pairs = []
    for i in range(count):
        digit = i // stride % size
        pairs.append((i, i + ((digit + step) % size - digit) * stride))
    return pairs


def split_rows(array, count):
    rows, cols = array.shape
    sizes = [size for _, size in stages(count)]
    return array.reshape(*sizes[::-1], rows // count, cols)


def reduce_stage(total, count, stage, held=()):
    stride, size = stages(count)[stage]
    digit = lax.axis_index("dp") // stride % size
    axis = total.ndim - 3
    kept = lax.dynamic_index_in_dim(total, digit, axis, keepdims=False).astype(F32)
    found = []
    for step in range(1, size):
        sent = lax.dynamic_index_in_dim(total, (digit + step) % size, axis, keepdims=False)
        found.append(lax.ppermute(sent, "dp", shift_pairs(count, stride, size, step)))
    for got in hold_all(found, held):
        kept = kept + got.astype(F32)
    return kept.astype(BF16)


def reduce_first(array, count, held=()):
    return reduce_stage(split_rows(array, count), count, 0, held)


def reduce_rest(total, count, held=()):
    for stage in range(1, len(stages(count))):
        total = reduce_stage(total, count, stage, held)
    return total


def gather_stage(part, count, stage, held=()):
    stride, size = stages(count)[stage]
    digit = lax.axis_index("dp") // stride % size
    axis = part.ndim - 2
    found = [
        lax.ppermute(part, "dp", shift_pairs(count, stride, size, step)) for step in range(1, size)
    ]
    if size == 2:
        got = hold_all(found, held)[0]
        return jnp.stack(
            [jnp.where(digit == 0, part, got), jnp.where(digit == 0, got, part)], axis=axis
        )
    dims = part.shape[:axis] + (size,) + part.shape[axis:]
    whole_parts = lax.dynamic_update_index_in_dim(jnp.zeros(dims, BF16), part, digit, axis)
    for step, got in enumerate(hold_all(found, held), 1):
        whole_parts = lax.dynamic_update_index_in_dim(
            whole_parts, got, (digit - step) % size, axis
        )
    return whole_parts


def gather_rest(part, count, held=()):
    for stage in reversed(range(1, len(stages(count)))):
        part = gather_stage(part, count, stage, held)
    return part


def gather_first(part, count, held=()):
    return gather_stage(part, count, 0, held)


def spread(part):
    return lax.all_gather(part, "dp", axis=0, tiled=True)


def hold_all(arrays, others):
    if not others:
        return arrays
    return lax.optimization_barrier(tuple(arrays) + tuple(others))[: len(arrays)]


def hold(array, *others):
    return lax.optimization_barrier((array,) + others)[0]


def add(*parts):
    return sum(part.astype(F32) for part in parts).astype(BF16)


def segment_begin(segment):
    index = jnp.arange(segment.shape[0], dtype=jnp.int32)
    is_start = jnp.concatenate([jnp.ones((1,), dtype=bool), segment[1:] != segment[:-1]])
    return lax.cummax(jnp.where(is_start, index, jnp.zeros_like(index)), axis=0)


def rope_tables(position):
    frequency = ROPE_BASE ** (-(jnp.arange(ROT, dtype=F32) * 2.0 / HDIM))
    angles = frequency[:, None] * position.astype(F32)[None, :]
    return jnp.cos(angles), jnp.sin(angles)


def per_device(
    count,
    hidden_in,
    query_weight,
    key_weight,
    value_weight,
    output_weight,
    gate_weight,
    up_weight,
    down_weight,
    attn_gain,
    ffn_gain,
    out_grad,
    segment_ids,
):
    col, row = lax.axis_index("col"), lax.axis_index("row")
    first = col == 0

    def own_tokens(array):
        outer = jnp.concatenate([array[..., :BLOCK], array[..., 3 * BLOCK :]], axis=-1)
        inner = array[..., BLOCK : 3 * BLOCK]
        return jnp.where(first, outer, inner), jnp.where(first, inner, outer)

    def in_window(own, got):
        outer, inner = jnp.where(first, own, got), jnp.where(first, got, own)
        return jnp.concatenate([outer[:, :BLOCK], inner, outer[:, BLOCK:]], axis=1)

    w_near = jnp.concatenate(
        [query_weight[:, 0].T, key_weight[:, 0].T, value_weight[:, 0].T], axis=0
    )
    w_far = swap(w_near, "row")
    wo_near = output_weight[0]
    wo_far = swap(wo_near, "row")
    x_own, x_other = own_tokens(hidden_in.T)
    x_got = swap(x_other, "col")
    gains = jnp.stack([attn_gain, ffn_gain])
    gains_got = swap(gains, "col").astype(F32)
    gains = gains.astype(F32)
    gin_own, gmid_own = gains[0][:, None], gains[1][:, None]
    gin_got, gmid_got = gains_got[0][:, None], gains_got[1][:, None]
    segment = jnp.where(col == row, segment_ids, swap(segment_ids, "col"))
    begin, _ = own_tokens(segment_begin(segment))
    index, _ = own_tokens(jnp.arange(MAXLEN, dtype=jnp.int32))
    cosine, sine = rope_tables(index - begin)
    begin = begin[None]
    live_near = jnp.where(row == 0, LIVE[0], LIVE[1])
    where_near = jnp.stack([col, live_near]).astype(jnp.int32)
    where_far = jnp.stack([col, LIVE[0] + LIVE[1] - live_near]).astype(jnp.int32)

    w_near_got = swap(w_near, "col")
    heads = (shape((QUERY, LOCAL)), shape((2 * KEY, LOCAL)))
    nm_in, q_near, kv_near = run(
        project_near_kernel,
        (x_own, x_got, gin_own, gin_got, cosine, sine, w_near, w_near_got),
        (shape((D, LOCAL)),) + heads,
        2 * LOCAL * D * D,
    )
    kv_near_got = swap(kv_near, "col")
    wo_near_got = swap(wo_near, "col")
    att_near, lse_near = attend(where_near, begin, q_near, kv_near, kv_near_got)
    w_far_got = swap(hold(w_far, lse_near), "col")
    q_far, kv_far = run(
        project_far_kernel,
        (nm_in, cosine, sine, w_far, w_far_got),
        heads,
        2 * LOCAL * D * D,
    )
    kv_far_got = swap(kv_far, "col")
    att_far, lse_far = attend(where_far, begin, q_far, kv_far, kv_far_got)
    wo_far_got = swap(hold(wo_far, kv_far), "col")
    og_own, og_other = own_tokens(out_grad.T)
    og = jnp.concatenate([og_own, swap(og_other, "col")], axis=0)
    og_far = swap(og, "row")
    mid, nm = run(
        mid_kernel,
        (
            att_near, att_far, wo_near, wo_near_got, wo_far, wo_far_got, x_own, x_got,
            gmid_own, gmid_got,
        ),
        (shape((D, LOCAL), F32), shape((D, LOCAL))),
        2 * LOCAL * D * D,
    )

    mlp_weights = ()
    for weight in (gate_weight, up_weight, down_weight.T):
        mlp_weights += (weight, swap(weight, "col"))
    nm_far = swap(nm, "row")
    out_part, gnm_part, act, gg, gu = feed_forward(nm, og, mlp_weights, F32, after=(og_far,))
    out_send, gnm_send, act_far, gg_far, gu_far = feed_forward(
        nm_far, og_far, mlp_weights, BF16, after=(act,)
    )
    gnm_back = swap(gnm_send, "row")
    down_keep, down_send = weight_grads(((og, og_far),), ((act, act_far),), (0,))
    down_got = swap(down_send, "col")
    gate_keep, gate_send, up_keep, up_send = weight_grads(
        ((nm, nm_far),), ((gg, gg_far), (gu, gu_far)), (0, 0), after=(down_keep,)
    )
    down_sum = add(down_keep, hold(down_got, gate_keep))
    gate_send, up_send = hold_all((gate_send, up_send), (gnm_back,))

    gmid, gb, gatt_near, gatt_far, ggain_mid = run(
        mid_back_kernel,
        (
            og, mid, gnm_part, gnm_back, gmid_own, gmid_got, wo_near, wo_near_got, wo_far,
            wo_far_got,
        ),
        (
            shape((D, LOCAL), F32), shape((D, LOCAL)), shape((QUERY, LOCAL)),
            shape((QUERY, LOCAL)), shape((2, 16, HALF), F32),
        ),
        2 * LOCAL * D * D,
        after=(down_sum,),
    )
    down_x = reduce_first(down_sum, count, (ggain_mid,))
    gate_sum = add(gate_keep, hold(swap(gate_send, "col"), ggain_mid))
    up_sum = add(up_keep, hold(swap(up_send, "col"), ggain_mid))

    def out_grads(att):
        send = dot(att, gb[HALF:], 1, 1).astype(BF16)
        return add(dot(att, gb[:HALF], 1, 1), swap(send, "col"))

    wo_far_sum = out_grads(att_far)
    wo_near_sum = out_grads(att_near)

    dq_far, own_far, other_far = attend_back(
        where_far, begin, q_far, kv_far, kv_far_got, gatt_far, lse_far, after=(down_x, gate_sum, up_sum)
    )
    gate_x = reduce_first(gate_sum, count, (dq_far,))
    down_z = reduce_rest(down_x, count, (dq_far,))

    got_far = swap(hold(other_far, gate_x, down_z), "col")
    joined = shape((ROWS, WIDE))
    gnm_in_part, far_keep, far_send = run(
        joined_far_kernel,
        (dq_far, own_far, got_far, cosine, sine, w_far, w_far_got, nm_in),
        (shape((D, LOCAL), F32), joined, joined),
        4 * LOCAL * D * D,
        after=(gate_x,),
        scratch=[pltpu.VMEM((D, LOCAL), BF16)],
    )
    gate_z = reduce_rest(gate_x, count, (far_keep,))
    up_x = reduce_first(hold(up_sum, gate_x), count, (far_keep,))
    wo_sum = add(wo_near_sum, swap(wo_far_sum, "row"))
    wo_sum = jnp.pad(wo_sum, ((0, 0), (0, WIDE - HALF)))
    dq_near, own_near, other_near = attend_back(
        where_near, begin, q_near, kv_near, kv_near_got, gatt_near, lse_near, after=(gate_z, up_x, wo_far_sum, wo_near_sum)
    )
    far_sum = add(far_keep, hold(swap(hold(far_send, gate_z, up_x), "col"), dq_near))
    got_near = swap(hold(other_near, far_sum, wo_sum), "col")
    near_keep, near_send, grad = run(
        joined_near_kernel,
        (
            dq_near, own_near, got_near, cosine, sine, w_near, w_near_got, nm_in, gnm_in_part,
            x_own, x_got, gin_own, gin_got, gmid, ggain_mid,
        ),
        (joined, joined, shape((D, LOCAL))),
        4 * LOCAL * D * D,
        scratch=[pltpu.VMEM((D, LOCAL), BF16)],
    )
    up_z = reduce_rest(up_x, count, (grad,))
    far_back = swap(far_sum, "row")
    last_sum = add(near_keep, swap(hold(near_send, far_back, up_z), "col"), far_back)

    def feature_cols(array):
        return in_window(array[:HALF], swap(array[HALF:], "col")).T


    def widened(whole_sum):
        parts = whole_sum.reshape(-1, HALF, LANE)
        return parts.transpose(1, 0, 2).reshape(HALF, -1).astype(F32)

    last_x = reduce_first(last_sum, count)
    out_x = reduce_first(wo_sum, count)
    last_z = reduce_rest(jnp.concatenate([last_x, out_x], axis=-2), count)
    last_rest = gather_rest(last_z, count)
    out_back = hold(swap(hold(out_send, gnm_back), "row"), last_z)
    block_out = feature_cols((mid + out_part + out_back.astype(F32)).astype(BF16))
    input_grad = feature_cols(hold(grad, last_x))
    down_grad = widened(hold(spread(down_z), last_rest))
    gate_grad = widened(hold(spread(gate_z), last_rest))
    up_rest = gather_rest(up_z, count, (last_x,))
    up_grad = widened(gather_first(up_rest, count, (last_z,)).reshape(up_sum.shape))
    last = gather_first(last_rest, count)
    last, out_weight_grad = last[..., : ROWS // count, :], last[..., ROWS // count :, :]
    last = last.reshape(last_sum.shape)[:, :HALF].astype(F32)
    out_weight_grad = out_weight_grad.reshape(wo_sum.shape)[:, :HALF].astype(F32)
    gain_grads = jnp.stack([last[D], last[D + 16]])
    gain_grads = gain_grads + swap(gain_grads, "row")
    return (
        block_out,
        input_grad,
        last[:QUERY].T[:, None, :],
        last[QUERY : QUERY + KEY].T[:, None, :],
        last[QUERY + KEY : D].T[:, None, :],
        out_weight_grad[None],
        gate_grad,
        up_grad,
        down_grad.T,
        gain_grads[0],
        gain_grads[1],
    )


def solution(mesh):
    return jax.shard_map(
        functools.partial(per_device, mesh.shape["dp"]),
        mesh=mesh,
        in_specs=(
            P(("dp", "row"), "col"),
            P("col", "row", None),
            P("col", "row", None),
            P("col", "row", None),
            P("row", None, "col"),
            P("col", "row"),
            P("col", "row"),
            P("row", "col"),
            P("col"),
            P("col"),
            P(("dp", "row"), "col"),
            P(("dp", "col")),
        ),
        out_specs=(
            P(("dp", "row"), "col"),
            P(("dp", "row"), "col"),
            P("col", "row", None),
            P("col", "row", None),
            P("col", "row", None),
            P("row", None, "col"),
            P("col", "row"),
            P("col", "row"),
            P("row", "col"),
            P("col"),
            P("col"),
        ),
        check_vma=False,
    )
```
